32 devices in a mesh: row: 4 (over x, core), col: 8 (over z, y).
Axes of the slice: x: 2, y: 2, z: 4, core: 2. Of those that a mesh axis runs over, the one named last changes fastest.
Arguments:
- region: bfloat16 [64, 256, 256], P('row', 'col'), may hold values from -6 to 6
- reduce_weight: bfloat16 [256, 512], P(None, 'col'), may hold values from -0.375 to 0.375
- group_weight: bfloat16 [144, 512], P(None, 'col'), may hold values from -0.5 to 0.5
- expand_weight: bfloat16 [512, 512], P(None, 'col'), may hold values from -0.25 to 0.25
- shortcut_weight: bfloat16 [256, 512], P(None, 'col'), may hold values from -0.375 to 0.375
- cotangent: bfloat16 [32, 128, 512], P('row', 'col'), may hold values from -6 to 6
Outputs:
- block_out: bfloat16 [32, 128, 512], P('row', 'col')
- region_grad: bfloat16 [64, 256, 256], P('row', 'col')
- reduce_grad: float32 [256, 512], P(None, 'col')
- group_grad: float32 [144, 512], P(None, 'col')
- expand_grad: float32 [512, 512], P(None, 'col')
- shortcut_grad: float32 [256, 512], P(None, 'col')
The draws below stay inside these ranges and needn't reach their ends.
All inputs are finite; a program needn't handle non-finite values.
Results may differ from the reference program's by a relative error of at most 0.0061.
Values may be sent and summed in bfloat16 or wider, within the bound.
No kernel may reach another device: no remote copies, remote signals or barrier semaphores. Data moves between devices by JAX's collectives and lax.ppermute only.
A program may use at most 128 MiB of HBM per device.

```python
import jax
import jax.numpy as jnp
from jax import lax

CIN = 256
MID = 512
OUT = 512
GROUPS = 32
GW = 16
H = 64
W = 256


def with_spikes(drawn, stream_key, source, target, parts, factor):
    def block_of(dim):
        return (jnp.arange(drawn.shape[dim]) // (drawn.shape[dim] // parts)).reshape((-1,) + (1,) * (drawn.ndim - 1 - dim))

    near = jax.random.permutation(stream_key, parts)[block_of(target)]
    second = (block_of(target) + parts // 2) % parts
    return jnp.where((block_of(source) == near) | (block_of(source) == second), factor * drawn, drawn)


def steps_of(stream_key, dims, shards, least, high):
    def one(axis_at, blocks):
        steps = jax.random.uniform(jax.random.fold_in(jax.random.fold_in(stream_key, 6), axis_at), (blocks,), jnp.float32, least / len(shards), high / len(shards))
        return jnp.repeat(jnp.exp(steps), dims[axis_at] // blocks).reshape((-1,) + (1,) * (len(dims) - axis_at - 1))

    factor_of = one(*shards[0])
    for cut in shards[1:]:
        factor_of = factor_of * one(*cut)
    return factor_of


def scatter_about(key, dims, scale, most, split=(), dtype=jnp.bfloat16):
    result = scale * jax.random.normal(key, dims, jnp.float32)
    if split:
        result = result * steps_of(key, dims, split, -0.22, 0.18)
    return jnp.clip(result, -most, most).astype(dtype)


def heavy_noise(rng, extent, deviation, most, cuts, heavy, kind=jnp.bfloat16):
    values = deviation * jax.random.normal(rng, extent, jnp.float32)
    if cuts:
        values = values * steps_of(rng, extent, cuts, -0.22, 0.18)
    return jnp.clip(with_spikes(values, jax.random.fold_in(rng, 3), *heavy), -most, most).astype(kind)


def setup_inputs(seed: int = 0) -> dict:
    seeds = jax.random.split(jax.random.key(seed), 7)
    return {
        "region": scatter_about(seeds[0], (H, W, CIN), 1.0, 6.0, ((0, 4), (1, 8))),
        "reduce_weight": scatter_about(seeds[1], (CIN, MID), CIN ** -0.5, 0.375, ((1, 8),)),
        "group_weight": scatter_about(seeds[2], (9 * GW, MID), (9 * GW) ** -0.5, 0.5, ((1, 8),)),
        "expand_weight": scatter_about(seeds[3], (MID, OUT), MID ** -0.5, 0.25, ((1, 8),)),
        "shortcut_weight": scatter_about(seeds[4], (CIN, OUT), CIN ** -0.5, 0.375, ((1, 8),)),
        "cotangent": heavy_noise(seeds[5], (H // 2, W // 2, OUT), 1.0, 6.0, ((0, 4), (1, 8)), (1, 2, 8, 2.0)),
    }


def activate(value):
    return value * jax.nn.sigmoid(value)


def slope(value):
    sigma = jax.nn.sigmoid(value)
    return sigma * (1.0 + value * (1.0 - sigma))


def reference(region, reduce_weight, group_weight, expand_weight, shortcut_weight, cotangent):
    height = region.shape[0]
    width = region.shape[1]
    rows_out = height // 2
    cols_out = width // 2
    flat = region.reshape(-1, CIN)
    pre_one = jnp.dot(flat, reduce_weight, preferred_element_type=jnp.float32).reshape(height, width, MID)
    hidden_one = activate(pre_one).astype(jnp.bfloat16)
    padded = jnp.pad(hidden_one, ((1, 0), (1, 0), (0, 0)))
    patches = []
    kernels = []
    pre_two = jnp.zeros((rows_out, cols_out, MID), jnp.float32)
    for offset in range(9):
        row_step, col_step = divmod(offset, 3)
        patch = lax.slice(padded, (row_step, col_step, 0), (row_step + height - 1, col_step + width - 1, MID), (2, 2, 1))
        patch = patch.reshape(rows_out, cols_out, GROUPS, GW).astype(jnp.float32)
        kernel = group_weight[offset * GW:(offset + 1) * GW].reshape(GW, GROUPS, GW).astype(jnp.float32)
        patches.append(patch)
        kernels.append(kernel)
        pre_two = pre_two + jnp.einsum("ijgc,cgo->ijgo", patch, kernel).reshape(rows_out, cols_out, MID)
    pre_flat = pre_two.reshape(-1, MID)
    hidden_two = activate(pre_flat).astype(jnp.bfloat16)
    strided = region[::2, ::2].reshape(-1, CIN)
    summed = jnp.dot(hidden_two, expand_weight, preferred_element_type=jnp.float32) + jnp.dot(strided, shortcut_weight, preferred_element_type=jnp.float32)
    block_out = activate(summed).astype(jnp.bfloat16).reshape(rows_out, cols_out, OUT)
    grad_sum = (cotangent.reshape(-1, OUT).astype(jnp.float32) * slope(summed)).astype(jnp.bfloat16)
    expand_grad = jnp.dot(hidden_two.T, grad_sum, preferred_element_type=jnp.float32)
    shortcut_grad = jnp.dot(strided.T, grad_sum, preferred_element_type=jnp.float32)
    grad_two = jnp.dot(grad_sum, expand_weight.T, preferred_element_type=jnp.float32)
    grad_two = (grad_two * slope(pre_flat)).astype(jnp.bfloat16)
    grad_two = grad_two.reshape(rows_out, cols_out, GROUPS, GW).astype(jnp.float32)
    spread = jnp.zeros((height + 1, width + 1, MID), jnp.float32)
    pieces = []
    for offset in range(9):
        row_step, col_step = divmod(offset, 3)
        pieces.append(jnp.einsum("ijgc,ijgo->cgo", patches[offset], grad_two).reshape(GW, MID))
        backed = jnp.einsum("ijgo,cgo->ijgc", grad_two, kernels[offset]).reshape(rows_out, cols_out, MID)
        spread = spread.at[row_step:row_step + height - 1:2, col_step:col_step + width - 1:2].add(backed)
    group_grad = jnp.concatenate(pieces, axis=0)
    grad_one = (spread[1:, 1:] * slope(pre_one)).astype(jnp.bfloat16).reshape(-1, MID)
    reduce_grad = jnp.dot(flat.T, grad_one, preferred_element_type=jnp.float32)
    region_grad = jnp.dot(grad_one, reduce_weight.T, preferred_element_type=jnp.float32).reshape(height, width, CIN)
    short_back = jnp.dot(grad_sum, shortcut_weight.T, preferred_element_type=jnp.float32).reshape(rows_out, cols_out, CIN)
    region_grad = region_grad.at[::2, ::2].add(short_back).astype(jnp.bfloat16)
    return (block_out, region_grad, reduce_grad, group_grad, expand_grad, shortcut_grad)
```

```python
import functools

import jax
import jax.numpy as jnp
from jax import lax
from jax.experimental import pallas as pl
from jax.experimental.pallas import tpu as pltpu
from jax.sharding import PartitionSpec as P

GW = 16
TAPS = 9
HALF = 256
BACK = (4, 5, 3, 7, 1, 8, 2, 6, 0)
F32 = jnp.float32
BF16 = jnp.bfloat16
VMEM_LIMIT = 40 * 1024 * 1024


class Sizes:
    def __init__(self, tile_rows, tile_cols):
        self.tr, self.tc = tile_rows, tile_cols
        self.hr, self.hc = tile_rows // 2, tile_cols // 2
        self.odd = (self.hr + 2) * self.hc
        self.even = (self.hr + 1) * self.hc
        self.band = self.odd + self.even
        self.side = 3 * self.band
        self.pixels = self.side + TAPS * 16
        self.main = self.hr * self.hc
        self.wide = self.main + self.hc
        self.out = self.wide + 16

    def tap(self, tap):
        a, b = divmod(tap, 3)
        return b * self.band + (0, self.odd, self.hc)[a]

    def tap_side(self, tap):
        return self.side + tap * 16

    def planes(self):
        return (
            self.band + self.odd,
            2 * self.band + self.odd,
            self.band + self.hc,
            2 * self.band + self.hc,
        )


def dot(a, b, dims=((1,), (0,))):
    return lax.dot_general(a, b, (dims, ((), ())), preferred_element_type=F32)


def sigmoid(value):
    return 1.0 / (1.0 + jnp.exp(-value))


def place():
    col = lax.axis_index("col")
    return col // 2, lax.rem(col, 2), lax.rem(lax.axis_index("row"), 2)


def gathered_positions(halves):
    h, low, core = place()
    other = 1 - low
    mine = low + core - 2 * low * core
    theirs = 1 - mine
    spots = [2 * h + low, 2 * h + other]
    for j in range(1, halves):
        spots.append(2 * lax.rem(h - j + halves, halves) + mine)
    for j in range(1, halves):
        spots.append(2 * lax.rem(h - j + halves, halves) + theirs)
    return spots


def row_of(sizes, r, north, region, south):
    if r < 0:
        return north[0]
    if r < sizes.tr:
        return region[r]
    return south[r - sizes.tr]


def pack_kernel(sizes, region, north, south, cot, cot_south, to_right, to_left, cols, cots):
    cols[...] = jnp.zeros_like(cols)
    cots[...] = jnp.zeros_like(cots)
    for r in range(-1, sizes.tr + 2):
        source = row_of(sizes, r, north, region, south)
        head = source[:16].astype(F32)
        tail = source[sizes.tc - 16 :].astype(F32)
        cols[0, r + 1 : r + 2] = tail[15:16]
        cols[1, r + 1 : r + 2] = head[0:1]
        cols[2, r + 1 : r + 2] = head[1:2]
    for i in range(sizes.hr + 1):
        source = cot[i] if i < sizes.hr else cot_south[0]
        cots[i : i + 1] = source[:16].astype(F32)[0:1]
    to_right[...] = cols[0].astype(BF16)
    to_left[0:32] = cols[1].astype(BF16)
    to_left[32:64] = cols[2].astype(BF16)
    half = cots.shape[1] // 2
    to_left[64:80] = cots[:, :half].astype(BF16)
    to_left[80:96] = cots[:, half:].astype(BF16)


def spread_kernel(sizes, region, north, south, west, east, x, ext, cols):
    cols[:, :, 32:40] = jnp.zeros((3, cols.shape[1], 8, 128), F32)
    for v in range(ext.shape[0]):
        lanes = slice(v * 128, (v + 1) * 128)
        cols[0, v, 0:32] = west[:, lanes].astype(F32)
        for r in range(-1, sizes.tr + 2):
            source = row_of(sizes, r, north, region, south)[:, lanes].astype(F32)
            ext[v, r + 1, 8 : 8 + sizes.tc] = source
            ext[v, r + 1, 7:8] = cols[0, v, r + 1 : r + 2]
        cols[0, v, 0:32] = jnp.zeros((32, 128), F32)
        for r in range(sizes.tr + 3):
            cols[0, v, r : r + 1] = ext[v, r, 7 + sizes.tc : 8 + sizes.tc]
        cols[1, v, 0:32] = east[0:32, lanes].astype(F32)
        cols[2, v, 0:32] = east[32:64, lanes].astype(F32)
        for b in range(3):
            base = b * sizes.band
            for r in list(range(0, sizes.tr + 3, 2)) + list(range(1, sizes.tr + 3, 2)):
                picked = ext[v, r, pl.ds(7 + b, sizes.hc, stride=2)]
                x[base : base + sizes.hc, lanes] = picked.astype(BF16)
                base += sizes.hc
            for a in range(3):
                at = sizes.tap_side(3 * a + b)
                x[at : at + 16, lanes] = cols[b, v, pl.ds(a, 16, stride=2)].astype(BF16)


def first_kernel(sizes, halves, x, *refs):
    blocks = refs[: 2 * halves]
    hidden, slope_one, hidden_two, slope_two, back, reduce_t = refs[2 * halves : 2 * halves + 6]
    pre, group_t, group, front, pre_two = refs[2 * halves + 6 :]
    shard = blocks[0].shape[0]
    cin = reduce_t.shape[1]
    mid = reduce_t.shape[0]
    for block, spot in zip(blocks, gathered_positions(halves), strict=True):
        rows = pl.ds(pl.multiple_of(spot * shard, shard), shard)
        reduce_t[rows, :] = block[:, :cin]
        group_t[rows, :] = block[:, cin:]
    pre[...] = dot(x[...], reduce_t[...], ((1,), (1,)))
    group[...] = group_t[...].astype(F32).T.astype(BF16)
    row_group = lax.broadcasted_iota(jnp.int32, (HALF, HALF), 0) // GW
    lane_group = lax.broadcasted_iota(jnp.int32, (HALF, HALF), 1) // GW
    mask = jnp.where(row_group == lane_group, 1.0, 0.0).astype(BF16)
    for n in range(mid // HALF):
        for tap in range(TAPS):
            rows = group[tap * GW : (tap + 1) * GW, n * HALF : (n + 1) * HALF]
            dense = jnp.concatenate([rows] * (HALF // GW), axis=0) * mask
            front[n, tap * HALF : (tap + 1) * HALF] = dense
            spot = BACK.index(tap)
            back[n, :, spot * HALF : (spot + 1) * HALF] = dense

    def silu_rows(at, _):
        rows = pl.ds(pl.multiple_of(at * 16, 16), 16)
        value = pre[rows, :]
        hidden[rows, :] = (value * sigmoid(value)).astype(BF16)
        return 0

    def plane_rows(at, start, to):
        source = pl.ds(pl.multiple_of(start + at * 16, 16), 16)
        target = pl.ds(pl.multiple_of(to + at * 16, 16), 16)
        value = pre[source, :]
        sigma = sigmoid(value)
        active = value * sigma
        hidden[source, :] = active.astype(BF16)
        slope_one[target, :] = sigma + active * (1.0 - sigma)

    lax.fori_loop(0, sizes.pixels // 16, silu_rows, 0, unroll=2)
    for i, start in enumerate(sizes.planes()):

        def body(at, _, start=start, to=i * sizes.main):
            plane_rows(at, start, to)
            return 0

        lax.fori_loop(0, sizes.main // 16, body, 0, unroll=2)

    for n in range(mid // HALF):
        lanes = slice(n * HALF, (n + 1) * HALF)
        patches = []
        for tap in range(TAPS):
            at, side = sizes.tap(tap), sizes.tap_side(tap)
            patches.append(
                jnp.concatenate(
                    [hidden[at : at + sizes.wide, lanes], hidden[side : side + 16, lanes]], axis=0
                )
            )
        pre_two[:, lanes] = dot(jnp.concatenate(patches, axis=1), front[n])
    value = pre_two[...]
    sigma = sigmoid(value)
    active = value * sigma
    hidden_two[...] = active.astype(BF16)
    slope_two[...] = sigma + active * (1.0 - sigma)


def split_out(halves, total, shard, keeps, give):
    h, low, core = place()
    keep = low + core - 2 * low * core
    for j in range(halves):
        base = 2 * lax.rem(h + j, halves)
        mine = pl.ds(pl.multiple_of((base + keep) * shard, shard), shard)
        theirs = pl.ds(pl.multiple_of((base + 1 - keep) * shard, shard), shard)
        keeps[j][...] = total[mine, :]
        give[j] = total[theirs, :].astype(BF16)


def second_kernel(sizes, halves, x, hidden_two, slope_two, cot, cot_south, east, *refs):
    blocks = refs[: 2 * halves]
    refs = refs[2 * halves :]
    block_out, grad_two, grad_side, short_back, give = refs[:5]
    keeps = refs[5 : 5 + halves]
    expand_t, short_t, total, shift = refs[5 + halves :]
    shard = blocks[0].shape[0]
    mid = expand_t.shape[1]
    width = expand_t.shape[0]
    for block, spot in zip(blocks, gathered_positions(halves), strict=True):
        rows = pl.ds(pl.multiple_of(spot * shard, shard), shard)
        expand_t[rows, :] = block[:, :mid]
        short_t[rows, :] = block[:, mid:]
    at, side = sizes.tap(4), sizes.tap_side(4)
    strided = jnp.concatenate([x[at : at + sizes.wide], x[side : side + 16]], axis=0)
    summed = dot(hidden_two[...], expand_t[...], ((1,), (1,))) + dot(
        strided, short_t[...], ((1,), (1,))
    )
    sigma = sigmoid(summed)
    active = summed * sigma
    block_out[...] = (
        active[: sizes.main].astype(BF16).reshape(sizes.hr, sizes.hc, width)
    )
    cotangent = jnp.concatenate(
        [
            cot[...].reshape(sizes.main, width),
            cot_south[...].reshape(sizes.hc, width),
            jnp.concatenate([east[64:80], east[80:96]], axis=1),
        ],
        axis=0,
    )
    grad_sum = (cotangent.astype(F32) * (sigma + active * (1.0 - sigma))).astype(BF16)
    own = grad_sum[: sizes.main]
    flipped = own.astype(F32).T.astype(BF16)
    total[:, :mid] = dot(flipped, hidden_two[: sizes.main])
    total[:, mid:] = dot(flipped, strided[: sizes.main])
    split_out(halves, total, shard, keeps, give)
    short_back[...] = dot(own, short_t[...])
    back = dot(grad_sum, expand_t[...]) * slope_two[...]
    grad_two[...] = back[: sizes.wide].astype(BF16)
    for i in range(sizes.hr + 1):
        shift[i, : sizes.hc] = back[i * sizes.hc : (i + 1) * sizes.hc]
        shift[i, sizes.hc : sizes.hc + 1] = back[sizes.wide + i : sizes.wide + i + 1]
    for i in range(sizes.hr + 1):
        grad_side[i * sizes.hc : (i + 1) * sizes.hc] = shift[i, 1 : sizes.hc + 1].astype(BF16)


def third_kernel(
    sizes, halves, x, hidden, slope_one, back, reduce_t, grad_two, grad_side, short_back, *refs
):
    region_grad, give = refs[:2]
    keeps = refs[2 : 2 + halves]
    total, grad_one, planes, spread_out = refs[2 + halves :]
    mid, cin = reduce_t.shape
    main, hc = sizes.main, sizes.hc
    shard = keeps[0].shape[0]
    down = slice(hc, hc + main)
    own = slice(0, main)
    for n in range(mid // HALF):
        lanes = slice(n * HALF, (n + 1) * HALF)
        two, low = grad_two[own, lanes], grad_two[down, lanes]
        side, corner = grad_side[own, lanes], grad_side[down, lanes]
        first = 0
        for i, parts in enumerate(((two,), (two, side), (two, low), (two, low, side, corner))):
            left = jnp.concatenate(parts, axis=1)
            last = first + len(parts) * HALF
            spread = dot(left, back[n, :, first:last], ((1,), (1,)))
            first = last
            rows = slice(i * main, (i + 1) * main)
            grad_one[rows, lanes] = (spread * slope_one[rows, lanes]).astype(BF16)
    flat = jnp.concatenate([x[at : at + main] for at in sizes.planes()], axis=0)
    total[:, :cin] = dot(grad_one[...].astype(F32).T.astype(BF16), flat)
    flipped = grad_two[own, :].astype(F32).T.astype(BF16)
    lane = lax.broadcasted_iota(jnp.int32, (GW, 128), 1) // GW
    for n in range(mid // HALF):
        lanes = slice(n * HALF, (n + 1) * HALF)
        sums = [jnp.zeros((GW, 128), F32)] * (HALF // GW)
        for tap in range(TAPS):
            at = sizes.tap(tap)
            piece = dot(flipped[n * HALF : (n + 1) * HALF], hidden[at : at + main, lanes])
            for q in range(HALF // GW):
                tile = q // 8
                block = piece[q * GW : (q + 1) * GW, tile * 128 : (tile + 1) * 128]
                block = pltpu.roll(block, (GW * (tap - q)) % 128, 1)
                if tap < 8:
                    sums[q] = jnp.where(lane == tap, block, sums[q])
                else:
                    rows = slice(n * HALF + q * GW, n * HALF + (q + 1) * GW)
                    total[rows, cin : cin + 128] = sums[q]
                    total[rows, cin + 128 : cin + 256] = jnp.where(lane == 0, block, 0.0)
    split_out(halves, total, shard, keeps, give)
    planes[...] = dot(grad_one[...], reduce_t[...])
    planes[:main] += short_back[...]
    for i in range(4):
        for r in range(sizes.hr):
            at = i * main + r * hc
            for v in range(cin // 128):
                lanes = slice(v * 128, (v + 1) * 128)
                spread_out[v, 2 * r + i // 2, pl.ds(i % 2, hc, stride=2)] = planes[at : at + hc, lanes]
    for v in range(cin // 128):
        region_grad[:, :, v * 128 : (v + 1) * 128] = spread_out[v].astype(BF16)


def call(kernel, out_shape, scratch, *operands, flops=0):
    sizes = sum(o.size * o.dtype.itemsize for o in operands)
    sizes += sum(o.size * o.dtype.itemsize for o in jax.tree.leaves(out_shape))
    return pl.pallas_call(
        kernel,
        out_shape=out_shape,
        in_specs=[pl.BlockSpec(memory_space=pltpu.VMEM)] * len(operands),
        out_specs=jax.tree.map(lambda _: pl.BlockSpec(memory_space=pltpu.VMEM), out_shape),
        scratch_shapes=scratch,
        compiler_params=pltpu.CompilerParams(vmem_limit_bytes=VMEM_LIMIT),
        cost_estimate=pl.CostEstimate(flops=flops, bytes_accessed=sizes, transcendentals=0),
    )(*operands)


def both(rows, cols, target):
    pairs = []
    for r in range(rows):
        for c in range(cols):
            to = target(r % 2, c // 2, c % 2)
            if to is not None:
                pairs.append((r * cols + c, r * cols + 2 * to[0] + to[1]))
    return pairs


def shifted(x, axis, by):
    devices = lax.axis_size(axis)
    pairs = [(i, i + by) for i in range(devices) if 0 <= i + by < devices]
    return lax.ppermute(x, axis, pairs)


def core_swap(x):
    return lax.ppermute(x, "row", [(r, r ^ 1) for r in range(lax.axis_size("row"))])


def gather(message):
    rows, cols = lax.axis_size("row"), lax.axis_size("col")
    halves = cols // 2
    far = {}
    for j in range(halves - 1, 0, -1):
        pairs = both(rows, cols, lambda k, h, low: ((h + j) % halves, low ^ k))
        far[j] = lax.ppermute(message, ("row", "col"), pairs)
    beside = lax.ppermute(message, "col", [(c, c ^ 1) for c in range(cols)])
    order = range(1, halves)
    return [message, beside] + [far[j] for j in order] + [core_swap(far[j]) for j in order]


def reduce(keeps, give):
    rows, cols = lax.axis_size("row"), lax.axis_size("col")
    halves = cols // 2
    core = lax.axis_index("row") % 2
    other = core_swap(give)
    sums = [keeps[j] + other[j].astype(F32) for j in range(halves)]
    total = None
    for j in range(halves - 1, -1, -1):
        pairs = both(
            rows, cols, lambda k, h, low: None if j == k == 0 else ((h + j) % halves, low ^ k)
        )
        came = lax.ppermute(sums[j].astype(BF16), ("row", "col"), pairs).astype(F32)
        if j == 0:
            came = jnp.where(core == 0, sums[0], came)
        total = came if total is None else total + came
    if rows != 4:
        return lax.psum(total, "row")
    total = total + core_swap(total)
    total = total.astype(BF16)
    across = lax.ppermute(total, "row", [(r, r ^ 2) for r in range(4)])
    return total.astype(F32) + across.astype(F32)


def per_device(region, reduce_weight, group_weight, expand_weight, shortcut_weight, cotangent):
    tile_rows, tile_cols, cin = region.shape
    sizes = Sizes(tile_rows, tile_cols)
    halves = lax.axis_size("col") // 2
    mid, shard = expand_weight.shape
    width = shard * lax.axis_size("col")
    taps = group_weight.shape[0]
    pad = jnp.zeros((shard, 256 - taps), BF16)
    early = jnp.concatenate([reduce_weight.T, group_weight.T, pad], axis=1)
    late = jnp.concatenate([expand_weight.T, shortcut_weight.T], axis=1)
    early_blocks = gather(early)
    north = shifted(region[-1:], "row", 1)
    south = shifted(region[:2], "row", -1)
    cot_south = shifted(cotangent[:1], "row", -1)
    late_blocks = gather(late)

    def shape(dims, dtype=BF16):
        return jax.ShapeDtypeStruct(dims, dtype)

    to_right, to_left = call(
        functools.partial(pack_kernel, sizes),
        (shape((32, cin)), shape((96, cin))),
        [pltpu.VMEM((3, 32, cin), F32), pltpu.VMEM((16, width), F32)],
        region, north, south, cotangent, cot_south,
    )
    west = shifted(to_right, "col", 1)
    east = shifted(to_left, "col", -1)
    x = call(
        functools.partial(spread_kernel, sizes),
        shape((sizes.pixels, cin)),
        [
            pltpu.VMEM((cin // 128, tile_rows + 3, 8 + tile_cols, 128), F32),
            pltpu.VMEM((3, cin // 128, 40, 128), F32),
        ],
        region, north, south, west, east,
    )
    hidden, slope_one, hidden_two, slope_two, back, reduce_t = call(
        functools.partial(first_kernel, sizes, halves),
        (
            shape((sizes.pixels, mid)),
            shape((4 * sizes.main, mid), F32),
            shape((sizes.out, mid)),
            shape((sizes.out, mid), F32),
            shape((mid // HALF, HALF, TAPS * HALF)),
            shape((mid, cin)),
        ),
        [
            pltpu.VMEM((sizes.pixels, mid), F32),
            pltpu.VMEM((mid, 256), BF16),
            pltpu.VMEM((256, mid), BF16),
            pltpu.VMEM((mid // HALF, TAPS * HALF, HALF), BF16),
            pltpu.VMEM((sizes.out, mid), F32),
        ],
        x, *early_blocks,
        flops=2 * sizes.pixels * cin * mid + 2 * sizes.out * TAPS * HALF * mid,
    )
    block_out, grad_two, grad_side, short_back, give, *keeps = call(
        functools.partial(second_kernel, sizes, halves),
        (
            shape((sizes.hr, sizes.hc, width)),
            shape((sizes.wide, mid)),
            shape((sizes.wide, mid)),
            shape((sizes.main, cin), F32),
            shape((halves, shard, mid + cin)),
        )
        + (shape((shard, mid + cin), F32),) * halves,
        [
            pltpu.VMEM((width, mid), BF16),
            pltpu.VMEM((width, cin), BF16),
            pltpu.VMEM((width, mid + cin), F32),
            pltpu.VMEM((sizes.hr + 1, 24, mid), F32),
        ],
        x, hidden_two, slope_two, cotangent, cot_south, east, *late_blocks,
        flops=6 * sizes.out * width * (mid + cin),
    )
    late_sum = reduce(keeps, give)
    region_grad, give, *keeps = call(
        functools.partial(third_kernel, sizes, halves),
        (shape(region.shape), shape((halves, shard, cin + 256)))
        + (shape((shard, cin + 256), F32),) * halves,
        [
            pltpu.VMEM((mid, cin + 256), F32),
            pltpu.VMEM((4 * sizes.main, mid), BF16),
            pltpu.VMEM((4 * sizes.main, cin), F32),
            pltpu.VMEM((cin // 128, tile_rows, tile_cols, 128), F32),
        ],
        x, hidden, slope_one, back, reduce_t, grad_two, grad_side, short_back,
        flops=4 * 4 * sizes.main * cin * mid + 4 * sizes.main * TAPS * HALF * mid,
    )
    early_sum = reduce(keeps, give)
    return (
        block_out,
        region_grad,
        early_sum[:, :cin].T,
        early_sum[:, cin : cin + taps].T,
        late_sum[:, :mid].T,
        late_sum[:, mid:].T,
    )


def solution(mesh):
    tiles, split = P("row", "col", None), P(None, "col")
    return jax.shard_map(
        per_device,
        mesh=mesh,
        in_specs=(tiles, split, split, split, split, tiles),
        out_specs=(tiles, tiles, split, split, split, split),
        check_vma=False,
    )
```

```python
import functools

import jax
import jax.numpy as jnp
from jax import lax
from jax.experimental import pallas as pl
from jax.experimental.pallas import tpu as pltpu
from jax.sharding import PartitionSpec as P

GW = 16
TAPS = 9
HALF = 256
BACK = (4, 5, 3, 7, 1, 8, 2, 6, 0)
F32 = jnp.float32
BF16 = jnp.bfloat16
VMEM_LIMIT = 40 * 1024 * 1024


class Sizes:
    def __init__(self, tile_rows, tile_cols):
        self.tr, self.tc = tile_rows, tile_cols
        self.hr, self.hc = tile_rows // 2, tile_cols // 2
        self.odd = (self.hr + 2) * self.hc
        self.even = (self.hr + 1) * self.hc
        self.band = self.odd + self.even
        self.side = 3 * self.band
        self.pixels = self.side + TAPS * 16
        self.main = self.hr * self.hc
        self.wide = self.main + self.hc
        self.out = self.wide + 16

    def tap(self, tap):
        a, b = divmod(tap, 3)
        return b * self.band + (0, self.odd, self.hc)[a]

    def tap_side(self, tap):
        return self.side + tap * 16

    def planes(self):
        return (
            self.band + self.odd,
            2 * self.band + self.odd,
            self.band + self.hc,
            2 * self.band + self.hc,
        )


def dot(a, b, dims=((1,), (0,))):
    return lax.dot_general(a, b, (dims, ((), ())), preferred_element_type=F32)


def sigmoid(value):
    return 1.0 / (1.0 + jnp.exp(-value))


def place():
    col = lax.axis_index("col")
    return col // 2, lax.rem(col, 2), lax.rem(lax.axis_index("row"), 2)


def pieces(halves, own, passed, swapped):
    h, low, core = place()
    shard = own.shape[0]
    flips = (low + core - 2 * low * core, 1 - low - core + 2 * low * core)
    found = [(own, (2 * h + low) * shard)]
    for ref, flip in zip((passed, swapped), flips, strict=True):
        for j in range(1, halves):
            spot = 2 * lax.rem(h - j + halves, halves) + flip
            found.append((ref.at[(j - 1) * shard : j * shard], spot * shard))
    share = passed.shape[0] - (halves - 1) * shard
    beside = (2 * h + 1 - low) * shard
    if share == shard:
        return found + [(passed.at[(halves - 1) * shard :], beside)]
    for ref, part in ((passed, core), (swapped, 1 - core)):
        found.append((ref.at[(halves - 1) * shard :], beside + part * share))
    return found


def send_kernel(sizes, *refs):
    given, (weights, outer, draft, cols) = refs[:6], refs[6:10]
    local, arrived = refs[10:16], refs[16]
    copies = [
        pltpu.make_async_copy(given[i], local[i], arrived.at[i]) for i in range(len(given))
    ]
    for copy in copies:
        copy.start()
    for copy in copies:
        copy.wait()
    region, cot, reduce_t, group_t, expand_t, short_t = local
    shard, taps = group_t.shape
    cin, mid = reduce_t.shape[1], expand_t.shape[1]
    last = cin + 256 + mid
    pad = jnp.zeros((shard, 256 - taps), BF16)
    weights[:, :cin] = reduce_t[...]
    weights[:, cin : cin + 256] = jnp.concatenate([group_t[...], pad], axis=1)
    weights[:, cin + 256 : last] = expand_t[...]
    weights[:, last:] = short_t[...]
    tc, half = sizes.tc, cot.shape[2] // 2
    for i, r in enumerate((sizes.tr - 1, 0, 1)):
        outer[i * tc : (i + 1) * tc] = region[r]
    outer[3 * tc : 3 * tc + sizes.hc] = cot[0, :, :half]
    outer[3 * tc + sizes.hc :] = cot[0, :, half:]
    cols[...] = jnp.zeros_like(cols)
    for r in range(sizes.tr):
        head, tail = region[r, :16].astype(F32), region[r, tc - 16 :].astype(F32)
        cols[r + 1 : r + 2, :cin] = head[0:1]
        cols[r + 1 : r + 2, cin : 2 * cin] = head[1:2]
        cols[r + 1 : r + 2, 2 * cin : 3 * cin] = tail[15:16]
    for i in range(sizes.hr):
        cols[i : i + 1, 3 * cin :] = cot[i, :16].astype(F32)[0:1]
    share = draft.shape[0] - 32
    if share == shard:
        draft[:share] = weights[...]
    else:
        core = lax.rem(lax.axis_index("row"), 2)
        draft[:share] = weights[pl.ds(pl.multiple_of(core * share, share), share), :]
    draft[share:] = cols[...].astype(BF16)


def choose(first, one, other, to_one, to_other):
    @pl.when(first)
    def _():
        to_one[...] = one[...]
        to_other[...] = other[...]

    @pl.when(jnp.logical_not(first))
    def _():
        to_one[...] = other[...]
        to_other[...] = one[...]


def columns_kernel(sizes, core_rows, far_rows, draft, beside, edge, north, south, cols):
    choose(lax.rem(lax.axis_index("row"), 2) == 0, core_rows, far_rows, south, north)
    cin, tc, tr = core_rows.shape[1], sizes.tc, sizes.tr
    share = draft.shape[0] - 32
    beside[:share] = draft[:share]
    cols[...] = draft[share:].astype(F32)
    for to, rows, at in ((0, north, 0), (tr + 1, south, tc), (tr + 2, south, 2 * tc)):
        head = rows[at : at + 16].astype(F32)
        tail = rows[at + tc - 16 : at + tc].astype(F32)
        cols[to : to + 1, :cin] = head[0:1]
        cols[to : to + 1, cin : 2 * cin] = head[1:2]
        cols[to : to + 1, 2 * cin : 3 * cin] = tail[15:16]
    for i in range(2):
        at, lanes = 3 * tc + i * sizes.hc, slice((3 + i) * cin, (4 + i) * cin)
        cols[sizes.hr : sizes.hr + 1, lanes] = south[at : at + 16].astype(F32)[0:1]
    beside[share:] = cols[...].astype(BF16)
    edge[...] = cols[...].astype(BF16)


def pass_kernel(beside, _, *refs):
    far, passed = refs[:-1], refs[-1]
    shard, share = far[0].shape[0], beside.shape[0] - 32
    for j, block in enumerate(far):
        passed[j * shard : (j + 1) * shard] = block[...]
    passed[len(far) * shard :] = beside[:share]


def spread_kernel(sizes, region, cot, core_rows, far_rows, beside, edge, *refs):
    x, cot_all, north, south, west, east, left, right, ext, cols = refs
    choose(lax.rem(lax.axis_index("row"), 2) == 0, core_rows, far_rows, south, north)
    choose(lax.rem(lax.axis_index("col"), 2) == 0, beside.at[beside.shape[0] - 32 :], edge, east, west)
    cin, tc, tr, hc = region.shape[2], sizes.tc, sizes.tr, sizes.hc
    left[...] = west[:, 2 * cin : 3 * cin].astype(F32)
    right[...] = east[:, : 2 * cin].astype(F32)
    cols[...] = jnp.zeros_like(cols)
    for v in range(cin // 128):
        lanes = slice(v * 128, (v + 1) * 128)
        for r in range(tr + 3):
            if r == 0:
                row = north[:tc, lanes]
            elif r <= tr:
                row = region[r - 1, :, lanes]
            else:
                row = south[(r - tr) * tc : (1 + r - tr) * tc, lanes]
            ext[v, r, 8 : 8 + tc] = row.astype(F32)
            ext[v, r, 7:8] = left[r : r + 1, lanes]
            cols[0, v, r : r + 1] = ext[v, r, 7 + tc : 8 + tc]
        for b in (1, 2):
            cols[b, v, :32] = right[:, (b - 1) * cin + v * 128 : (b - 1) * cin + (v + 1) * 128]
        for b in range(3):
            base = b * sizes.band
            for r in list(range(0, tr + 3, 2)) + list(range(1, tr + 3, 2)):
                picked = ext[v, r, pl.ds(7 + b, hc, stride=2)]
                x[base : base + hc, lanes] = picked.astype(BF16)
                base += hc
            for a in range(3):
                at = sizes.tap_side(3 * a + b)
                x[at : at + 16, lanes] = cols[b, v, pl.ds(a, 16, stride=2)].astype(BF16)
    half = cot_all.shape[1] // 2
    cot_all[: sizes.main] = cot[...].reshape(sizes.main, 2 * half)
    cot_all[sizes.main : sizes.wide, :half] = south[3 * tc : 3 * tc + hc]
    cot_all[sizes.main : sizes.wide, half:] = south[3 * tc + hc :]
    cot_all[sizes.wide :] = east[:16, 3 * cin :]


def first_kernel(sizes, halves, x, *refs):
    hidden, slope_one, hidden_two, slope_two, back, reduce_t = refs[3:9]
    pre, group_t, group, front, pre_two = refs[9:]
    cin = reduce_t.shape[1]
    mid = reduce_t.shape[0]
    for block, first in pieces(halves, *refs[:3]):
        rows = pl.ds(pl.multiple_of(first, 16), block.shape[0])
        reduce_t[rows, :] = block[:, :cin]
        group_t[rows, :] = block[:, cin : cin + 256]
    pre[...] = dot(x[...], reduce_t[...], ((1,), (1,)))
    group[...] = group_t[...].astype(F32).T.astype(BF16)
    row_group = lax.broadcasted_iota(jnp.int32, (HALF, HALF), 0) // GW
    lane_group = lax.broadcasted_iota(jnp.int32, (HALF, HALF), 1) // GW
    mask = jnp.where(row_group == lane_group, 1.0, 0.0).astype(BF16)
    for n in range(mid // HALF):
        for tap in range(TAPS):
            rows = group[tap * GW : (tap + 1) * GW, n * HALF : (n + 1) * HALF]
            dense = jnp.concatenate([rows] * (HALF // GW), axis=0) * mask
            front[n, tap * HALF : (tap + 1) * HALF] = dense
            spot = BACK.index(tap)
            back[n, :, spot * HALF : (spot + 1) * HALF] = dense

    def silu_rows(at, _):
        rows = pl.ds(pl.multiple_of(at * 16, 16), 16)
        value = pre[rows, :]
        hidden[rows, :] = (value * sigmoid(value)).astype(BF16)
        return 0

    def plane_rows(at, start, to):
        source = pl.ds(pl.multiple_of(start + at * 16, 16), 16)
        target = pl.ds(pl.multiple_of(to + at * 16, 16), 16)
        value = pre[source, :]
        sigma = sigmoid(value)
        active = value * sigma
        hidden[source, :] = active.astype(BF16)
        slope_one[target, :] = sigma + active * (1.0 - sigma)

    lax.fori_loop(0, sizes.pixels // 16, silu_rows, 0, unroll=2)
    for i, start in enumerate(sizes.planes()):

        def body(at, _, start=start, to=i * sizes.main):
            plane_rows(at, start, to)
            return 0

        lax.fori_loop(0, sizes.main // 16, body, 0, unroll=2)

    for n in range(mid // HALF):
        lanes = slice(n * HALF, (n + 1) * HALF)
        patches = []
        for tap in range(TAPS):
            at, side = sizes.tap(tap), sizes.tap_side(tap)
            patches.append(
                jnp.concatenate(
                    [hidden[at : at + sizes.wide, lanes], hidden[side : side + 16, lanes]], axis=0
                )
            )
        pre_two[:, lanes] = dot(jnp.concatenate(patches, axis=1), front[n])
    value = pre_two[...]
    sigma = sigmoid(value)
    active = value * sigma
    hidden_two[...] = active.astype(BF16)
    slope_two[...] = sigma + active * (1.0 - sigma)


def split_out(halves, total, shard, keeps, give):
    h, low, core = place()
    keep = low + core - 2 * low * core
    for j in range(halves):
        base = 2 * lax.rem(h + j, halves)
        mine = pl.ds(pl.multiple_of((base + keep) * shard, shard), shard)
        theirs = pl.ds(pl.multiple_of((base + 1 - keep) * shard, shard), shard)
        keeps[j][...] = total[mine, :]
        give[j] = total[theirs, :].astype(BF16)


def second_kernel(sizes, halves, x, hidden_two, slope_two, cot, *refs):
    block_out, grad_two, grad_side, short_back, total, expand_t, short_t, shift = refs[3:]
    skip = refs[0].shape[1] - total.shape[1]
    mid = expand_t.shape[1]
    width = expand_t.shape[0]
    for block, first in pieces(halves, *refs[:3]):
        rows = pl.ds(pl.multiple_of(first, 16), block.shape[0])
        expand_t[rows, :] = block[:, skip : skip + mid]
        short_t[rows, :] = block[:, skip + mid :]
    at, side = sizes.tap(4), sizes.tap_side(4)
    strided = jnp.concatenate([x[at : at + sizes.wide], x[side : side + 16]], axis=0)
    summed = dot(hidden_two[...], expand_t[...], ((1,), (1,))) + dot(
        strided, short_t[...], ((1,), (1,))
    )
    sigma = sigmoid(summed)
    active = summed * sigma
    block_out[...] = (
        active[: sizes.main].astype(BF16).reshape(sizes.hr, sizes.hc, width)
    )
    grad_sum = (cot[...].astype(F32) * (sigma + active * (1.0 - sigma))).astype(BF16)
    own = grad_sum[: sizes.main]
    flipped = own.astype(F32).T.astype(BF16)
    total[:, :mid] = dot(flipped, hidden_two[: sizes.main])
    total[:, mid:] = dot(flipped, strided[: sizes.main])
    short_back[...] = dot(own, short_t[...])
    back = dot(grad_sum, expand_t[...]) * slope_two[...]
    grad_two[...] = back[: sizes.wide].astype(BF16)
    for i in range(sizes.hr + 1):
        shift[i, : sizes.hc] = back[i * sizes.hc : (i + 1) * sizes.hc]
        shift[i, sizes.hc : sizes.hc + 1] = back[sizes.wide + i : sizes.wide + i + 1]
    for i in range(sizes.hr + 1):
        grad_side[i * sizes.hc : (i + 1) * sizes.hc] = shift[i, 1 : sizes.hc + 1].astype(BF16)


def third_kernel(
    sizes, halves, x, hidden, slope_one, back, reduce_t, grad_two, grad_side, short_back, late, *refs
):
    region_grad, give = refs[:2]
    keeps = refs[2 : 2 + halves]
    total, grad_one, planes, spread_out = refs[2 + halves :]
    mid, cin = reduce_t.shape
    main, hc = sizes.main, sizes.hc
    shard = keeps[0].shape[0]
    down = slice(hc, hc + main)
    own = slice(0, main)
    for n in range(mid // HALF):
        lanes = slice(n * HALF, (n + 1) * HALF)
        two, low = grad_two[own, lanes], grad_two[down, lanes]
        side, corner = grad_side[own, lanes], grad_side[down, lanes]
        first = 0
        for i, parts in enumerate(((two,), (two, side), (two, low), (two, low, side, corner))):
            left = jnp.concatenate(parts, axis=1)
            last = first + len(parts) * HALF
            spread = dot(left, back[n, :, first:last], ((1,), (1,)))
            first = last
            rows = slice(i * main, (i + 1) * main)
            grad_one[rows, lanes] = (spread * slope_one[rows, lanes]).astype(BF16)
    flat = jnp.concatenate([x[at : at + main] for at in sizes.planes()], axis=0)
    total[:, :cin] = dot(grad_one[...].astype(F32).T.astype(BF16), flat)
    flipped = grad_two[own, :].astype(F32).T.astype(BF16)
    lane = lax.broadcasted_iota(jnp.int32, (GW, 128), 1) // GW
    for n in range(mid // HALF):
        lanes = slice(n * HALF, (n + 1) * HALF)
        sums = [jnp.zeros((GW, 128), F32)] * (HALF // GW)
        for tap in range(TAPS):
            at = sizes.tap(tap)
            piece = dot(flipped[n * HALF : (n + 1) * HALF], hidden[at : at + main, lanes])
            for q in range(HALF // GW):
                tile = q // 8
                block = piece[q * GW : (q + 1) * GW, tile * 128 : (tile + 1) * 128]
                block = pltpu.roll(block, (GW * (tap - q)) % 128, 1)
                if tap < 8:
                    sums[q] = jnp.where(lane == tap, block, sums[q])
                else:
                    rows = slice(n * HALF + q * GW, n * HALF + (q + 1) * GW)
                    total[rows, cin : cin + 128] = sums[q]
                    total[rows, cin + 128 : cin + 256] = jnp.where(lane == 0, block, 0.0)
    total[:, cin + 256 :] = late[...]
    split_out(halves, total, shard, keeps, give)
    planes[...] = dot(grad_one[...], reduce_t[...])
    planes[:main] += short_back[...]
    for i in range(4):
        for r in range(sizes.hr):
            at = i * main + r * hc
            for v in range(cin // 128):
                lanes = slice(v * 128, (v + 1) * 128)
                spread_out[v, 2 * r + i // 2, pl.ds(i % 2, hc, stride=2)] = planes[at : at + hc, lanes]
    for v in range(cin // 128):
        region_grad[:, :, v * 128 : (v + 1) * 128] = spread_out[v].astype(BF16)


def call(kernel, out_shape, scratch, *operands, flops=0, space=pltpu.VMEM, limit=VMEM_LIMIT):
    sizes = sum(o.size * o.dtype.itemsize for o in operands)
    sizes += sum(o.size * o.dtype.itemsize for o in jax.tree.leaves(out_shape))
    return pl.pallas_call(
        kernel,
        out_shape=out_shape,
        in_specs=[pl.BlockSpec(memory_space=space)] * len(operands),
        out_specs=jax.tree.map(lambda _: pl.BlockSpec(memory_space=pltpu.VMEM), out_shape),
        scratch_shapes=scratch,
        compiler_params=pltpu.CompilerParams(vmem_limit_bytes=limit),
        cost_estimate=pl.CostEstimate(flops=flops, bytes_accessed=sizes, transcendentals=0),
    )(*operands)


def finish_kernel(total, across, *outs):
    value = total[...].astype(F32) + across[...].astype(F32)
    at = 0
    for out, skip in zip(outs, (0, 256 - outs[1].shape[1], 0, 0), strict=True):
        out[...] = value[:, at : at + out.shape[1]]
        at += out.shape[1] + skip


def both(rows, cols, target):
    pairs = []
    for r in range(rows):
        for c in range(cols):
            to = target(r % 2, c // 2, c % 2)
            if to is not None:
                pairs.append((r * cols + c, r * cols + 2 * to[0] + to[1]))
    return pairs


def swap_odd(x, axis):
    pairs = []
    for i in range(1, lax.axis_size(axis) - 1, 2):
        pairs += [(i, i + 1), (i + 1, i)]
    return lax.ppermute(x, axis, pairs)


def swap_even(x, axis):
    return lax.ppermute(x, axis, [(i, i ^ 1) for i in range(lax.axis_size(axis))])


def cross(x, j):
    rows, cols = lax.axis_size("row"), lax.axis_size("col")
    halves = cols // 2

    def target(k, h, low):
        return None if j == k == 0 else ((h + j) % halves, low ^ k)

    return lax.ppermute(x, ("row", "col"), both(rows, cols, target))


def reduce(keeps, give):
    rows, halves = lax.axis_size("row"), lax.axis_size("col") // 2
    core = lax.axis_index("row") % 2
    other = swap_even(give, "row")
    sums = [keeps[j] + other[j].astype(F32) for j in range(halves)]
    total = None
    for j in range(halves - 1, -1, -1):
        came = cross(sums[j].astype(BF16), j).astype(F32)
        if j == 0:
            came = jnp.where(core == 0, sums[0], came)
        total = came if total is None else total + came
    if rows != 4:
        return lax.psum(total, "row"), jnp.zeros_like(total)
    total = (total + swap_even(total, "row")).astype(BF16)
    return total, lax.ppermute(total, "row", [(r, r ^ 2) for r in range(4)])


def per_device(region, reduce_weight, group_weight, expand_weight, shortcut_weight, cotangent):
    tile_rows, tile_cols, cin = region.shape
    sizes = Sizes(tile_rows, tile_cols)
    halves = lax.axis_size("col") // 2
    mid, shard = expand_weight.shape
    width = shard * lax.axis_size("col")
    taps = group_weight.shape[0]
    early, late = cin + 256, mid + cin
    halo = 3 * cin + width
    share = shard // 2 if shard % 32 == 0 else shard

    def shape(dims, dtype=BF16):
        return jax.ShapeDtypeStruct(dims, dtype)

    def scratch(*dims, dtype=F32):
        return pltpu.VMEM(dims, dtype)

    inputs = (
        region, cotangent, reduce_weight.T, group_weight.T, expand_weight.T, shortcut_weight.T,
    )
    weights, outer, draft = call(
        functools.partial(send_kernel, sizes),
        (
            shape((shard, early + late)),
            shape((4 * tile_cols, cin)),
            shape((share + 32, halo)),
        ),
        [scratch(32, halo)]
        + [scratch(*given.shape, dtype=BF16) for given in inputs]
        + [pltpu.SemaphoreType.DMA((len(inputs),))],
        *inputs,
        space=pltpu.HBM,
        limit=62 * 1024 * 1024,
    )
    far = [cross(weights, j) for j in range(1, halves)]
    core_rows = swap_even(outer, "row")
    far_rows = swap_odd(outer, "row")
    rows_scratch = [scratch(4 * tile_cols, cin, dtype=BF16)] * 2
    beside, edge = call(
        functools.partial(columns_kernel, sizes),
        (shape(draft.shape), shape((32, halo))),
        rows_scratch + [scratch(32, halo)],
        core_rows, far_rows, draft,
    )
    beside, edge = swap_even(beside, "col"), swap_odd(edge, "col")
    x, cot_all = call(
        functools.partial(spread_kernel, sizes),
        (shape((sizes.pixels, cin)), shape((sizes.out, width))),
        rows_scratch
        + [
            scratch(32, halo, dtype=BF16),
            scratch(32, halo, dtype=BF16),
            scratch(32, cin),
            scratch(32, 2 * cin),
            scratch(cin // 128, tile_rows + 3, 8 + tile_cols, 128),
            scratch(3, cin // 128, 40, 128),
        ],
        region, cotangent, core_rows, far_rows, beside, edge,
    )
    passed = call(
        pass_kernel,
        shape(((halves - 1) * shard + share, early + late)),
        [],
        beside, edge, *far,
    )
    blocks = [weights, passed, swap_even(passed, "row")]
    hidden, slope_one, hidden_two, slope_two, back, reduce_t = call(
        functools.partial(first_kernel, sizes, halves),
        (
            shape((sizes.pixels, mid)),
            shape((4 * sizes.main, mid), F32),
            shape((sizes.out, mid)),
            shape((sizes.out, mid), F32),
            shape((mid // HALF, HALF, TAPS * HALF)),
            shape((mid, cin)),
        ),
        [
            scratch(sizes.pixels, mid),
            scratch(mid, 256, dtype=BF16),
            scratch(256, mid, dtype=BF16),
            scratch(mid // HALF, TAPS * HALF, HALF, dtype=BF16),
            scratch(sizes.out, mid),
        ],
        x, *blocks,
        flops=2 * sizes.pixels * cin * mid + 2 * sizes.out * TAPS * HALF * mid,
    )
    block_out, grad_two, grad_side, short_back, late_total = call(
        functools.partial(second_kernel, sizes, halves),
        (
            shape((sizes.hr, sizes.hc, width)),
            shape((sizes.wide, mid)),
            shape((sizes.wide, mid)),
            shape((sizes.main, cin), F32),
            shape((width, late), F32),
        ),
        [
            scratch(width, mid, dtype=BF16),
            scratch(width, cin, dtype=BF16),
            scratch(sizes.hr + 1, 24, mid),
        ],
        x, hidden_two, slope_two, cot_all, *blocks,
        flops=6 * sizes.out * width * (mid + cin),
    )
    region_grad, give, *keeps = call(
        functools.partial(third_kernel, sizes, halves),
        (shape(region.shape), shape((halves, shard, early + late)))
        + (shape((shard, early + late), F32),) * halves,
        [
            scratch(mid, early + late),
            scratch(4 * sizes.main, mid, dtype=BF16),
            scratch(4 * sizes.main, cin),
            scratch(cin // 128, tile_rows, tile_cols, 128),
        ],
        x, hidden, slope_one, back, reduce_t, grad_two, grad_side, short_back, late_total,
        flops=4 * 4 * sizes.main * cin * mid + 4 * sizes.main * TAPS * HALF * mid,
    )
    total, across = reduce(keeps, give)
    grads = call(
        finish_kernel,
        tuple(shape((shard, lanes), F32) for lanes in (cin, taps, mid, cin)),
        [],
        total, across,
    )
    return (block_out, region_grad, *(grad.T for grad in grads))


def solution(mesh):
    tiles, split = P("row", "col", None), P(None, "col")
    return jax.shard_map(
        per_device,
        mesh=mesh,
        in_specs=(tiles, split, split, split, split, tiles),
        out_specs=(tiles, tiles, split, split, split, split),
        check_vma=False,
    )
```

```python
import functools

import jax
import jax.numpy as jnp
from jax import lax
from jax.experimental import pallas as pl
from jax.experimental.pallas import tpu as pltpu
from jax.sharding import PartitionSpec as P

GW = 16
TAPS = 9
HALF = 256
BACK = (4, 5, 3, 7, 1, 8, 2, 6, 0)
F32 = jnp.float32
BF16 = jnp.bfloat16
VMEM_LIMIT = 40 * 1024 * 1024


class Sizes:
    def __init__(self, tile_rows, tile_cols):
        self.tr, self.tc = tile_rows, tile_cols
        self.hr, self.hc = tile_rows // 2, tile_cols // 2
        self.odd = (self.hr + 2) * self.hc
        self.even = (self.hr + 1) * self.hc
        self.band = self.odd + self.even
        self.side = 3 * self.band
        self.pixels = self.side + TAPS * 16
        self.main = self.hr * self.hc
        self.wide = self.main + self.hc
        self.out = self.wide + 16

    def tap(self, tap):
        a, b = divmod(tap, 3)
        return b * self.band + (0, self.odd, self.hc)[a]

    def tap_side(self, tap):
        return self.side + tap * 16

    def planes(self):
        return (
            self.band + self.odd,
            2 * self.band + self.odd,
            self.band + self.hc,
            2 * self.band + self.hc,
        )


def dot(a, b, dims=((1,), (0,))):
    return lax.dot_general(a, b, (dims, ((), ())), preferred_element_type=F32)


def sigmoid(value):
    below = 1.0 + jnp.exp(jnp.minimum(-value, 80.0))
    guess = pl.reciprocal(below, approx=True)
    return guess * (2.0 - below * guess)


def place():
    col = lax.axis_index("col")
    return col // 2, lax.rem(col, 2), lax.rem(lax.axis_index("row"), 2)


def pieces(halves, own, passed, swapped):
    h, low, core = place()
    shard = own.shape[0]
    flips = (low + core - 2 * low * core, 1 - low - core + 2 * low * core)
    found = [(own, (2 * h + low) * shard)]
    for ref, flip in zip((passed, swapped), flips, strict=True):
        for j in range(1, halves):
            spot = 2 * lax.rem(h - j + halves, halves) + flip
            found.append((ref.at[(j - 1) * shard : j * shard], spot * shard))
    share = passed.shape[0] - (halves - 1) * shard
    beside = (2 * h + 1 - low) * shard
    if share == shard:
        return found + [(passed.at[(halves - 1) * shard :], beside)]
    for ref, part in ((passed, core), (swapped, 1 - core)):
        found.append((ref.at[(halves - 1) * shard :], beside + part * share))
    return found


def send_kernel(sizes, *refs):
    given, (weights, outer, draft, cols) = refs[:6], refs[6:10]
    local, arrived = refs[10:16], refs[16]
    copies = [
        pltpu.make_async_copy(given[i], local[i], arrived.at[i]) for i in range(len(given))
    ]
    for copy in copies:
        copy.start()
    for copy in copies:
        copy.wait()
    region, cot, reduce_t, group_t, expand_t, short_t = local
    shard, taps = group_t.shape
    cin, mid = reduce_t.shape[1], expand_t.shape[1]
    last = cin + 256 + mid
    pad = jnp.zeros((shard, 256 - taps), BF16)
    weights[:, :cin] = reduce_t[...]
    weights[:, cin : cin + 256] = jnp.concatenate([group_t[...], pad], axis=1)
    weights[:, cin + 256 : last] = expand_t[...]
    weights[:, last:] = short_t[...]
    tc, half = sizes.tc, cot.shape[2] // 2
    for i, r in enumerate((sizes.tr - 1, 0, 1)):
        outer[i * tc : (i + 1) * tc] = region[r]
    outer[3 * tc : 3 * tc + sizes.hc] = cot[0, :, :half]
    outer[3 * tc + sizes.hc :] = cot[0, :, half:]
    cols[...] = jnp.zeros_like(cols)
    for r in range(sizes.tr):
        head, tail = region[r, :16].astype(F32), region[r, tc - 16 :].astype(F32)
        cols[r + 1 : r + 2, :cin] = head[0:1]
        cols[r + 1 : r + 2, cin : 2 * cin] = head[1:2]
        cols[r + 1 : r + 2, 2 * cin : 3 * cin] = tail[15:16]
    for i in range(sizes.hr):
        cols[i : i + 1, 3 * cin :] = cot[i, :16].astype(F32)[0:1]
    share = draft.shape[0] - 32
    if share == shard:
        draft[:share] = weights[...]
    else:
        core = lax.rem(lax.axis_index("row"), 2)
        draft[:share] = weights[pl.ds(pl.multiple_of(core * share, share), share), :]
    draft[share:] = cols[...].astype(BF16)


def choose(first, one, other, to_one, to_other):
    @pl.when(first)
    def _():
        to_one[...] = one[...]
        to_other[...] = other[...]

    @pl.when(jnp.logical_not(first))
    def _():
        to_one[...] = other[...]
        to_other[...] = one[...]


def columns_kernel(sizes, core_rows, far_rows, draft, beside, edge, north, south, cols):
    choose(lax.rem(lax.axis_index("row"), 2) == 0, core_rows, far_rows, south, north)
    cin, tc, tr = core_rows.shape[1], sizes.tc, sizes.tr
    share = draft.shape[0] - 32
    beside[:share] = draft[:share]
    cols[...] = draft[share:].astype(F32)
    for to, rows, at in ((0, north, 0), (tr + 1, south, tc), (tr + 2, south, 2 * tc)):
        head = rows[at : at + 16].astype(F32)
        tail = rows[at + tc - 16 : at + tc].astype(F32)
        cols[to : to + 1, :cin] = head[0:1]
        cols[to : to + 1, cin : 2 * cin] = head[1:2]
        cols[to : to + 1, 2 * cin : 3 * cin] = tail[15:16]
    for i in range(2):
        at, lanes = 3 * tc + i * sizes.hc, slice((3 + i) * cin, (4 + i) * cin)
        cols[sizes.hr : sizes.hr + 1, lanes] = south[at : at + 16].astype(F32)[0:1]
    beside[share:] = cols[...].astype(BF16)
    edge[...] = cols[...].astype(BF16)


def pass_kernel(beside, _, *refs):
    far, passed = refs[:-1], refs[-1]
    shard, share = far[0].shape[0], beside.shape[0] - 32
    for j, block in enumerate(far):
        passed[j * shard : (j + 1) * shard] = block[...]
    passed[len(far) * shard :] = beside[:share]


def spread_kernel(sizes, region, cot, core_rows, far_rows, beside, edge, *refs):
    x, cot_all, north, south, west, east, left, right, ext, cols = refs
    choose(lax.rem(lax.axis_index("row"), 2) == 0, core_rows, far_rows, south, north)
    choose(lax.rem(lax.axis_index("col"), 2) == 0, beside.at[beside.shape[0] - 32 :], edge, east, west)
    cin, tc, tr, hc = region.shape[2], sizes.tc, sizes.tr, sizes.hc
    left[...] = west[:, 2 * cin : 3 * cin].astype(F32)
    right[...] = east[:, : 2 * cin].astype(F32)
    cols[...] = jnp.zeros_like(cols)
    for v in range(cin // 128):
        lanes = slice(v * 128, (v + 1) * 128)
        for r in range(tr + 3):
            if r == 0:
                row = north[:tc, lanes]
            elif r <= tr:
                row = region[r - 1, :, lanes]
            else:
                row = south[(r - tr) * tc : (1 + r - tr) * tc, lanes]
            ext[v, r, 8 : 8 + tc] = row.astype(F32)
            ext[v, r, 7:8] = left[r : r + 1, lanes]
            cols[0, v, r : r + 1] = ext[v, r, 7 + tc : 8 + tc]
        for b in (1, 2):
            cols[b, v, :32] = right[:, (b - 1) * cin + v * 128 : (b - 1) * cin + (v + 1) * 128]
        for b in range(3):
            base = b * sizes.band
            for r in list(range(0, tr + 3, 2)) + list(range(1, tr + 3, 2)):
                picked = ext[v, r, pl.ds(7 + b, hc, stride=2)]
                x[base : base + hc, lanes] = picked.astype(BF16)
                base += hc
            for a in range(3):
                at = sizes.tap_side(3 * a + b)
                x[at : at + 16, lanes] = cols[b, v, pl.ds(a, 16, stride=2)].astype(BF16)
    half = cot_all.shape[1] // 2
    cot_all[: sizes.main] = cot[...].reshape(sizes.main, 2 * half)
    cot_all[sizes.main : sizes.wide, :half] = south[3 * tc : 3 * tc + hc]
    cot_all[sizes.main : sizes.wide, half:] = south[3 * tc + hc :]
    cot_all[sizes.wide :] = east[:16, 3 * cin :]


def first_kernel(sizes, halves, x, *refs):
    hidden, slope_one, hidden_two, slope_two, back, reduce_t = refs[3:9]
    pre, group_t, group, front, pre_two = refs[9:]
    cin = reduce_t.shape[1]
    mid = reduce_t.shape[0]
    for block, first in pieces(halves, *refs[:3]):
        rows = pl.ds(pl.multiple_of(first, 16), block.shape[0])
        reduce_t[rows, :] = block[:, :cin]
        group_t[rows, :] = block[:, cin : cin + 256]
    pre[...] = dot(x[...], reduce_t[...], ((1,), (1,)))
    group[...] = group_t[...].astype(F32).T.astype(BF16)
    row_group = lax.broadcasted_iota(jnp.int32, (HALF, HALF), 0) // GW
    lane_group = lax.broadcasted_iota(jnp.int32, (HALF, HALF), 1) // GW
    mask = jnp.where(row_group == lane_group, 1.0, 0.0).astype(BF16)
    for n in range(mid // HALF):
        for tap in range(TAPS):
            rows = group[tap * GW : (tap + 1) * GW, n * HALF : (n + 1) * HALF]
            dense = jnp.concatenate([rows] * (HALF // GW), axis=0) * mask
            front[n, tap * HALF : (tap + 1) * HALF] = dense
            spot = BACK.index(tap)
            back[n, :, spot * HALF : (spot + 1) * HALF] = dense

    planes = sizes.planes()
    first = 0
    for start in sorted(planes) + [sizes.pixels]:
        for at in range(first, start, 32):
            rows = slice(at, min(at + 32, start))
            value = pre[rows, :]
            hidden[rows, :] = (value * sigmoid(value)).astype(BF16)
        first = start + sizes.main
    for i, start in enumerate(planes):
        for at in range(0, sizes.main, 32):
            rows = slice(start + at, start + at + 32)
            value = pre[rows, :]
            sigma = sigmoid(value)
            active = value * sigma
            hidden[rows, :] = active.astype(BF16)
            rows = slice(i * sizes.main + at, i * sizes.main + at + 32)
            slope_one[rows, :] = sigma + active * (1.0 - sigma)
    for n in range(mid // HALF):
        lanes = slice(n * HALF, (n + 1) * HALF)
        patches = []
        for tap in range(TAPS):
            at, side = sizes.tap(tap), sizes.tap_side(tap)
            patches.append(
                jnp.concatenate(
                    [hidden[at : at + sizes.wide, lanes], hidden[side : side + 16, lanes]], axis=0
                )
            )
        pre_two[:, lanes] = dot(jnp.concatenate(patches, axis=1), front[n])
    value = pre_two[...]
    sigma = sigmoid(value)
    active = value * sigma
    hidden_two[...] = active.astype(BF16)
    slope_two[...] = sigma + active * (1.0 - sigma)


def split_out(halves, total, shard, keeps, give):
    h, low, core = place()
    keep = low + core - 2 * low * core
    for j in range(halves):
        base = 2 * lax.rem(h + j, halves)
        mine = pl.ds(pl.multiple_of((base + keep) * shard, shard), shard)
        theirs = pl.ds(pl.multiple_of((base + 1 - keep) * shard, shard), shard)
        keeps[j][...] = total[mine, :]
        give[j] = total[theirs, :].astype(BF16)


def second_kernel(sizes, halves, x, hidden_two, slope_two, cot, *refs):
    block_out, grad_two, grad_side, short_back, total, expand_t, short_t, shift = refs[3:]
    skip = refs[0].shape[1] - total.shape[1]
    mid = expand_t.shape[1]
    width = expand_t.shape[0]
    for block, first in pieces(halves, *refs[:3]):
        rows = pl.ds(pl.multiple_of(first, 16), block.shape[0])
        expand_t[rows, :] = block[:, skip : skip + mid]
        short_t[rows, :] = block[:, skip + mid :]
    at, side = sizes.tap(4), sizes.tap_side(4)
    strided = jnp.concatenate([x[at : at + sizes.wide], x[side : side + 16]], axis=0)
    summed = dot(hidden_two[...], expand_t[...], ((1,), (1,))) + dot(
        strided, short_t[...], ((1,), (1,))
    )
    sigma = sigmoid(summed)
    active = summed * sigma
    block_out[...] = (
        active[: sizes.main].astype(BF16).reshape(sizes.hr, sizes.hc, width)
    )
    grad_sum = (cot[...].astype(F32) * (sigma + active * (1.0 - sigma))).astype(BF16)
    own = grad_sum[: sizes.main]
    flipped = own.astype(F32).T.astype(BF16)
    total[:, :mid] = dot(flipped, hidden_two[: sizes.main])
    total[:, mid:] = dot(flipped, strided[: sizes.main])
    short_back[...] = dot(own, short_t[...])
    back = dot(grad_sum, expand_t[...]) * slope_two[...]
    grad_two[...] = back[: sizes.wide].astype(BF16)
    for i in range(sizes.hr + 1):
        shift[i, : sizes.hc] = back[i * sizes.hc : (i + 1) * sizes.hc]
        shift[i, sizes.hc : sizes.hc + 1] = back[sizes.wide + i : sizes.wide + i + 1]
    for i in range(sizes.hr + 1):
        grad_side[i * sizes.hc : (i + 1) * sizes.hc] = shift[i, 1 : sizes.hc + 1].astype(BF16)


def third_kernel(
    sizes, halves, x, hidden, slope_one, back, reduce_t, grad_two, grad_side, short_back, late, *refs
):
    region_grad, give = refs[:2]
    keeps = refs[2 : 2 + halves]
    total, grad_one, planes, spread_out = refs[2 + halves :]
    mid, cin = reduce_t.shape
    main, hc = sizes.main, sizes.hc
    shard = keeps[0].shape[0]
    down = slice(hc, hc + main)
    own = slice(0, main)
    for n in range(mid // HALF):
        lanes = slice(n * HALF, (n + 1) * HALF)
        two, low = grad_two[own, lanes], grad_two[down, lanes]
        side, corner = grad_side[own, lanes], grad_side[down, lanes]
        first = 0
        for i, parts in enumerate(((two,), (two, side), (two, low), (two, low, side, corner))):
            left = jnp.concatenate(parts, axis=1)
            last = first + len(parts) * HALF
            spread = dot(left, back[n, :, first:last], ((1,), (1,)))
            first = last
            rows = slice(i * main, (i + 1) * main)
            grad_one[rows, lanes] = (spread * slope_one[rows, lanes]).astype(BF16)
    flat = jnp.concatenate([x[at : at + main] for at in sizes.planes()], axis=0)
    total[:, :cin] = dot(grad_one[...].astype(F32).T.astype(BF16), flat)
    flipped = grad_two[own, :].astype(F32).T.astype(BF16)
    lane = lax.broadcasted_iota(jnp.int32, (GW, 128), 1) // GW
    for n in range(mid // HALF):
        lanes = slice(n * HALF, (n + 1) * HALF)
        sums = [jnp.zeros((GW, 128), F32)] * (HALF // GW)
        for tap in range(TAPS):
            at = sizes.tap(tap)
            piece = dot(flipped[n * HALF : (n + 1) * HALF], hidden[at : at + main, lanes])
            for q in range(HALF // GW):
                tile = q // 8
                block = piece[q * GW : (q + 1) * GW, tile * 128 : (tile + 1) * 128]
                block = pltpu.roll(block, (GW * (tap - q)) % 128, 1)
                if tap < 8:
                    sums[q] = jnp.where(lane == tap, block, sums[q])
                else:
                    rows = slice(n * HALF + q * GW, n * HALF + (q + 1) * GW)
                    total[rows, cin : cin + 128] = sums[q]
                    total[rows, cin + 128 : cin + 256] = jnp.where(lane == 0, block, 0.0)
    total[:, cin + 256 :] = late[...]
    split_out(halves, total, shard, keeps, give)
    planes[...] = dot(grad_one[...], reduce_t[...])
    planes[:main] += short_back[...]
    for i in range(4):
        for r in range(sizes.hr):
            at = i * main + r * hc
            for v in range(cin // 128):
                lanes = slice(v * 128, (v + 1) * 128)
                spread_out[v, 2 * r + i // 2, pl.ds(i % 2, hc, stride=2)] = planes[at : at + hc, lanes]
    for v in range(cin // 128):
        region_grad[:, :, v * 128 : (v + 1) * 128] = spread_out[v].astype(BF16)


def call(kernel, out_shape, scratch, *operands, flops=0, space=pltpu.VMEM, limit=VMEM_LIMIT):
    sizes = sum(o.size * o.dtype.itemsize for o in operands)
    sizes += sum(o.size * o.dtype.itemsize for o in jax.tree.leaves(out_shape))
    return pl.pallas_call(
        kernel,
        out_shape=out_shape,
        in_specs=[pl.BlockSpec(memory_space=space)] * len(operands),
        out_specs=jax.tree.map(lambda _: pl.BlockSpec(memory_space=pltpu.VMEM), out_shape),
        scratch_shapes=scratch,
        compiler_params=pltpu.CompilerParams(vmem_limit_bytes=limit),
        cost_estimate=pl.CostEstimate(flops=flops, bytes_accessed=sizes, transcendentals=0),
    )(*operands)


def finish_kernel(total, across, *outs):
    value = total[...].astype(F32) + across[...].astype(F32)
    at = 0
    for out, skip in zip(outs, (0, 256 - outs[1].shape[1], 0, 0), strict=True):
        out[...] = value[:, at : at + out.shape[1]]
        at += out.shape[1] + skip


def both(rows, cols, target):
    pairs = []
    for r in range(rows):
        for c in range(cols):
            to = target(r % 2, c // 2, c % 2)
            if to is not None:
                pairs.append((r * cols + c, r * cols + 2 * to[0] + to[1]))
    return pairs


def swap_odd(x, axis):
    pairs = []
    for i in range(1, lax.axis_size(axis) - 1, 2):
        pairs += [(i, i + 1), (i + 1, i)]
    return lax.ppermute(x, axis, pairs)


def swap_even(x, axis):
    return lax.ppermute(x, axis, [(i, i ^ 1) for i in range(lax.axis_size(axis))])


def cross(x, j):
    rows, cols = lax.axis_size("row"), lax.axis_size("col")
    halves = cols // 2

    def target(k, h, low):
        return None if j == k == 0 else ((h + j) % halves, low ^ k)

    return lax.ppermute(x, ("row", "col"), both(rows, cols, target))


def reduce(keeps, give):
    rows, halves = lax.axis_size("row"), lax.axis_size("col") // 2
    core = lax.axis_index("row") % 2
    other = swap_even(give, "row")
    sums = [keeps[j] + other[j].astype(F32) for j in range(halves)]
    total = None
    for j in sorted(range(halves), key=lambda j: min(j, halves - j)):
        came = cross(sums[j].astype(BF16), j).astype(F32)
        if j == 0:
            came = jnp.where(core == 0, sums[0], came)
        total = came if total is None else total + came
    if rows != 4:
        return lax.psum(total, "row"), jnp.zeros_like(total)
    total = (total + swap_even(total, "row")).astype(BF16)
    return total, lax.ppermute(total, "row", [(r, r ^ 2) for r in range(4)])


def per_device(region, reduce_weight, group_weight, expand_weight, shortcut_weight, cotangent):
    tile_rows, tile_cols, cin = region.shape
    sizes = Sizes(tile_rows, tile_cols)
    halves = lax.axis_size("col") // 2
    mid, shard = expand_weight.shape
    width = shard * lax.axis_size("col")
    taps = group_weight.shape[0]
    early, late = cin + 256, mid + cin
    halo = 3 * cin + width
    share = shard // 2 if shard % 32 == 0 else shard

    def shape(dims, dtype=BF16):
        return jax.ShapeDtypeStruct(dims, dtype)

    def scratch(*dims, dtype=F32):
        return pltpu.VMEM(dims, dtype)

    inputs = (
        region, cotangent, reduce_weight.T, group_weight.T, expand_weight.T, shortcut_weight.T,
    )
    weights, outer, draft = call(
        functools.partial(send_kernel, sizes),
        (
            shape((shard, early + late)),
            shape((4 * tile_cols, cin)),
            shape((share + 32, halo)),
        ),
        [scratch(32, halo)]
        + [scratch(*given.shape, dtype=BF16) for given in inputs]
        + [pltpu.SemaphoreType.DMA((len(inputs),))],
        *inputs,
        space=pltpu.HBM,
        limit=62 * 1024 * 1024,
    )
    far = [cross(weights, j) for j in range(1, halves)]
    core_rows = swap_even(outer, "row")
    far_rows = swap_odd(outer, "row")
    rows_scratch = [scratch(4 * tile_cols, cin, dtype=BF16)] * 2
    beside, edge = call(
        functools.partial(columns_kernel, sizes),
        (shape(draft.shape), shape((32, halo))),
        rows_scratch + [scratch(32, halo)],
        core_rows, far_rows, draft,
    )
    beside, edge = swap_even(beside, "col"), swap_odd(edge, "col")
    x, cot_all = call(
        functools.partial(spread_kernel, sizes),
        (shape((sizes.pixels, cin)), shape((sizes.out, width))),
        rows_scratch
        + [
            scratch(32, halo, dtype=BF16),
            scratch(32, halo, dtype=BF16),
            scratch(32, cin),
            scratch(32, 2 * cin),
            scratch(cin // 128, tile_rows + 3, 8 + tile_cols, 128),
            scratch(3, cin // 128, 40, 128),
        ],
        region, cotangent, core_rows, far_rows, beside, edge,
    )
    passed = call(
        pass_kernel,
        shape(((halves - 1) * shard + share, early + late)),
        [],
        beside, edge, *far,
    )
    blocks = [weights, passed, swap_even(passed, "row")]
    hidden, slope_one, hidden_two, slope_two, back, reduce_t = call(
        functools.partial(first_kernel, sizes, halves),
        (
            shape((sizes.pixels, mid)),
            shape((4 * sizes.main, mid), F32),
            shape((sizes.out, mid)),
            shape((sizes.out, mid), F32),
            shape((mid // HALF, HALF, TAPS * HALF)),
            shape((mid, cin)),
        ),
        [
            scratch(sizes.pixels, mid),
            scratch(mid, 256, dtype=BF16),
            scratch(256, mid, dtype=BF16),
            scratch(mid // HALF, TAPS * HALF, HALF, dtype=BF16),
            scratch(sizes.out, mid),
        ],
        x, *blocks,
        flops=2 * sizes.pixels * cin * mid + 2 * sizes.out * TAPS * HALF * mid,
    )
    block_out, grad_two, grad_side, short_back, late_total = call(
        functools.partial(second_kernel, sizes, halves),
        (
            shape((sizes.hr, sizes.hc, width)),
            shape((sizes.wide, mid)),
            shape((sizes.wide, mid)),
            shape((sizes.main, cin), F32),
            shape((width, late), F32),
        ),
        [
            scratch(width, mid, dtype=BF16),
            scratch(width, cin, dtype=BF16),
            scratch(sizes.hr + 1, 24, mid),
        ],
        x, hidden_two, slope_two, cot_all, *blocks,
        flops=6 * sizes.out * width * (mid + cin),
    )
    region_grad, give, *keeps = call(
        functools.partial(third_kernel, sizes, halves),
        (shape(region.shape), shape((halves, shard, early + late)))
        + (shape((shard, early + late), F32),) * halves,
        [
            scratch(mid, early + late),
            scratch(4 * sizes.main, mid, dtype=BF16),
            scratch(4 * sizes.main, cin),
            scratch(cin // 128, tile_rows, tile_cols, 128),
        ],
        x, hidden, slope_one, back, reduce_t, grad_two, grad_side, short_back, late_total,
        flops=4 * 4 * sizes.main * cin * mid + 4 * sizes.main * TAPS * HALF * mid,
    )
    total, across = reduce(keeps, give)
    grads = call(
        finish_kernel,
        tuple(shape((shard, lanes), F32) for lanes in (cin, taps, mid, cin)),
        [],
        total, across,
    )
    return (block_out, region_grad, *(grad.T for grad in grads))


def solution(mesh):
    tiles, split = P("row", "col", None), P(None, "col")
    return jax.shard_map(
        per_device,
        mesh=mesh,
        in_specs=(tiles, split, split, split, split, tiles),
        out_specs=(tiles, tiles, split, split, split, split),
        check_vma=False,
    )
```

```python
import functools

import jax
import jax.numpy as jnp
from jax import lax
from jax.experimental import pallas as pl
from jax.experimental.pallas import tpu as pltpu
from jax.sharding import PartitionSpec as P

GW = 16
TAPS = 9
HALF = 256
BACK = (4, 5, 3, 7, 1, 8, 2, 6, 0)
F32 = jnp.float32
BF16 = jnp.bfloat16
VMEM_LIMIT = 40 * 1024 * 1024


class Sizes:
    def __init__(self, tile_rows, tile_cols):
        self.tr, self.tc = tile_rows, tile_cols
        self.hr, self.hc = tile_rows // 2, tile_cols // 2
        self.odd = (self.hr + 2) * self.hc
        self.even = (self.hr + 1) * self.hc
        self.band = self.odd + self.even
        self.side = 3 * self.band
        self.pixels = self.side + TAPS * 16
        self.main = self.hr * self.hc
        self.wide = self.main + self.hc
        self.out = self.wide + 16

    def tap(self, tap):
        a, b = divmod(tap, 3)
        return b * self.band + (0, self.odd, self.hc)[a]

    def tap_side(self, tap):
        return self.side + tap * 16

    def planes(self):
        return (
            self.band + self.odd,
            2 * self.band + self.odd,
            self.band + self.hc,
            2 * self.band + self.hc,
        )


def dot(a, b, dims=((1,), (0,))):
    return lax.dot_general(a, b, (dims, ((), ())), preferred_element_type=F32)


def sigmoid(value):
    below = 1.0 + jnp.exp(jnp.minimum(-value, 80.0))
    guess = pl.reciprocal(below, approx=True)
    return guess * (2.0 - below * guess)


def place():
    col = lax.axis_index("col")
    return col // 2, lax.rem(col, 2), lax.rem(lax.axis_index("row"), 2)


def fold(block):
    parts = [
        pltpu.roll(block[at : at + GW], at, 1) if at else block[:GW]
        for at in range(0, block.shape[0], GW)
    ]
    return sum(parts[1:], parts[0])


def unfold(tail, rows):
    return [pltpu.roll(tail, (128 - at) % 128, 1) if at else tail for at in range(0, rows, GW)]


def pieces(halves, shard, own, passed, swapped, beside):
    h, low, core = place()
    length = own.shape[0]
    flips = (low + core - 2 * low * core, 1 - low - core + 2 * low * core)
    found = [(own, (2 * h + low) * shard)]
    for ref, flip in zip((passed, swapped), flips, strict=True):
        for j in range(1, halves):
            spot = 2 * lax.rem(h - j + halves, halves) + flip
            found.append((ref.at[(j - 1) * length : j * length], spot * shard))
    first = (halves - 1) * length
    share = passed.shape[0] - first
    for ref, part in ((passed, core), (swapped, 1 - core)):
        rows = pl.ds(pl.multiple_of(part * (length - share), 16), share)
        beside[rows, :] = ref[first : first + share]
    return found + [(beside, (2 * h + 1 - low) * shard)]


def send_kernel(sizes, *refs):
    given, (weights, outer, draft, cols) = refs[:6], refs[6:10]
    local, arrived = refs[10:16], refs[16]
    copies = [
        pltpu.make_async_copy(given[i], local[i], arrived.at[i]) for i in range(len(given))
    ]
    for copy in copies:
        copy.start()
    for copy in copies:
        copy.wait()
    region, cot, reduce_t, group_t, expand_t, short_t = local
    shard, taps = group_t.shape
    cin, mid = reduce_t.shape[1], expand_t.shape[1]
    tiles = [reduce_t[:, at : at + 128] for at in range(0, cin, 128)]
    tiles.append(group_t[:, :128])
    tiles += [expand_t[:, at : at + 128] for at in range(0, mid, 128)]
    tiles += [short_t[:, at : at + 128] for at in range(0, cin, 128)]
    for i, tile in enumerate(tiles):
        weights[i * shard : (i + 1) * shard] = tile
    pad = jnp.zeros((shard, 256 - taps), BF16)
    rest = jnp.concatenate([group_t[...], pad], axis=1)[:, 128:].astype(F32)
    weights[len(tiles) * shard :] = fold(rest).astype(BF16)
    tc, half = sizes.tc, cot.shape[2] // 2
    for i, r in enumerate((sizes.tr - 1, 0, 1)):
        outer[i * tc : (i + 1) * tc] = region[r]
    outer[3 * tc : 3 * tc + sizes.hc] = cot[0, :, :half]
    outer[3 * tc + sizes.hc :] = cot[0, :, half:]
    cols[...] = jnp.zeros_like(cols)
    for r in range(sizes.tr):
        put_columns(cols, r + 1, region[r, :16], region[r, tc - 16 :])
    for i in range(sizes.hr):
        put_cotangent(cols, i, cot[i, :16])
    share = draft.shape[0] - cols.shape[0]
    core = lax.rem(lax.axis_index("row"), 2)
    first = pl.multiple_of(core * (weights.shape[0] - share), 16)
    draft[:share] = weights[pl.ds(first, share), :]
    draft[share:] = cols[...].astype(BF16)


def put_columns(cols, row, head, tail):
    head, tail = head.astype(F32), tail.astype(F32)
    tiles = head.shape[1] // 128
    for i, pixel in enumerate((head[0:1], head[1:2], tail[15:16])):
        for v in range(tiles):
            at = (i * tiles + v) * 32 + row
            cols[at : at + 1] = pixel[:, v * 128 : (v + 1) * 128]


def put_cotangent(cols, row, head):
    pixel = head.astype(F32)[0:1]
    tiles = pixel.shape[1] // 128
    for v in range(tiles):
        at = cols.shape[0] - (tiles - v) * 16 + row
        cols[at : at + 1] = pixel[:, v * 128 : (v + 1) * 128]


def choose(first, one, other, to_one, to_other):
    @pl.when(first)
    def _():
        to_one[...] = one[...]
        to_other[...] = other[...]

    @pl.when(jnp.logical_not(first))
    def _():
        to_one[...] = other[...]
        to_other[...] = one[...]


def columns_kernel(sizes, core_rows, far_rows, draft, beside, edge, north, south, cols):
    choose(lax.rem(lax.axis_index("row"), 2) == 0, core_rows, far_rows, south, north)
    tc, tr, hc = sizes.tc, sizes.tr, sizes.hc
    share = draft.shape[0] - cols.shape[0]
    beside[:share] = draft[:share]
    cols[...] = draft[share:].astype(F32)
    for to, rows, at in ((0, north, 0), (tr + 1, south, tc), (tr + 2, south, 2 * tc)):
        put_columns(cols, to, rows[at : at + 16], rows[at + tc - 16 : at + tc])
    ends = [south[at : at + 16] for at in (3 * tc, 3 * tc + hc)]
    put_cotangent(cols, sizes.hr, jnp.concatenate(ends, axis=1))
    beside[share:] = cols[...].astype(BF16)
    edge[...] = cols[...].astype(BF16)


def pass_kernel(beside, edge, *refs):
    far, passed = refs[:-1], refs[-1]
    length, share = far[0].shape[0], beside.shape[0] - edge.shape[0]
    for j, block in enumerate(far):
        passed[j * length : (j + 1) * length] = block[...]
    passed[len(far) * length :] = beside[:share]


def spread_kernel(sizes, region, cot, core_rows, far_rows, beside, edge, *refs):
    x, cot_all, north, south, west, east, left, ext, cols = refs
    choose(lax.rem(lax.axis_index("row"), 2) == 0, core_rows, far_rows, south, north)
    choose(lax.rem(lax.axis_index("col"), 2) == 0, beside.at[beside.shape[0] - edge.shape[0] :], edge, east, west)
    cin, tc, tr, hc = region.shape[2], sizes.tc, sizes.tr, sizes.hc
    tiles = cin // 128
    for v in range(tiles):
        at = (2 * tiles + v) * 32
        left[:, v * 128 : (v + 1) * 128] = west[at : at + 32].astype(F32)
    cols[...] = jnp.zeros_like(cols)
    for v in range(cin // 128):
        lanes = slice(v * 128, (v + 1) * 128)
        for r in range(tr + 3):
            if r == 0:
                row = north[:tc, lanes]
            elif r <= tr:
                row = region[r - 1, :, lanes]
            else:
                row = south[(r - tr) * tc : (1 + r - tr) * tc, lanes]
            ext[v, r, 8 : 8 + tc] = row.astype(F32)
            ext[v, r, 7:8] = left[r : r + 1, lanes]
            cols[0, v, r : r + 1] = ext[v, r, 7 + tc : 8 + tc]
        for b in (1, 2):
            at = ((b - 1) * tiles + v) * 32
            cols[b, v, :32] = east[at : at + 32].astype(F32)
        for b in range(3):
            base = b * sizes.band
            for r in list(range(0, tr + 3, 2)) + list(range(1, tr + 3, 2)):
                picked = ext[v, r, pl.ds(7 + b, hc, stride=2)]
                x[base : base + hc, lanes] = picked.astype(BF16)
                base += hc
            for a in range(3):
                at = sizes.tap_side(3 * a + b)
                x[at : at + 16, lanes] = cols[b, v, pl.ds(a, 16, stride=2)].astype(BF16)
    half = cot_all.shape[1] // 2
    cot_all[: sizes.main] = cot[...].reshape(sizes.main, 2 * half)
    cot_all[sizes.main : sizes.wide, :half] = south[3 * tc : 3 * tc + hc]
    cot_all[sizes.main : sizes.wide, half:] = south[3 * tc + hc :]
    for v in range(2 * half // 128):
        at = 3 * tiles * 32 + v * 16
        cot_all[sizes.wide :, v * 128 : (v + 1) * 128] = east[at : at + 16]


def first_kernel(sizes, halves, x, *refs):
    hidden, slope_one, hidden_two, slope_two, back, reduce_t = refs[3:9]
    pre, group_t, group, front, pre_two, beside = refs[9:]
    cin = reduce_t.shape[1]
    mid = reduce_t.shape[0]
    shard = mid // (2 * halves)
    lane = lax.broadcasted_iota(jnp.int32, (GW, 128), 1)
    for block, first in pieces(halves, shard, *refs[:3], beside):
        rows = pl.ds(pl.multiple_of(first, 16), shard)
        for v in range(cin // 128):
            reduce_t[rows, v * 128 : (v + 1) * 128] = block[v * shard : (v + 1) * shard]
        at = cin // 128 * shard
        group_t[rows, :128] = block[at : at + shard]
        tail = block[block.shape[0] - GW :].astype(F32)
        for i, part in enumerate(unfold(tail, shard)):
            rows = pl.ds(pl.multiple_of(first + i * GW, 16), GW)
            group_t[rows, 128:] = jnp.where(lane < GW, part, 0.0).astype(BF16)
    pre[...] = dot(x[...], reduce_t[...], ((1,), (1,)))
    group[...] = group_t[...].astype(F32).T.astype(BF16)
    row_group = lax.broadcasted_iota(jnp.int32, (HALF, HALF), 0) // GW
    lane_group = lax.broadcasted_iota(jnp.int32, (HALF, HALF), 1) // GW
    mask = jnp.where(row_group == lane_group, 1.0, 0.0).astype(BF16)
    for n in range(mid // HALF):
        for tap in range(TAPS):
            rows = group[tap * GW : (tap + 1) * GW, n * HALF : (n + 1) * HALF]
            dense = jnp.concatenate([rows] * (HALF // GW), axis=0) * mask
            front[n, tap * HALF : (tap + 1) * HALF] = dense
            spot = BACK.index(tap)
            back[n, :, spot * HALF : (spot + 1) * HALF] = dense

    planes = sizes.planes()
    first = 0
    for start in sorted(planes) + [sizes.pixels]:
        for at in range(first, start, 32):
            rows = slice(at, min(at + 32, start))
            value = pre[rows, :]
            hidden[rows, :] = (value * sigmoid(value)).astype(BF16)
        first = start + sizes.main
    for i, start in enumerate(planes):
        for at in range(0, sizes.main, 32):
            rows = slice(start + at, start + at + 32)
            value = pre[rows, :]
            sigma = sigmoid(value)
            active = value * sigma
            hidden[rows, :] = active.astype(BF16)
            rows = slice(i * sizes.main + at, i * sizes.main + at + 32)
            slope_one[rows, :] = sigma + active * (1.0 - sigma)
    for n in range(mid // HALF):
        lanes = slice(n * HALF, (n + 1) * HALF)
        patches = []
        for tap in range(TAPS):
            at, side = sizes.tap(tap), sizes.tap_side(tap)
            patches.append(
                jnp.concatenate(
                    [hidden[at : at + sizes.wide, lanes], hidden[side : side + 16, lanes]], axis=0
                )
            )
        pre_two[:, lanes] = dot(jnp.concatenate(patches, axis=1), front[n])
    value = pre_two[...]
    sigma = sigmoid(value)
    active = value * sigma
    hidden_two[...] = active.astype(BF16)
    slope_two[...] = sigma + active * (1.0 - sigma)


def split_out(halves, total, shard, rest, keeps, give):
    tiles = [at for at in range(0, total.shape[1], 128) if at != rest]
    h, low, core = place()
    keep = low + core - 2 * low * core
    for j in range(halves):
        base = 2 * lax.rem(h + j, halves)
        mine = pl.ds(pl.multiple_of((base + keep) * shard, shard), shard)
        theirs = pl.ds(pl.multiple_of((base + 1 - keep) * shard, shard), shard)
        for i, at in enumerate(tiles):
            slab = slice(i * shard, (i + 1) * shard)
            keeps[j][slab] = total[mine, at : at + 128]
            give[j, slab] = total[theirs, at : at + 128].astype(BF16)
        keeps[j][len(tiles) * shard :] = fold(total[mine, rest : rest + 128])
        give[j, len(tiles) * shard :] = fold(total[theirs, rest : rest + 128]).astype(BF16)


def second_kernel(sizes, halves, x, hidden_two, slope_two, cot, *refs):
    block_out, grad_two, grad_side, short_back, total, expand_t, short_t, shift, beside = refs[3:]
    mid = expand_t.shape[1]
    width = expand_t.shape[0]
    shard = width // (2 * halves)
    cin = short_t.shape[1]
    for block, first in pieces(halves, shard, *refs[:3], beside):
        rows = pl.ds(pl.multiple_of(first, 16), shard)
        at = (cin // 128 + 1) * shard
        for ref in (expand_t, short_t):
            for v in range(ref.shape[1] // 128):
                ref[rows, v * 128 : (v + 1) * 128] = block[at : at + shard]
                at += shard
    at, side = sizes.tap(4), sizes.tap_side(4)
    strided = jnp.concatenate([x[at : at + sizes.wide], x[side : side + 16]], axis=0)
    summed = dot(hidden_two[...], expand_t[...], ((1,), (1,))) + dot(
        strided, short_t[...], ((1,), (1,))
    )
    sigma = sigmoid(summed)
    active = summed * sigma
    block_out[...] = (
        active[: sizes.main].astype(BF16).reshape(sizes.hr, sizes.hc, width)
    )
    grad_sum = (cot[...].astype(F32) * (sigma + active * (1.0 - sigma))).astype(BF16)
    own = grad_sum[: sizes.main]
    flipped = own.astype(F32).T.astype(BF16)
    total[:, :mid] = dot(flipped, hidden_two[: sizes.main])
    total[:, mid:] = dot(flipped, strided[: sizes.main])
    short_back[...] = dot(own, short_t[...])
    back = dot(grad_sum, expand_t[...]) * slope_two[...]
    grad_two[...] = back[: sizes.wide].astype(BF16)
    for i in range(sizes.hr + 1):
        shift[i, : sizes.hc] = back[i * sizes.hc : (i + 1) * sizes.hc]
        shift[i, sizes.hc : sizes.hc + 1] = back[sizes.wide + i : sizes.wide + i + 1]
    for i in range(sizes.hr + 1):
        grad_side[i * sizes.hc : (i + 1) * sizes.hc] = shift[i, 1 : sizes.hc + 1].astype(BF16)


def third_kernel(
    sizes, halves, x, hidden, slope_one, back, reduce_t, grad_two, grad_side, short_back, late, *refs
):
    region_grad, give = refs[:2]
    keeps = refs[2 : 2 + halves]
    total, grad_one, planes, spread_out = refs[2 + halves :]
    mid, cin = reduce_t.shape
    main, hc = sizes.main, sizes.hc
    shard = mid // (2 * halves)
    down = slice(hc, hc + main)
    own = slice(0, main)
    for n in range(mid // HALF):
        lanes = slice(n * HALF, (n + 1) * HALF)
        two, low = grad_two[own, lanes], grad_two[down, lanes]
        side, corner = grad_side[own, lanes], grad_side[down, lanes]
        first = 0
        for i, parts in enumerate(((two,), (two, side), (two, low), (two, low, side, corner))):
            left = jnp.concatenate(parts, axis=1)
            last = first + len(parts) * HALF
            spread = dot(left, back[n, :, first:last], ((1,), (1,)))
            first = last
            rows = slice(i * main, (i + 1) * main)
            grad_one[rows, lanes] = (spread * slope_one[rows, lanes]).astype(BF16)
    flat = jnp.concatenate([x[at : at + main] for at in sizes.planes()], axis=0)
    total[:, :cin] = dot(grad_one[...].astype(F32).T.astype(BF16), flat)
    flipped = grad_two[own, :].astype(F32).T.astype(BF16)
    lane = lax.broadcasted_iota(jnp.int32, (GW, 128), 1) // GW
    for n in range(mid // HALF):
        lanes = slice(n * HALF, (n + 1) * HALF)
        sums = [jnp.zeros((GW, 128), F32)] * (HALF // GW)
        for tap in range(TAPS):
            at = sizes.tap(tap)
            piece = dot(flipped[n * HALF : (n + 1) * HALF], hidden[at : at + main, lanes])
            for q in range(HALF // GW):
                tile = q // 8
                block = piece[q * GW : (q + 1) * GW, tile * 128 : (tile + 1) * 128]
                block = pltpu.roll(block, (GW * (tap - q)) % 128, 1)
                if tap < 8:
                    sums[q] = jnp.where(lane == tap, block, sums[q])
                else:
                    rows = slice(n * HALF + q * GW, n * HALF + (q + 1) * GW)
                    total[rows, cin : cin + 128] = sums[q]
                    total[rows, cin + 128 : cin + 256] = jnp.where(lane == 0, block, 0.0)
    total[:, cin + 256 :] = late[...]
    split_out(halves, total, shard, cin + 128, keeps, give)
    planes[...] = dot(grad_one[...], reduce_t[...])
    planes[:main] += short_back[...]
    for i in range(4):
        for r in range(sizes.hr):
            at = i * main + r * hc
            for v in range(cin // 128):
                lanes = slice(v * 128, (v + 1) * 128)
                spread_out[v, 2 * r + i // 2, pl.ds(i % 2, hc, stride=2)] = planes[at : at + hc, lanes]
    for v in range(cin // 128):
        region_grad[:, :, v * 128 : (v + 1) * 128] = spread_out[v].astype(BF16)


def call(kernel, out_shape, scratch, *operands, flops=0, space=pltpu.VMEM, limit=VMEM_LIMIT):
    sizes = sum(o.size * o.dtype.itemsize for o in operands)
    sizes += sum(o.size * o.dtype.itemsize for o in jax.tree.leaves(out_shape))
    return pl.pallas_call(
        kernel,
        out_shape=out_shape,
        in_specs=[pl.BlockSpec(memory_space=space)] * len(operands),
        out_specs=jax.tree.map(lambda _: pl.BlockSpec(memory_space=pltpu.VMEM), out_shape),
        scratch_shapes=scratch,
        compiler_params=pltpu.CompilerParams(vmem_limit_bytes=limit),
        cost_estimate=pl.CostEstimate(flops=flops, bytes_accessed=sizes, transcendentals=0),
    )(*operands)


def finish_kernel(total, across, *outs):
    value = total[...].astype(F32) + across[...].astype(F32)
    shard = outs[0].shape[0]
    at = 0
    for out in outs:
        for v in range(out.shape[1] // 128):
            out[:, v * 128 : (v + 1) * 128] = value[at : at + shard]
            at += shard
    rest = outs[1].shape[1] - 128
    for i, part in enumerate(unfold(value[at:], shard)):
        outs[1][i * GW : (i + 1) * GW, 128:] = part[:, :rest]


def both(rows, cols, target):
    pairs = []
    for r in range(rows):
        for c in range(cols):
            to = target(r % 2, c // 2, c % 2)
            if to is not None:
                pairs.append((r * cols + c, r * cols + 2 * to[0] + to[1]))
    return pairs


def swap_odd(x, axis):
    pairs = []
    for i in range(1, lax.axis_size(axis) - 1, 2):
        pairs += [(i, i + 1), (i + 1, i)]
    return lax.ppermute(x, axis, pairs)


def swap_even(x, axis):
    return lax.ppermute(x, axis, [(i, i ^ 1) for i in range(lax.axis_size(axis))])


def cross(x, j):
    rows, cols = lax.axis_size("row"), lax.axis_size("col")
    halves = cols // 2

    def target(k, h, low):
        return None if j == k == 0 else ((h + j) % halves, low ^ k)

    return lax.ppermute(x, ("row", "col"), both(rows, cols, target))


def reduce(keeps, give):
    rows, halves = lax.axis_size("row"), lax.axis_size("col") // 2
    core = lax.axis_index("row") % 2
    other = swap_even(give, "row")
    sums = [keeps[j] + other[j].astype(F32) for j in range(halves)]
    total = None
    for j in sorted(range(halves), key=lambda j: min(j, halves - j)):
        came = cross(sums[j].astype(BF16), j).astype(F32)
        if j == 0:
            came = jnp.where(core == 0, sums[0], came)
        total = came if total is None else total + came
    if rows != 4:
        return lax.psum(total, "row"), jnp.zeros_like(total)
    total = (total + swap_even(total, "row")).astype(BF16)
    return total, lax.ppermute(total, "row", [(r, r ^ 2) for r in range(4)])


def per_device(region, reduce_weight, group_weight, expand_weight, shortcut_weight, cotangent):
    tile_rows, tile_cols, cin = region.shape
    sizes = Sizes(tile_rows, tile_cols)
    halves = lax.axis_size("col") // 2
    mid, shard = expand_weight.shape
    width = shard * lax.axis_size("col")
    taps = group_weight.shape[0]
    early, late = cin + 256, mid + cin
    length = (early + late) // 128 * shard - shard + GW
    share = (length + 31) // 32 * 16
    halo = 3 * cin // 128 * 32 + width // 128 * 16

    def shape(dims, dtype=BF16):
        return jax.ShapeDtypeStruct(dims, dtype)

    def scratch(*dims, dtype=F32):
        return pltpu.VMEM(dims, dtype)

    inputs = (
        region, cotangent, reduce_weight.T, group_weight.T, expand_weight.T, shortcut_weight.T,
    )
    weights, outer, draft = call(
        functools.partial(send_kernel, sizes),
        (
            shape((length, 128)),
            shape((4 * tile_cols, cin)),
            shape((share + halo, 128)),
        ),
        [scratch(halo, 128)]
        + [scratch(*given.shape, dtype=BF16) for given in inputs]
        + [pltpu.SemaphoreType.DMA((len(inputs),))],
        *inputs,
        space=pltpu.HBM,
        limit=62 * 1024 * 1024,
    )
    far = [cross(weights, j) for j in range(1, halves)]
    core_rows = swap_even(outer, "row")
    far_rows = swap_odd(outer, "row")
    rows_scratch = [scratch(4 * tile_cols, cin, dtype=BF16)] * 2
    beside, edge = call(
        functools.partial(columns_kernel, sizes),
        (shape(draft.shape), shape((halo, 128))),
        rows_scratch + [scratch(halo, 128)],
        core_rows, far_rows, draft,
    )
    beside, edge = swap_even(beside, "col"), swap_odd(edge, "col")
    x, cot_all = call(
        functools.partial(spread_kernel, sizes),
        (shape((sizes.pixels, cin)), shape((sizes.out, width))),
        rows_scratch
        + [
            scratch(halo, 128, dtype=BF16),
            scratch(halo, 128, dtype=BF16),
            scratch(32, cin),
            scratch(cin // 128, tile_rows + 3, 8 + tile_cols, 128),
            scratch(3, cin // 128, 40, 128),
        ],
        region, cotangent, core_rows, far_rows, beside, edge,
    )
    passed = call(
        pass_kernel,
        shape(((halves - 1) * length + share, 128)),
        [],
        beside, edge, *far,
    )
    blocks = [weights, passed, swap_even(passed, "row")]
    hidden, slope_one, hidden_two, slope_two, back, reduce_t = call(
        functools.partial(first_kernel, sizes, halves),
        (
            shape((sizes.pixels, mid)),
            shape((4 * sizes.main, mid), F32),
            shape((sizes.out, mid)),
            shape((sizes.out, mid), F32),
            shape((mid // HALF, HALF, TAPS * HALF)),
            shape((mid, cin)),
        ),
        [
            scratch(sizes.pixels, mid),
            scratch(mid, 256, dtype=BF16),
            scratch(256, mid, dtype=BF16),
            scratch(mid // HALF, TAPS * HALF, HALF, dtype=BF16),
            scratch(sizes.out, mid),
            scratch(length, 128, dtype=BF16),
        ],
        x, *blocks,
        flops=2 * sizes.pixels * cin * mid + 2 * sizes.out * TAPS * HALF * mid,
    )
    block_out, grad_two, grad_side, short_back, late_total = call(
        functools.partial(second_kernel, sizes, halves),
        (
            shape((sizes.hr, sizes.hc, width)),
            shape((sizes.wide, mid)),
            shape((sizes.wide, mid)),
            shape((sizes.main, cin), F32),
            shape((width, late), F32),
        ),
        [
            scratch(width, mid, dtype=BF16),
            scratch(width, cin, dtype=BF16),
            scratch(sizes.hr + 1, 24, mid),
            scratch(length, 128, dtype=BF16),
        ],
        x, hidden_two, slope_two, cot_all, *blocks,
        flops=6 * sizes.out * width * (mid + cin),
    )
    region_grad, give, *keeps = call(
        functools.partial(third_kernel, sizes, halves),
        (shape(region.shape), shape((halves, length, 128)))
        + (shape((length, 128), F32),) * halves,
        [
            scratch(mid, early + late),
            scratch(4 * sizes.main, mid, dtype=BF16),
            scratch(4 * sizes.main, cin),
            scratch(cin // 128, tile_rows, tile_cols, 128),
        ],
        x, hidden, slope_one, back, reduce_t, grad_two, grad_side, short_back, late_total,
        flops=4 * 4 * sizes.main * cin * mid + 4 * sizes.main * TAPS * HALF * mid,
    )
    total, across = reduce(keeps, give)
    grads = call(
        finish_kernel,
        tuple(shape((shard, lanes), F32) for lanes in (cin, taps, mid, cin)),
        [],
        total, across,
    )
    return (block_out, region_grad, *(grad.T for grad in grads))


def solution(mesh):
    tiles, split = P("row", "col", None), P(None, "col")
    return jax.shard_map(
        per_device,
        mesh=mesh,
        in_specs=(tiles, split, split, split, split, tiles),
        out_specs=(tiles, tiles, split, split, split, split),
        check_vma=False,
    )
```

```python
import functools

import jax
import jax.numpy as jnp
from jax import lax
from jax.experimental import pallas as pl
from jax.experimental.pallas import tpu as pltpu
from jax.sharding import PartitionSpec as P

GW = 16
TAPS = 9
HALF = 256
BACK = (4, 5, 3, 7, 1, 8, 2, 6, 0)
F32 = jnp.float32
BF16 = jnp.bfloat16
VMEM_LIMIT = 40 * 1024 * 1024


class Sizes:
    def __init__(self, tile_rows, tile_cols):
        self.tr, self.tc = tile_rows, tile_cols
        self.hr, self.hc = tile_rows // 2, tile_cols // 2
        self.odd = (self.hr + 2) * self.hc
        self.even = (self.hr + 1) * self.hc
        self.band = self.odd + self.even
        self.side = 3 * self.band
        self.pixels = self.side + TAPS * 16
        self.main = self.hr * self.hc
        self.wide = self.main + self.hc
        self.out = self.wide + 16

    def tap(self, tap):
        a, b = divmod(tap, 3)
        return b * self.band + (0, self.odd, self.hc)[a]

    def tap_side(self, tap):
        return self.side + tap * 16

    def planes(self):
        return (
            self.band + self.odd,
            2 * self.band + self.odd,
            self.band + self.hc,
            2 * self.band + self.hc,
        )


def dot(a, b, dims=((1,), (0,))):
    return lax.dot_general(a, b, (dims, ((), ())), preferred_element_type=F32)


def sigmoid(value):
    below = 1.0 + jnp.exp(jnp.minimum(-value, 80.0))
    guess = pl.reciprocal(below, approx=True)
    return guess * (2.0 - below * guess)


def place():
    col = lax.axis_index("col")
    return col // 2, lax.rem(col, 2), lax.rem(lax.axis_index("row"), 2)


def fold(block):
    parts = [
        pltpu.roll(block[at : at + GW], at, 1) if at else block[:GW]
        for at in range(0, block.shape[0], GW)
    ]
    return sum(parts[1:], parts[0])


def unfold(tail, rows):
    return [pltpu.roll(tail, (128 - at) % 128, 1) if at else tail for at in range(0, rows, GW)]


def pieces(halves, shard, own, passed, swapped, beside):
    h, low, core = place()
    length = own.shape[0]
    flips = (low + core - 2 * low * core, 1 - low - core + 2 * low * core)
    found = [(own, (2 * h + low) * shard)]
    for ref, flip in zip((passed, swapped), flips, strict=True):
        for j in range(1, halves):
            spot = 2 * lax.rem(h - j + halves, halves) + flip
            found.append((ref.at[(j - 1) * length : j * length], spot * shard))
    first = (halves - 1) * length
    share = passed.shape[0] - first
    for ref, part in ((passed, core), (swapped, 1 - core)):
        rows = pl.ds(pl.multiple_of(part * (length - share), 16), share)
        beside[rows, :] = ref[first : first + share]
    return found + [(beside, (2 * h + 1 - low) * shard)]


def send_kernel(sizes, *refs):
    given, (weights, outer, draft, cols) = refs[:6], refs[6:10]
    local, arrived = refs[10:16], refs[16]
    copies = [
        pltpu.make_async_copy(given[i], local[i], arrived.at[i]) for i in range(len(given))
    ]
    for copy in copies:
        copy.start()
    for copy in copies:
        copy.wait()
    region, cot, reduce_t, group_t, expand_t, short_t = local
    shard, taps = group_t.shape
    cin, mid = reduce_t.shape[1], expand_t.shape[1]
    tiles = [reduce_t[:, at : at + 128] for at in range(0, cin, 128)]
    tiles.append(group_t[:, :128])
    tiles += [expand_t[:, at : at + 128] for at in range(0, mid, 128)]
    tiles += [short_t[:, at : at + 128] for at in range(0, cin, 128)]
    for i, tile in enumerate(tiles):
        weights[i * shard : (i + 1) * shard] = tile
    pad = jnp.zeros((shard, 256 - taps), BF16)
    rest = jnp.concatenate([group_t[...], pad], axis=1)[:, 128:].astype(F32)
    weights[len(tiles) * shard :] = fold(rest).astype(BF16)
    tc, half = sizes.tc, cot.shape[2] // 2
    for i, r in enumerate((sizes.tr - 1, 0, 1)):
        outer[i * tc : (i + 1) * tc] = region[r]
    outer[3 * tc : 3 * tc + sizes.hc] = cot[0, :, :half]
    outer[3 * tc + sizes.hc :] = cot[0, :, half:]
    cols[...] = jnp.zeros_like(cols)
    for r in range(sizes.tr):
        put_columns(cols, r + 1, region[r, :16], region[r, tc - 16 :])
    for i in range(sizes.hr):
        put_cotangent(cols, i, cot[i, :16])
    share = draft.shape[0] - cols.shape[0]
    core = lax.rem(lax.axis_index("row"), 2)
    first = pl.multiple_of(core * (weights.shape[0] - share), 16)
    draft[:share] = weights[pl.ds(first, share), :]
    draft[share:] = cols[...].astype(BF16)


def put_columns(cols, row, head, tail):
    head, tail = head.astype(F32), tail.astype(F32)
    tiles = head.shape[1] // 128
    for i, pixel in enumerate((head[0:1], head[1:2], tail[15:16])):
        for v in range(tiles):
            at = (i * tiles + v) * 32 + row
            cols[at : at + 1] = pixel[:, v * 128 : (v + 1) * 128]


def put_cotangent(cols, row, head):
    pixel = head.astype(F32)[0:1]
    tiles = pixel.shape[1] // 128
    for v in range(tiles):
        at = cols.shape[0] - (tiles - v) * 16 + row
        cols[at : at + 1] = pixel[:, v * 128 : (v + 1) * 128]


def choose(first, one, other, to_one, to_other):
    @pl.when(first)
    def _():
        to_one[...] = one[...]
        to_other[...] = other[...]

    @pl.when(jnp.logical_not(first))
    def _():
        to_one[...] = other[...]
        to_other[...] = one[...]


def columns_kernel(sizes, core_rows, far_rows, draft, beside, edge, north, south, cols):
    choose(lax.rem(lax.axis_index("row"), 2) == 0, core_rows, far_rows, south, north)
    tc, tr, hc = sizes.tc, sizes.tr, sizes.hc
    share = draft.shape[0] - cols.shape[0]
    beside[:share] = draft[:share]
    cols[...] = draft[share:].astype(F32)
    for to, rows, at in ((0, north, 0), (tr + 1, south, tc), (tr + 2, south, 2 * tc)):
        put_columns(cols, to, rows[at : at + 16], rows[at + tc - 16 : at + tc])
    ends = [south[at : at + 16] for at in (3 * tc, 3 * tc + hc)]
    put_cotangent(cols, sizes.hr, jnp.concatenate(ends, axis=1))
    beside[share:] = cols[...].astype(BF16)
    edge[...] = cols[...].astype(BF16)


def pass_kernel(beside, edge, *refs):
    far, passed = refs[:-1], refs[-1]
    length, share = far[0].shape[0], beside.shape[0] - edge.shape[0]
    for j, block in enumerate(far):
        passed[j * length : (j + 1) * length] = block[...]
    passed[len(far) * length :] = beside[:share]


def spread_kernel(sizes, region, cot, core_rows, far_rows, beside, edge, *refs):
    x, cot_all, north, south, west, east, left, ext, cols = refs
    choose(lax.rem(lax.axis_index("row"), 2) == 0, core_rows, far_rows, south, north)
    choose(lax.rem(lax.axis_index("col"), 2) == 0, beside.at[beside.shape[0] - edge.shape[0] :], edge, east, west)
    cin, tc, tr, hc = region.shape[2], sizes.tc, sizes.tr, sizes.hc
    tiles = cin // 128
    for v in range(tiles):
        at = (2 * tiles + v) * 32
        left[:, v * 128 : (v + 1) * 128] = west[at : at + 32].astype(F32)
    cols[...] = jnp.zeros_like(cols)
    for v in range(cin // 128):
        lanes = slice(v * 128, (v + 1) * 128)
        for r in range(tr + 3):
            if r == 0:
                row = north[:tc, lanes]
            elif r <= tr:
                row = region[r - 1, :, lanes]
            else:
                row = south[(r - tr) * tc : (1 + r - tr) * tc, lanes]
            ext[v, r, 8 : 8 + tc] = row.astype(F32)
            ext[v, r, 7:8] = left[r : r + 1, lanes]
            cols[0, v, r : r + 1] = ext[v, r, 7 + tc : 8 + tc]
        for b in (1, 2):
            at = ((b - 1) * tiles + v) * 32
            cols[b, v, :32] = east[at : at + 32].astype(F32)
        for b in range(3):
            base = b * sizes.band
            for r in list(range(0, tr + 3, 2)) + list(range(1, tr + 3, 2)):
                picked = ext[v, r, pl.ds(7 + b, hc, stride=2)]
                x[base : base + hc, lanes] = picked.astype(BF16)
                base += hc
            for a in range(3):
                at = sizes.tap_side(3 * a + b)
                x[at : at + 16, lanes] = cols[b, v, pl.ds(a, 16, stride=2)].astype(BF16)
    half = cot_all.shape[1] // 2
    cot_all[: sizes.main] = cot[...].reshape(sizes.main, 2 * half)
    cot_all[sizes.main : sizes.wide, :half] = south[3 * tc : 3 * tc + hc]
    cot_all[sizes.main : sizes.wide, half:] = south[3 * tc + hc :]
    for v in range(2 * half // 128):
        at = 3 * tiles * 32 + v * 16
        cot_all[sizes.wide :, v * 128 : (v + 1) * 128] = east[at : at + 16]


def first_kernel(sizes, halves, x, *refs):
    hidden, slope_one, hidden_two, slope_two, back, reduce_t = refs[3:9]
    pre, group_t, group, front, pre_two, beside = refs[9:]
    cin = reduce_t.shape[1]
    mid = reduce_t.shape[0]
    shard = mid // (2 * halves)
    lane = lax.broadcasted_iota(jnp.int32, (GW, 128), 1)
    for block, first in pieces(halves, shard, *refs[:3], beside):
        rows = pl.ds(pl.multiple_of(first, 16), shard)
        for v in range(cin // 128):
            reduce_t[rows, v * 128 : (v + 1) * 128] = block[v * shard : (v + 1) * shard]
        at = cin // 128 * shard
        group_t[rows, :128] = block[at : at + shard]
        tail = block[block.shape[0] - GW :].astype(F32)
        for i, part in enumerate(unfold(tail, shard)):
            rows = pl.ds(pl.multiple_of(first + i * GW, 16), GW)
            group_t[rows, 128:] = jnp.where(lane < GW, part, 0.0).astype(BF16)
    pre[...] = dot(x[...], reduce_t[...], ((1,), (1,)))
    group[...] = group_t[...].astype(F32).T.astype(BF16)
    row_group = lax.broadcasted_iota(jnp.int32, (HALF, HALF), 0) // GW
    lane_group = lax.broadcasted_iota(jnp.int32, (HALF, HALF), 1) // GW
    mask = jnp.where(row_group == lane_group, 1.0, 0.0).astype(BF16)
    for n in range(mid // HALF):
        for tap in range(TAPS):
            rows = group[tap * GW : (tap + 1) * GW, n * HALF : (n + 1) * HALF]
            dense = jnp.concatenate([rows] * (HALF // GW), axis=0) * mask
            front[n, tap * HALF : (tap + 1) * HALF] = dense
            spot = BACK.index(tap)
            back[n, :, spot * HALF : (spot + 1) * HALF] = dense

    planes = sizes.planes()
    first = 0
    for start in sorted(planes) + [sizes.pixels]:
        for at in range(first, start, 32):
            rows = slice(at, min(at + 32, start))
            value = pre[rows, :]
            hidden[rows, :] = (value * sigmoid(value)).astype(BF16)
        first = start + sizes.main
    for i, start in enumerate(planes):
        for at in range(0, sizes.main, 32):
            rows = slice(start + at, start + at + 32)
            value = pre[rows, :]
            sigma = sigmoid(value)
            active = value * sigma
            hidden[rows, :] = active.astype(BF16)
            rows = slice(i * sizes.main + at, i * sizes.main + at + 32)
            slope_one[rows, :] = sigma + active * (1.0 - sigma)
    for n in range(mid // HALF):
        lanes = slice(n * HALF, (n + 1) * HALF)
        patches = []
        for tap in range(TAPS):
            at, side = sizes.tap(tap), sizes.tap_side(tap)
            patches.append(
                jnp.concatenate(
                    [hidden[at : at + sizes.wide, lanes], hidden[side : side + 16, lanes]], axis=0
                )
            )
        pre_two[:, lanes] = dot(jnp.concatenate(patches, axis=1), front[n])
    value = pre_two[...]
    sigma = sigmoid(value)
    active = value * sigma
    hidden_two[...] = active.astype(BF16)
    slope_two[...] = sigma + active * (1.0 - sigma)


def split_out(halves, total, shard, rest, keeps, give):
    tiles = [at for at in range(0, total.shape[1], 128) if at != rest]
    h, low, core = place()
    keep = low + core - 2 * low * core
    for j in range(halves):
        base = 2 * lax.rem(h + j, halves)
        mine = pl.ds(pl.multiple_of((base + keep) * shard, shard), shard)
        theirs = pl.ds(pl.multiple_of((base + 1 - keep) * shard, shard), shard)
        for i, at in enumerate(tiles):
            slab = slice(i * shard, (i + 1) * shard)
            keeps[j][slab] = total[mine, at : at + 128]
            give[j, slab] = total[theirs, at : at + 128].astype(BF16)
        keeps[j][len(tiles) * shard :] = fold(total[mine, rest : rest + 128])
        give[j, len(tiles) * shard :] = fold(total[theirs, rest : rest + 128]).astype(BF16)


def second_kernel(sizes, halves, x, hidden_two, slope_two, cot, *refs):
    active_three, grad_two, grad_side, own, short_t, total, expand_t, shift, beside = refs[3:]
    mid = expand_t.shape[1]
    width = expand_t.shape[0]
    shard = width // (2 * halves)
    cin = short_t.shape[1]
    for block, first in pieces(halves, shard, *refs[:3], beside):
        rows = pl.ds(pl.multiple_of(first, 16), shard)
        at = (cin // 128 + 1) * shard
        for ref in (expand_t, short_t):
            for v in range(ref.shape[1] // 128):
                ref[rows, v * 128 : (v + 1) * 128] = block[at : at + shard]
                at += shard
    at, side = sizes.tap(4), sizes.tap_side(4)
    strided = jnp.concatenate([x[at : at + sizes.wide], x[side : side + 16]], axis=0)
    summed = dot(hidden_two[...], expand_t[...], ((1,), (1,))) + dot(
        strided, short_t[...], ((1,), (1,))
    )
    sigma = sigmoid(summed)
    active = summed * sigma
    active_three[...] = active[: sizes.main].astype(BF16)
    grad_sum = (cot[...].astype(F32) * (sigma + active * (1.0 - sigma))).astype(BF16)
    own[...] = grad_sum[: sizes.main]
    flipped = grad_sum[: sizes.main].astype(F32).T.astype(BF16)
    total[:, :mid] = dot(flipped, hidden_two[: sizes.main])
    total[:, mid:] = dot(flipped, strided[: sizes.main])
    back = dot(grad_sum, expand_t[...]) * slope_two[...]
    grad_two[...] = back[: sizes.wide].astype(BF16)
    for i in range(sizes.hr + 1):
        shift[i, : sizes.hc] = back[i * sizes.hc : (i + 1) * sizes.hc]
        shift[i, sizes.hc : sizes.hc + 1] = back[sizes.wide + i : sizes.wide + i + 1]
    for i in range(sizes.hr + 1):
        grad_side[i * sizes.hc : (i + 1) * sizes.hc] = shift[i, 1 : sizes.hc + 1].astype(BF16)


def third_kernel(
    sizes, halves, cin, x, hidden, slope_one, back, grad_two, grad_side, late, *refs
):
    grad_one, give = refs[:2]
    keeps = refs[2 : 2 + halves]
    total = refs[2 + halves]
    mid = hidden.shape[1]
    main, hc = sizes.main, sizes.hc
    shard = mid // (2 * halves)
    down = slice(hc, hc + main)
    own = slice(0, main)
    for n in range(mid // HALF):
        lanes = slice(n * HALF, (n + 1) * HALF)
        two, low = grad_two[own, lanes], grad_two[down, lanes]
        side, corner = grad_side[own, lanes], grad_side[down, lanes]
        first = 0
        for i, parts in enumerate(((two,), (two, side), (two, low), (two, low, side, corner))):
            left = jnp.concatenate(parts, axis=1)
            last = first + len(parts) * HALF
            spread = dot(left, back[n, :, first:last], ((1,), (1,)))
            first = last
            rows = slice(i * main, (i + 1) * main)
            grad_one[rows, lanes] = (spread * slope_one[rows, lanes]).astype(BF16)
    flat = jnp.concatenate([x[at : at + main] for at in sizes.planes()], axis=0)
    total[:, :cin] = dot(grad_one[...].astype(F32).T.astype(BF16), flat)
    flipped = grad_two[own, :].astype(F32).T.astype(BF16)
    lane = lax.broadcasted_iota(jnp.int32, (GW, 128), 1) // GW
    for n in range(mid // HALF):
        lanes = slice(n * HALF, (n + 1) * HALF)
        sums = [jnp.zeros((GW, 128), F32)] * (HALF // GW)
        for tap in range(TAPS):
            at = sizes.tap(tap)
            piece = dot(flipped[n * HALF : (n + 1) * HALF], hidden[at : at + main, lanes])
            for q in range(HALF // GW):
                tile = q // 8
                block = piece[q * GW : (q + 1) * GW, tile * 128 : (tile + 1) * 128]
                block = pltpu.roll(block, (GW * (tap - q)) % 128, 1)
                if tap < 8:
                    sums[q] = jnp.where(lane == tap, block, sums[q])
                else:
                    rows = slice(n * HALF + q * GW, n * HALF + (q + 1) * GW)
                    total[rows, cin : cin + 128] = sums[q]
                    total[rows, cin + 128 : cin + 256] = jnp.where(lane == 0, block, 0.0)
    total[:, cin + 256 :] = late[...]
    split_out(halves, total, shard, cin + 128, keeps, give)


def outputs_kernel(sizes, grad_one, reduce_t, grad_sum, short_t, active, block_out, region_grad, planes, spread_out):
    main, hc, cin = sizes.main, sizes.hc, reduce_t.shape[1]
    block_out[...] = active[...].reshape(block_out.shape)
    planes[...] = dot(grad_one[...], reduce_t[...])
    planes[:main] += dot(grad_sum[...], short_t[...])
    for i in range(4):
        for r in range(sizes.hr):
            at = i * main + r * hc
            for v in range(cin // 128):
                lanes = slice(v * 128, (v + 1) * 128)
                spread_out[v, 2 * r + i // 2, pl.ds(i % 2, hc, stride=2)] = planes[at : at + hc, lanes]
    for v in range(cin // 128):
        region_grad[:, :, v * 128 : (v + 1) * 128] = spread_out[v].astype(BF16)


def call(kernel, out_shape, scratch, *operands, flops=0, space=pltpu.VMEM, limit=VMEM_LIMIT):
    sizes = sum(o.size * o.dtype.itemsize for o in operands)
    sizes += sum(o.size * o.dtype.itemsize for o in jax.tree.leaves(out_shape))
    return pl.pallas_call(
        kernel,
        out_shape=out_shape,
        in_specs=[pl.BlockSpec(memory_space=space)] * len(operands),
        out_specs=jax.tree.map(lambda _: pl.BlockSpec(memory_space=pltpu.VMEM), out_shape),
        scratch_shapes=scratch,
        compiler_params=pltpu.CompilerParams(vmem_limit_bytes=limit),
        cost_estimate=pl.CostEstimate(flops=flops, bytes_accessed=sizes, transcendentals=0),
    )(*operands)


def finish_kernel(total, across, *outs):
    value = total[...].astype(F32) + across[...].astype(F32)
    shard = outs[0].shape[0]
    at = 0
    for out in outs:
        for v in range(out.shape[1] // 128):
            out[:, v * 128 : (v + 1) * 128] = value[at : at + shard]
            at += shard
    rest = outs[1].shape[1] - 128
    for i, part in enumerate(unfold(value[at:], shard)):
        outs[1][i * GW : (i + 1) * GW, 128:] = part[:, :rest]


def both(rows, cols, target):
    pairs = []
    for r in range(rows):
        for c in range(cols):
            to = target(r % 2, c // 2, c % 2)
            if to is not None:
                pairs.append((r * cols + c, r * cols + 2 * to[0] + to[1]))
    return pairs


def swap_odd(x, axis):
    pairs = []
    for i in range(1, lax.axis_size(axis) - 1, 2):
        pairs += [(i, i + 1), (i + 1, i)]
    return lax.ppermute(x, axis, pairs)


def swap_even(x, axis):
    return lax.ppermute(x, axis, [(i, i ^ 1) for i in range(lax.axis_size(axis))])


def cross(x, j):
    rows, cols = lax.axis_size("row"), lax.axis_size("col")
    halves = cols // 2

    def target(k, h, low):
        return None if j == k == 0 else ((h + j) % halves, low ^ k)

    return lax.ppermute(x, ("row", "col"), both(rows, cols, target))


def reduce(keeps, give):
    rows, halves = lax.axis_size("row"), lax.axis_size("col") // 2
    core = lax.axis_index("row") % 2
    other = swap_even(give, "row")
    sums = [keeps[j] + other[j].astype(F32) for j in range(halves)]
    total = None
    for j in sorted(range(halves), key=lambda j: (j > 0, -min(j, halves - j), -j)):
        came = cross(sums[j].astype(BF16), j).astype(F32)
        if j == 0:
            came = jnp.where(core == 0, sums[0], came)
        total = came if total is None else total + came
    if rows != 4:
        return lax.psum(total, "row"), jnp.zeros_like(total)
    total = (total + swap_even(total, "row")).astype(BF16)
    return total, lax.ppermute(total, "row", [(r, r ^ 2) for r in range(4)])


def per_device(region, reduce_weight, group_weight, expand_weight, shortcut_weight, cotangent):
    tile_rows, tile_cols, cin = region.shape
    sizes = Sizes(tile_rows, tile_cols)
    halves = lax.axis_size("col") // 2
    mid, shard = expand_weight.shape
    width = shard * lax.axis_size("col")
    taps = group_weight.shape[0]
    early, late = cin + 256, mid + cin
    length = (early + late) // 128 * shard - shard + GW
    share = (length + 31) // 32 * 16
    halo = 3 * cin // 128 * 32 + width // 128 * 16

    def shape(dims, dtype=BF16):
        return jax.ShapeDtypeStruct(dims, dtype)

    def scratch(*dims, dtype=F32):
        return pltpu.VMEM(dims, dtype)

    inputs = (
        region, cotangent, reduce_weight.T, group_weight.T, expand_weight.T, shortcut_weight.T,
    )
    weights, outer, draft = call(
        functools.partial(send_kernel, sizes),
        (
            shape((length, 128)),
            shape((4 * tile_cols, cin)),
            shape((share + halo, 128)),
        ),
        [scratch(halo, 128)]
        + [scratch(*given.shape, dtype=BF16) for given in inputs]
        + [pltpu.SemaphoreType.DMA((len(inputs),))],
        *inputs,
        space=pltpu.HBM,
        limit=62 * 1024 * 1024,
    )
    far = [cross(weights, j) for j in range(1, halves)]
    core_rows = swap_even(outer, "row")
    far_rows = swap_odd(outer, "row")
    rows_scratch = [scratch(4 * tile_cols, cin, dtype=BF16)] * 2
    beside, edge = call(
        functools.partial(columns_kernel, sizes),
        (shape(draft.shape), shape((halo, 128))),
        rows_scratch + [scratch(halo, 128)],
        core_rows, far_rows, draft,
    )
    beside, edge = swap_even(beside, "col"), swap_odd(edge, "col")
    x, cot_all = call(
        functools.partial(spread_kernel, sizes),
        (shape((sizes.pixels, cin)), shape((sizes.out, width))),
        rows_scratch
        + [
            scratch(halo, 128, dtype=BF16),
            scratch(halo, 128, dtype=BF16),
            scratch(32, cin),
            scratch(cin // 128, tile_rows + 3, 8 + tile_cols, 128),
            scratch(3, cin // 128, 40, 128),
        ],
        region, cotangent, core_rows, far_rows, beside, edge,
    )
    passed = call(
        pass_kernel,
        shape(((halves - 1) * length + share, 128)),
        [],
        beside, edge, *far,
    )
    blocks = [weights, passed, swap_even(passed, "row")]
    hidden, slope_one, hidden_two, slope_two, back, reduce_t = call(
        functools.partial(first_kernel, sizes, halves),
        (
            shape((sizes.pixels, mid)),
            shape((4 * sizes.main, mid), F32),
            shape((sizes.out, mid)),
            shape((sizes.out, mid), F32),
            shape((mid // HALF, HALF, TAPS * HALF)),
            shape((mid, cin)),
        ),
        [
            scratch(sizes.pixels, mid),
            scratch(mid, 256, dtype=BF16),
            scratch(256, mid, dtype=BF16),
            scratch(mid // HALF, TAPS * HALF, HALF, dtype=BF16),
            scratch(sizes.out, mid),
            scratch(length, 128, dtype=BF16),
        ],
        x, *blocks,
        flops=2 * sizes.pixels * cin * mid + 2 * sizes.out * TAPS * HALF * mid,
    )
    active_three, grad_two, grad_side, grad_sum, short_t, late_total = call(
        functools.partial(second_kernel, sizes, halves),
        (
            shape((sizes.main, width)),
            shape((sizes.wide, mid)),
            shape((sizes.wide, mid)),
            shape((sizes.main, width)),
            shape((width, cin)),
            shape((width, late), F32),
        ),
        [
            scratch(width, mid, dtype=BF16),
            scratch(sizes.hr + 1, 24, mid),
            scratch(length, 128, dtype=BF16),
        ],
        x, hidden_two, slope_two, cot_all, *blocks,
        flops=6 * sizes.out * width * (mid + cin),
    )
    grad_one, give, *keeps = call(
        functools.partial(third_kernel, sizes, halves, cin),
        (shape((4 * sizes.main, mid)), shape((halves, length, 128)))
        + (shape((length, 128), F32),) * halves,
        [
            scratch(mid, early + late),
        ],
        x, hidden, slope_one, back, grad_two, grad_side, late_total,
        flops=2 * 4 * sizes.main * cin * mid + 4 * sizes.main * TAPS * HALF * mid,
    )
    block_out, region_grad = call(
        functools.partial(outputs_kernel, sizes),
        (shape((sizes.hr, sizes.hc, width)), shape(region.shape)),
        [
            scratch(4 * sizes.main, cin),
            scratch(cin // 128, tile_rows, tile_cols, 128),
        ],
        grad_one, reduce_t, grad_sum, short_t, active_three,
        flops=2 * 4 * sizes.main * cin * mid,
    )
    total, across = reduce(keeps, give)
    grads = call(
        finish_kernel,
        tuple(shape((shard, lanes), F32) for lanes in (cin, taps, mid, cin)),
        [],
        total, across,
    )
    return (block_out, region_grad, *(grad.T for grad in grads))


def solution(mesh):
    tiles, split = P("row", "col", None), P(None, "col")
    return jax.shard_map(
        per_device,
        mesh=mesh,
        in_specs=(tiles, split, split, split, split, tiles),
        out_specs=(tiles, tiles, split, split, split, split),
        check_vma=False,
    )
```

```python
import functools

import jax
import jax.numpy as jnp
from jax import lax
from jax.experimental import pallas as pl
from jax.experimental.pallas import tpu as pltpu
from jax.sharding import PartitionSpec as P

GW = 16
TAPS = 9
HALF = 256
BACK = (4, 5, 3, 7, 1, 8, 2, 6, 0)
F32 = jnp.float32
BF16 = jnp.bfloat16
VMEM_LIMIT = 40 * 1024 * 1024


class Sizes:
    def __init__(self, tile_rows, tile_cols):
        self.tr, self.tc = tile_rows, tile_cols
        self.hr, self.hc = tile_rows // 2, tile_cols // 2
        self.odd = (self.hr + 2) * self.hc
        self.even = (self.hr + 1) * self.hc
        self.band = self.odd + self.even
        self.side = 3 * self.band
        self.pixels = self.side + TAPS * 16
        self.main = self.hr * self.hc
        self.wide = self.main + self.hc
        self.out = self.wide + 16

    def tap(self, tap):
        a, b = divmod(tap, 3)
        return b * self.band + (0, self.odd, self.hc)[a]

    def tap_side(self, tap):
        return self.side + tap * 16

    def planes(self):
        return (
            self.band + self.odd,
            2 * self.band + self.odd,
            self.band + self.hc,
            2 * self.band + self.hc,
        )


def dot(a, b, dims=((1,), (0,))):
    return lax.dot_general(a, b, (dims, ((), ())), preferred_element_type=F32)


def sigmoid(value):
    below = 1.0 + jnp.exp(jnp.minimum(-value, 80.0))
    guess = pl.reciprocal(below, approx=True)
    return guess * (2.0 - below * guess)


def place():
    col = lax.axis_index("col")
    return col // 2, lax.rem(col, 2), lax.rem(lax.axis_index("row"), 2)


def fold(block):
    parts = [
        pltpu.roll(block[at : at + GW], at, 1) if at else block[:GW]
        for at in range(0, block.shape[0], GW)
    ]
    return sum(parts[1:], parts[0])


def unfold(tail, rows):
    return [pltpu.roll(tail, (128 - at) % 128, 1) if at else tail for at in range(0, rows, GW)]


def pieces(halves, shard, own, passed, swapped, beside):
    h, low, core = place()
    length = own.shape[0]
    flips = (low + core - 2 * low * core, 1 - low - core + 2 * low * core)
    found = [(own, (2 * h + low) * shard)]
    for ref, flip in zip((passed, swapped), flips, strict=True):
        for j in range(1, halves):
            spot = 2 * lax.rem(h - j + halves, halves) + flip
            found.append((ref.at[(j - 1) * length : j * length], spot * shard))
    first = (halves - 1) * length
    share = passed.shape[0] - first
    for ref, part in ((passed, core), (swapped, 1 - core)):
        rows = pl.ds(pl.multiple_of(part * (length - share), 16), share)
        beside[rows, :] = ref[first : first + share]
    return found + [(beside, (2 * h + 1 - low) * shard)]


def send_kernel(sizes, *refs):
    given, (weights, outer, draft, cols) = refs[:6], refs[6:10]
    local, arrived = refs[10:16], refs[16]
    copies = [
        pltpu.make_async_copy(given[i], local[i], arrived.at[i]) for i in range(len(given))
    ]
    for copy in copies:
        copy.start()
    for copy in copies:
        copy.wait()
    region, cot, reduce_t, group_t, expand_t, short_t = local
    shard, taps = group_t.shape
    cin, mid = reduce_t.shape[1], expand_t.shape[1]
    tiles = [reduce_t[:, at : at + 128] for at in range(0, cin, 128)]
    tiles.append(group_t[:, :128])
    tiles += [expand_t[:, at : at + 128] for at in range(0, mid, 128)]
    tiles += [short_t[:, at : at + 128] for at in range(0, cin, 128)]
    for i, tile in enumerate(tiles):
        weights[i * shard : (i + 1) * shard] = tile
    pad = jnp.zeros((shard, 256 - taps), BF16)
    rest = jnp.concatenate([group_t[...], pad], axis=1)[:, 128:].astype(F32)
    weights[len(tiles) * shard :] = fold(rest).astype(BF16)
    tc, half = sizes.tc, cot.shape[2] // 2
    for i, r in enumerate((sizes.tr - 1, 0, 1)):
        outer[i * tc : (i + 1) * tc] = region[r]
    outer[3 * tc : 3 * tc + sizes.hc] = cot[0, :, :half]
    outer[3 * tc + sizes.hc :] = cot[0, :, half:]
    cols[...] = jnp.zeros_like(cols)
    for r in range(sizes.tr):
        put_columns(cols, r + 1, region[r, :16], region[r, tc - 16 :])
    for i in range(sizes.hr):
        put_cotangent(cols, i, cot[i, :16])
    share = draft.shape[0] - cols.shape[0]
    core = lax.rem(lax.axis_index("row"), 2)
    first = pl.multiple_of(core * (weights.shape[0] - share), 16)
    draft[:share] = weights[pl.ds(first, share), :]
    draft[share:] = cols[...].astype(BF16)


def put_columns(cols, row, head, tail):
    head, tail = head.astype(F32), tail.astype(F32)
    tiles = head.shape[1] // 128
    for i, pixel in enumerate((tail[15:16], head[0:1], head[1:2])):
        for v in range(tiles):
            at = (i * tiles + v) * 32 + row
            cols[at : at + 1] = pixel[:, v * 128 : (v + 1) * 128]


def put_cotangent(cols, row, head):
    pixel = head.astype(F32)[0:1]
    tiles = pixel.shape[1] // 128
    for v in range(tiles):
        at = cols.shape[0] - (tiles - v) * 16 + row
        cols[at : at + 1] = pixel[:, v * 128 : (v + 1) * 128]


def choose(first, one, other, to_one, to_other):
    @pl.when(first)
    def _():
        to_one[...] = one[...]
        to_other[...] = other[...]

    @pl.when(jnp.logical_not(first))
    def _():
        to_one[...] = other[...]
        to_other[...] = one[...]


def columns_kernel(sizes, core_rows, far_rows, draft, beside, edge, north, south, cols):
    choose(lax.rem(lax.axis_index("row"), 2) == 0, core_rows, far_rows, south, north)
    tc, tr, hc = sizes.tc, sizes.tr, sizes.hc
    share = draft.shape[0] - cols.shape[0]
    beside[:share] = draft[:share]
    cols[...] = draft[share:].astype(F32)
    for to, rows, at in ((0, north, 0), (tr + 1, south, tc), (tr + 2, south, 2 * tc)):
        put_columns(cols, to, rows[at : at + 16], rows[at + tc - 16 : at + tc])
    ends = [south[at : at + 16] for at in (3 * tc, 3 * tc + hc)]
    put_cotangent(cols, sizes.hr, jnp.concatenate(ends, axis=1))
    low = lax.rem(lax.axis_index("col"), 2)
    skip = cols.shape[0] - edge.shape[0]
    for out, first in ((beside.at[share:], skip * low), (edge, skip * (1 - low))):
        first = pl.multiple_of(first, 16)
        out[...] = cols[pl.ds(first, out.shape[0]), :].astype(BF16)


def pass_kernel(beside, edge, *refs):
    far, passed = refs[:-1], refs[-1]
    length, share = far[0].shape[0], beside.shape[0] - edge.shape[0]
    for j, block in enumerate(far):
        passed[j * length : (j + 1) * length] = block[...]
    passed[len(far) * length :] = beside[:share]


def spread_kernel(sizes, region, cot, core_rows, far_rows, beside, edge, *refs):
    x, cot_all, north, south, west, east, left, ext, cols = refs
    choose(lax.rem(lax.axis_index("row"), 2) == 0, core_rows, far_rows, south, north)
    choose(lax.rem(lax.axis_index("col"), 2) == 0, beside.at[beside.shape[0] - edge.shape[0] :], edge, east, west)
    cin, tc, tr, hc = region.shape[2], sizes.tc, sizes.tr, sizes.hc
    tiles = cin // 128
    for v in range(tiles):
        left[:, v * 128 : (v + 1) * 128] = west[v * 32 : (v + 1) * 32].astype(F32)
    cols[...] = jnp.zeros_like(cols)
    for v in range(cin // 128):
        lanes = slice(v * 128, (v + 1) * 128)
        for r in range(tr + 3):
            if r == 0:
                row = north[:tc, lanes]
            elif r <= tr:
                row = region[r - 1, :, lanes]
            else:
                row = south[(r - tr) * tc : (1 + r - tr) * tc, lanes]
            ext[v, r, 8 : 8 + tc] = row.astype(F32)
            ext[v, r, 7:8] = left[r : r + 1, lanes]
            cols[0, v, r : r + 1] = ext[v, r, 7 + tc : 8 + tc]
        for b in (1, 2):
            at = ((b - 1) * tiles + v) * 32
            cols[b, v, :32] = east[at : at + 32].astype(F32)
        for b in range(3):
            base = b * sizes.band
            for r in list(range(0, tr + 3, 2)) + list(range(1, tr + 3, 2)):
                picked = ext[v, r, pl.ds(7 + b, hc, stride=2)]
                x[base : base + hc, lanes] = picked.astype(BF16)
                base += hc
            for a in range(3):
                at = sizes.tap_side(3 * a + b)
                x[at : at + 16, lanes] = cols[b, v, pl.ds(a, 16, stride=2)].astype(BF16)
    half = cot_all.shape[1] // 2
    cot_all[: sizes.main] = cot[...].reshape(sizes.main, 2 * half)
    cot_all[sizes.main : sizes.wide, :half] = south[3 * tc : 3 * tc + hc]
    cot_all[sizes.main : sizes.wide, half:] = south[3 * tc + hc :]
    for v in range(2 * half // 128):
        at = 2 * tiles * 32 + v * 16
        cot_all[sizes.wide :, v * 128 : (v + 1) * 128] = east[at : at + 16]


def forward_part(sizes, halves, x, *refs):
    hidden, slope_one, hidden_two, slope_two, back, reduce_t = refs[3:9]
    pre, group_t, group, front, pre_two, beside = refs[9:]
    cin = reduce_t.shape[1]
    mid = reduce_t.shape[0]
    shard = mid // (2 * halves)
    lane = lax.broadcasted_iota(jnp.int32, (GW, 128), 1)
    for block, first in pieces(halves, shard, *refs[:3], beside):
        rows = pl.ds(pl.multiple_of(first, 16), shard)
        for v in range(cin // 128):
            reduce_t[rows, v * 128 : (v + 1) * 128] = block[v * shard : (v + 1) * shard]
        at = cin // 128 * shard
        group_t[rows, :128] = block[at : at + shard]
        tail = block[block.shape[0] - GW :].astype(F32)
        for i, part in enumerate(unfold(tail, shard)):
            rows = pl.ds(pl.multiple_of(first + i * GW, 16), GW)
            group_t[rows, 128:] = jnp.where(lane < GW, part, 0.0).astype(BF16)
    pre[...] = dot(x[...], reduce_t[...], ((1,), (1,)))
    group[...] = group_t[...].astype(F32).T.astype(BF16)
    row_group = lax.broadcasted_iota(jnp.int32, (HALF, HALF), 0) // GW
    lane_group = lax.broadcasted_iota(jnp.int32, (HALF, HALF), 1) // GW
    mask = jnp.where(row_group == lane_group, 1.0, 0.0).astype(BF16)
    for n in range(mid // HALF):
        for tap in range(TAPS):
            rows = group[tap * GW : (tap + 1) * GW, n * HALF : (n + 1) * HALF]
            dense = jnp.concatenate([rows] * (HALF // GW), axis=0) * mask
            front[n, tap * HALF : (tap + 1) * HALF] = dense
            spot = BACK.index(tap)
            back[n, :, spot * HALF : (spot + 1) * HALF] = dense

    planes = sizes.planes()
    first = 0
    for start in sorted(planes) + [sizes.pixels]:
        for at in range(first, start, 32):
            rows = slice(at, min(at + 32, start))
            value = pre[rows, :]
            hidden[rows, :] = (value * sigmoid(value)).astype(BF16)
        first = start + sizes.main
    for i, start in enumerate(planes):
        for at in range(0, sizes.main, 32):
            rows = slice(start + at, start + at + 32)
            value = pre[rows, :]
            sigma = sigmoid(value)
            active = value * sigma
            hidden[rows, :] = active.astype(BF16)
            rows = slice(i * sizes.main + at, i * sizes.main + at + 32)
            slope_one[rows, :] = sigma + active * (1.0 - sigma)
    for n in range(mid // HALF):
        lanes = slice(n * HALF, (n + 1) * HALF)
        patches = []
        for tap in range(TAPS):
            at, side = sizes.tap(tap), sizes.tap_side(tap)
            patches.append(
                jnp.concatenate(
                    [hidden[at : at + sizes.wide, lanes], hidden[side : side + 16, lanes]], axis=0
                )
            )
        pre_two[:, lanes] = dot(jnp.concatenate(patches, axis=1), front[n])
    value = pre_two[...]
    sigma = sigmoid(value)
    active = value * sigma
    hidden_two[...] = active.astype(BF16)
    slope_two[...] = sigma + active * (1.0 - sigma)


def split_out(halves, total, shard, rest, keeps, give):
    tiles = [at for at in range(0, total.shape[1], 128) if at != rest]
    h, low, core = place()
    keep = low + core - 2 * low * core
    for j in range(halves):
        base = 2 * lax.rem(h + j, halves)
        mine = pl.ds(pl.multiple_of((base + keep) * shard, shard), shard)
        theirs = pl.ds(pl.multiple_of((base + 1 - keep) * shard, shard), shard)
        for i, at in enumerate(tiles):
            slab = slice(i * shard, (i + 1) * shard)
            keeps[j][slab] = total[mine, at : at + 128]
            give[j, slab] = total[theirs, at : at + 128].astype(BF16)
        keeps[j][len(tiles) * shard :] = fold(total[mine, rest : rest + 128])
        give[j, len(tiles) * shard :] = fold(total[theirs, rest : rest + 128]).astype(BF16)


def middle_part(sizes, halves, x, hidden_two, slope_two, cot, *refs):
    active_three, grad_two, grad_side, own, short_t, total, expand_t, shift, beside = refs[3:]
    mid = expand_t.shape[1]
    width = expand_t.shape[0]
    shard = width // (2 * halves)
    cin = short_t.shape[1]
    for block, first in pieces(halves, shard, *refs[:3], beside):
        rows = pl.ds(pl.multiple_of(first, 16), shard)
        at = (cin // 128 + 1) * shard
        for ref in (expand_t, short_t):
            for v in range(ref.shape[1] // 128):
                ref[rows, v * 128 : (v + 1) * 128] = block[at : at + shard]
                at += shard
    at, side = sizes.tap(4), sizes.tap_side(4)
    strided = jnp.concatenate([x[at : at + sizes.wide], x[side : side + 16]], axis=0)
    summed = dot(hidden_two[...], expand_t[...], ((1,), (1,))) + dot(
        strided, short_t[...], ((1,), (1,))
    )
    sigma = sigmoid(summed)
    active = summed * sigma
    active_three[...] = active[: sizes.main].astype(BF16)
    grad_sum = (cot[...].astype(F32) * (sigma + active * (1.0 - sigma))).astype(BF16)
    own[...] = grad_sum[: sizes.main]
    flipped = grad_sum[: sizes.main].astype(F32).T.astype(BF16)
    total[:, :mid] = dot(flipped, hidden_two[: sizes.main])
    total[:, mid:] = dot(flipped, strided[: sizes.main])
    back = dot(grad_sum, expand_t[...]) * slope_two[...]
    grad_two[...] = back[: sizes.wide].astype(BF16)
    for i in range(sizes.hr + 1):
        shift[i, : sizes.hc] = back[i * sizes.hc : (i + 1) * sizes.hc]
        shift[i, sizes.hc : sizes.hc + 1] = back[sizes.wide + i : sizes.wide + i + 1]
    for i in range(sizes.hr + 1):
        grad_side[i * sizes.hc : (i + 1) * sizes.hc] = shift[i, 1 : sizes.hc + 1].astype(BF16)


def backward_part(
    sizes, halves, cin, x, hidden, slope_one, back, grad_two, grad_side, *refs
):
    grad_one, give = refs[:2]
    keeps = refs[2 : 2 + halves]
    total = refs[2 + halves]
    mid = hidden.shape[1]
    main, hc = sizes.main, sizes.hc
    shard = mid // (2 * halves)
    down = slice(hc, hc + main)
    own = slice(0, main)
    for n in range(mid // HALF):
        lanes = slice(n * HALF, (n + 1) * HALF)
        two, low = grad_two[own, lanes], grad_two[down, lanes]
        side, corner = grad_side[own, lanes], grad_side[down, lanes]
        first = 0
        for i, parts in enumerate(((two,), (two, side), (two, low), (two, low, side, corner))):
            left = jnp.concatenate(parts, axis=1)
            last = first + len(parts) * HALF
            spread = dot(left, back[n, :, first:last], ((1,), (1,)))
            first = last
            rows = slice(i * main, (i + 1) * main)
            grad_one[rows, lanes] = (spread * slope_one[rows, lanes]).astype(BF16)
    flat = jnp.concatenate([x[at : at + main] for at in sizes.planes()], axis=0)
    total[:, :cin] = dot(grad_one[...].astype(F32).T.astype(BF16), flat)
    flipped = grad_two[own, :].astype(F32).T.astype(BF16)
    lane = lax.broadcasted_iota(jnp.int32, (GW, 128), 1) // GW
    for n in range(mid // HALF):
        lanes = slice(n * HALF, (n + 1) * HALF)
        sums = [jnp.zeros((GW, 128), F32)] * (HALF // GW)
        for tap in range(TAPS):
            at = sizes.tap(tap)
            piece = dot(flipped[n * HALF : (n + 1) * HALF], hidden[at : at + main, lanes])
            for q in range(HALF // GW):
                tile = q // 8
                block = piece[q * GW : (q + 1) * GW, tile * 128 : (tile + 1) * 128]
                block = pltpu.roll(block, (GW * (tap - q)) % 128, 1)
                if tap < 8:
                    sums[q] = jnp.where(lane == tap, block, sums[q])
                else:
                    rows = slice(n * HALF + q * GW, n * HALF + (q + 1) * GW)
                    total[rows, cin : cin + 128] = sums[q]
                    total[rows, cin + 128 : cin + 256] = jnp.where(lane == 0, block, 0.0)
    split_out(halves, total, shard, cin + 128, keeps, give)


def main_kernel(sizes, halves, cin, x, cot, own, passed, swapped, *refs):
    active_three, grad_sum, short_t, reduce_t, grad_one, give = refs[:6]
    keeps, refs = refs[6 : 6 + halves], refs[6 + halves :]
    hidden, slope_one, hidden_two, slope_two, back, pre, group_t, group, front = refs[:9]
    pre_two, beside, grad_two, grad_side, expand_t, shift, total = refs[9:]
    weights = (own, passed, swapped)
    forward_part(
        sizes, halves, x, *weights, hidden, slope_one, hidden_two, slope_two, back, reduce_t,
        pre, group_t, group, front, pre_two, beside,
    )
    middle_part(
        sizes, halves, x, hidden_two, slope_two, cot, *weights, active_three, grad_two, grad_side,
        grad_sum, short_t, total.at[:, cin + 256 :], expand_t, shift, beside,
    )
    backward_part(
        sizes, halves, cin, x, hidden, slope_one, back, grad_two, grad_side, grad_one, give,
        *keeps, total,
    )


def outputs_kernel(sizes, grad_one, reduce_t, grad_sum, short_t, active, block_out, region_grad, planes, spread_out):
    main, hc, cin = sizes.main, sizes.hc, reduce_t.shape[1]
    block_out[...] = active[...].reshape(block_out.shape)
    planes[...] = dot(grad_one[...], reduce_t[...])
    planes[:main] += dot(grad_sum[...], short_t[...])
    for i in range(4):
        for r in range(sizes.hr):
            at = i * main + r * hc
            for v in range(cin // 128):
                lanes = slice(v * 128, (v + 1) * 128)
                spread_out[v, 2 * r + i // 2, pl.ds(i % 2, hc, stride=2)] = planes[at : at + hc, lanes]
    for v in range(cin // 128):
        region_grad[:, :, v * 128 : (v + 1) * 128] = spread_out[v].astype(BF16)


def call(kernel, out_shape, scratch, *operands, flops=0, space=pltpu.VMEM, limit=VMEM_LIMIT):
    sizes = sum(o.size * o.dtype.itemsize for o in operands)
    sizes += sum(o.size * o.dtype.itemsize for o in jax.tree.leaves(out_shape))
    return pl.pallas_call(
        kernel,
        out_shape=out_shape,
        in_specs=[pl.BlockSpec(memory_space=space)] * len(operands),
        out_specs=jax.tree.map(lambda _: pl.BlockSpec(memory_space=pltpu.VMEM), out_shape),
        scratch_shapes=scratch,
        compiler_params=pltpu.CompilerParams(vmem_limit_bytes=limit),
        cost_estimate=pl.CostEstimate(flops=flops, bytes_accessed=sizes, transcendentals=0),
    )(*operands)


def finish_kernel(total, across, *outs):
    value = total[...].astype(F32) + across[...].astype(F32)
    shard = outs[0].shape[0]
    at = 0
    for out in outs:
        for v in range(out.shape[1] // 128):
            out[:, v * 128 : (v + 1) * 128] = value[at : at + shard]
            at += shard
    rest = outs[1].shape[1] - 128
    for i, part in enumerate(unfold(value[at:], shard)):
        outs[1][i * GW : (i + 1) * GW, 128:] = part[:, :rest]


def both(rows, cols, target):
    pairs = []
    for r in range(rows):
        for c in range(cols):
            to = target(r % 2, c // 2, c % 2)
            if to is not None:
                pairs.append((r * cols + c, r * cols + 2 * to[0] + to[1]))
    return pairs


def swap_odd(x, axis):
    pairs = []
    for i in range(1, lax.axis_size(axis) - 1, 2):
        pairs += [(i, i + 1), (i + 1, i)]
    return lax.ppermute(x, axis, pairs)


def swap_even(x, axis):
    return lax.ppermute(x, axis, [(i, i ^ 1) for i in range(lax.axis_size(axis))])


def cross(x, j):
    rows, cols = lax.axis_size("row"), lax.axis_size("col")
    halves = cols // 2

    def target(k, h, low):
        return None if j == k == 0 else ((h + j) % halves, low ^ k)

    return lax.ppermute(x, ("row", "col"), both(rows, cols, target))


def reduce(keeps, give):
    rows, halves = lax.axis_size("row"), lax.axis_size("col") // 2
    core = lax.axis_index("row") % 2
    other = swap_even(give, "row")
    sums = [keeps[j] + other[j].astype(F32) for j in range(halves)]
    total = None
    for j in sorted(range(halves), key=lambda j: (j > 0, -min(j, halves - j), -j)):
        came = cross(sums[j].astype(BF16), j).astype(F32)
        if j == 0:
            came = jnp.where(core == 0, sums[0], came)
        total = came if total is None else total + came
    if rows != 4:
        return lax.psum(total, "row"), jnp.zeros_like(total)
    total = (total + swap_even(total, "row")).astype(BF16)
    return total, lax.ppermute(total, "row", [(r, r ^ 2) for r in range(4)])


def per_device(region, reduce_weight, group_weight, expand_weight, shortcut_weight, cotangent):
    tile_rows, tile_cols, cin = region.shape
    sizes = Sizes(tile_rows, tile_cols)
    halves = lax.axis_size("col") // 2
    mid, shard = expand_weight.shape
    width = shard * lax.axis_size("col")
    taps = group_weight.shape[0]
    early, late = cin + 256, mid + cin
    length = (early + late) // 128 * shard - shard + GW
    share = (length + 31) // 32 * 16
    halo = 3 * cin // 128 * 32 + width // 128 * 16
    sent = halo - cin // 128 * 32

    def shape(dims, dtype=BF16):
        return jax.ShapeDtypeStruct(dims, dtype)

    def scratch(*dims, dtype=F32):
        return pltpu.VMEM(dims, dtype)

    inputs = (
        region, cotangent, reduce_weight.T, group_weight.T, expand_weight.T, shortcut_weight.T,
    )
    weights, outer, draft = call(
        functools.partial(send_kernel, sizes),
        (
            shape((length, 128)),
            shape((4 * tile_cols, cin)),
            shape((share + halo, 128)),
        ),
        [scratch(halo, 128)]
        + [scratch(*given.shape, dtype=BF16) for given in inputs]
        + [pltpu.SemaphoreType.DMA((len(inputs),))],
        *inputs,
        space=pltpu.HBM,
        limit=62 * 1024 * 1024,
    )
    far = [cross(weights, j) for j in range(1, halves)]
    core_rows = swap_even(outer, "row")
    far_rows = swap_odd(outer, "row")
    rows_scratch = [scratch(4 * tile_cols, cin, dtype=BF16)] * 2
    beside, edge = call(
        functools.partial(columns_kernel, sizes),
        (shape((share + sent, 128)), shape((sent, 128))),
        rows_scratch + [scratch(halo, 128)],
        core_rows, far_rows, draft,
    )
    beside, edge = swap_even(beside, "col"), swap_odd(edge, "col")
    x, cot_all = call(
        functools.partial(spread_kernel, sizes),
        (shape((sizes.pixels, cin)), shape((sizes.out, width))),
        rows_scratch
        + [
            scratch(sent, 128, dtype=BF16),
            scratch(sent, 128, dtype=BF16),
            scratch(32, cin),
            scratch(cin // 128, tile_rows + 3, 8 + tile_cols, 128),
            scratch(3, cin // 128, 40, 128),
        ],
        region, cotangent, core_rows, far_rows, beside, edge,
    )
    passed = call(
        pass_kernel,
        shape(((halves - 1) * length + share, 128)),
        [],
        beside, edge, *far,
    )
    blocks = [weights, passed, swap_even(passed, "row")]
    active_three, grad_sum, short_t, reduce_t, grad_one, give, *keeps = call(
        functools.partial(main_kernel, sizes, halves, cin),
        (
            shape((sizes.main, width)),
            shape((sizes.main, width)),
            shape((width, cin)),
            shape((mid, cin)),
            shape((4 * sizes.main, mid)),
            shape((halves, length, 128)),
        )
        + (shape((length, 128), F32),) * halves,
        [
            scratch(sizes.pixels, mid, dtype=BF16),
            scratch(4 * sizes.main, mid),
            scratch(sizes.out, mid, dtype=BF16),
            scratch(sizes.out, mid),
            scratch(mid // HALF, HALF, TAPS * HALF, dtype=BF16),
            scratch(sizes.pixels, mid),
            scratch(mid, 256, dtype=BF16),
            scratch(256, mid, dtype=BF16),
            scratch(mid // HALF, TAPS * HALF, HALF, dtype=BF16),
            scratch(sizes.out, mid),
            scratch(length, 128, dtype=BF16),
            scratch(sizes.wide, mid, dtype=BF16),
            scratch(sizes.wide, mid, dtype=BF16),
            scratch(width, mid, dtype=BF16),
            scratch(sizes.hr + 1, 24, mid),
            scratch(mid, early + late),
        ],
        x, cot_all, *blocks,
        flops=2 * sizes.pixels * cin * mid + 10 * sizes.out * TAPS * HALF * mid,
    )
    block_out, region_grad = call(
        functools.partial(outputs_kernel, sizes),
        (shape((sizes.hr, sizes.hc, width)), shape(region.shape)),
        [
            scratch(4 * sizes.main, cin),
            scratch(cin // 128, tile_rows, tile_cols, 128),
        ],
        grad_one, reduce_t, grad_sum, short_t, active_three,
        flops=2 * 4 * sizes.main * cin * mid,
    )
    total, across = reduce(keeps, give)
    grads = call(
        finish_kernel,
        tuple(shape((shard, lanes), F32) for lanes in (cin, taps, mid, cin)),
        [],
        total, across,
    )
    return (block_out, region_grad, *(grad.T for grad in grads))


def solution(mesh):
    tiles, split = P("row", "col", None), P(None, "col")
    return jax.shard_map(
        per_device,
        mesh=mesh,
        in_specs=(tiles, split, split, split, split, tiles),
        out_specs=(tiles, tiles, split, split, split, split),
        check_vma=False,
    )
```

```python
import functools

import jax
import jax.numpy as jnp
from jax import lax
from jax.experimental import pallas as pl
from jax.experimental.pallas import tpu as pltpu
from jax.sharding import PartitionSpec as P

GW = 16
TAPS = 9
HALF = 256
BACK = (4, 5, 3, 7, 1, 8, 2, 6, 0)
F32 = jnp.float32
BF16 = jnp.bfloat16
VMEM_LIMIT = 40 * 1024 * 1024


class Sizes:
    def __init__(self, tile_rows, tile_cols):
        self.tr, self.tc = tile_rows, tile_cols
        self.hr, self.hc = tile_rows // 2, tile_cols // 2
        self.odd = (self.hr + 2) * self.hc
        self.even = (self.hr + 1) * self.hc
        self.band = self.odd + self.even
        self.side = 3 * self.band
        self.pixels = self.side + TAPS * 16
        self.main = self.hr * self.hc
        self.wide = self.main + self.hc
        self.out = self.wide + 16

    def tap(self, tap):
        a, b = divmod(tap, 3)
        return b * self.band + (0, self.odd, self.hc)[a]

    def tap_side(self, tap):
        return self.side + tap * 16

    def planes(self):
        return (
            self.band + self.odd,
            2 * self.band + self.odd,
            self.band + self.hc,
            2 * self.band + self.hc,
        )


def dot(a, b, dims=((1,), (0,))):
    return lax.dot_general(a, b, (dims, ((), ())), preferred_element_type=F32)


def sigmoid(value):
    below = 1.0 + jnp.exp(jnp.minimum(-value, 80.0))
    guess = pl.reciprocal(below, approx=True)
    return guess * (2.0 - below * guess)


def place():
    col = lax.axis_index("col")
    return col // 2, lax.rem(col, 2), lax.rem(lax.axis_index("row"), 2)


def fold(block):
    parts = [
        pltpu.roll(block[at : at + GW], at, 1) if at else block[:GW]
        for at in range(0, block.shape[0], GW)
    ]
    return sum(parts[1:], parts[0])


def unfold(tail, rows):
    return [pltpu.roll(tail, (128 - at) % 128, 1) if at else tail for at in range(0, rows, GW)]


def pieces(halves, shard, own, passed, swapped, beside):
    h, low, core = place()
    length = own.shape[0]
    flips = (low + core - 2 * low * core, 1 - low - core + 2 * low * core)
    found = [(own, (2 * h + low) * shard)]
    for ref, flip in zip((passed, swapped), flips, strict=True):
        for j in range(1, halves):
            spot = 2 * lax.rem(h - j + halves, halves) + flip
            found.append((ref.at[(j - 1) * length : j * length], spot * shard))
    first = (halves - 1) * length
    share = passed.shape[0] - first
    for ref, part in ((passed, core), (swapped, 1 - core)):
        rows = pl.ds(pl.multiple_of(part * (length - share), 16), share)
        beside[rows, :] = ref[first : first + share]
    return found + [(beside, (2 * h + 1 - low) * shard)]


def send_kernel(sizes, *refs):
    given, (weights, outer, draft, cols) = refs[:6], refs[6:10]
    local, arrived = refs[10:16], refs[16]
    copies = [
        pltpu.make_async_copy(given[i], local[i], arrived.at[i]) for i in range(len(given))
    ]
    for copy in copies:
        copy.start()
    for copy in copies:
        copy.wait()
    region, cot, reduce_t, group_t, expand_t, short_t = local
    shard, taps = group_t.shape
    cin, mid = reduce_t.shape[1], expand_t.shape[1]
    tiles = [reduce_t[:, at : at + 128] for at in range(0, cin, 128)]
    tiles.append(group_t[:, :128])
    tiles += [expand_t[:, at : at + 128] for at in range(0, mid, 128)]
    tiles += [short_t[:, at : at + 128] for at in range(0, cin, 128)]
    for i, tile in enumerate(tiles):
        weights[i * shard : (i + 1) * shard] = tile
    pad = jnp.zeros((shard, 256 - taps), BF16)
    rest = jnp.concatenate([group_t[...], pad], axis=1)[:, 128:].astype(F32)
    weights[len(tiles) * shard :] = fold(rest).astype(BF16)
    tc, half = sizes.tc, cot.shape[2] // 2
    for i, r in enumerate((sizes.tr - 1, 0, 1)):
        outer[i * tc : (i + 1) * tc] = region[r]
    outer[3 * tc : 3 * tc + sizes.hc] = cot[0, :, :half]
    outer[3 * tc + sizes.hc :] = cot[0, :, half:]
    cols[...] = jnp.zeros_like(cols)
    for r in range(sizes.tr):
        put_columns(cols, r + 1, region[r, :16], region[r, tc - 16 :])
    for i in range(sizes.hr):
        put_cotangent(cols, i, cot[i, :16])
    share = draft.shape[0] - cols.shape[0]
    core = lax.rem(lax.axis_index("row"), 2)
    first = pl.multiple_of(core * (weights.shape[0] - share), 16)
    draft[:share] = weights[pl.ds(first, share), :]
    draft[share:] = cols[...].astype(BF16)


def put_columns(cols, row, head, tail):
    head, tail = head.astype(F32), tail.astype(F32)
    tiles = head.shape[1] // 128
    for i, pixel in enumerate((tail[15:16], head[0:1], head[1:2])):
        for v in range(tiles):
            at = (i * tiles + v) * 32 + row
            cols[at : at + 1] = pixel[:, v * 128 : (v + 1) * 128]


def put_cotangent(cols, row, head):
    pixel = head.astype(F32)[0:1]
    tiles = pixel.shape[1] // 128
    for v in range(tiles):
        at = cols.shape[0] - (tiles - v) * 16 + row
        cols[at : at + 1] = pixel[:, v * 128 : (v + 1) * 128]


def choose(first, one, other, to_one, to_other):
    @pl.when(first)
    def _():
        to_one[...] = one[...]
        to_other[...] = other[...]

    @pl.when(jnp.logical_not(first))
    def _():
        to_one[...] = other[...]
        to_other[...] = one[...]


def columns_kernel(sizes, core_rows, far_rows, draft, beside, edge, north, south, cols):
    choose(lax.rem(lax.axis_index("row"), 2) == 0, core_rows, far_rows, south, north)
    tc, tr, hc = sizes.tc, sizes.tr, sizes.hc
    share = draft.shape[0] - cols.shape[0]
    beside[:share] = draft[:share]
    cols[...] = draft[share:].astype(F32)
    for to, rows, at in ((0, north, 0), (tr + 1, south, tc), (tr + 2, south, 2 * tc)):
        put_columns(cols, to, rows[at : at + 16], rows[at + tc - 16 : at + tc])
    ends = [south[at : at + 16] for at in (3 * tc, 3 * tc + hc)]
    put_cotangent(cols, sizes.hr, jnp.concatenate(ends, axis=1))
    low = lax.rem(lax.axis_index("col"), 2)
    skip = cols.shape[0] - edge.shape[0]
    for out, first in ((beside.at[share:], skip * low), (edge, skip * (1 - low))):
        first = pl.multiple_of(first, 16)
        out[...] = cols[pl.ds(first, out.shape[0]), :].astype(BF16)


def pass_kernel(beside, edge, *refs):
    far, passed = refs[:-1], refs[-1]
    length, share = far[0].shape[0], beside.shape[0] - edge.shape[0]
    for j, block in enumerate(far):
        passed[j * length : (j + 1) * length] = block[...]
    passed[len(far) * length :] = beside[:share]


def spread_kernel(sizes, region, cot, core_rows, far_rows, beside, edge, *refs):
    x, cot_all, north, south, west, east, left, ext, cols = refs
    choose(lax.rem(lax.axis_index("row"), 2) == 0, core_rows, far_rows, south, north)
    choose(lax.rem(lax.axis_index("col"), 2) == 0, beside.at[beside.shape[0] - edge.shape[0] :], edge, east, west)
    cin, tc, tr, hc = region.shape[2], sizes.tc, sizes.tr, sizes.hc
    tiles = cin // 128
    for v in range(tiles):
        left[:, v * 128 : (v + 1) * 128] = west[v * 32 : (v + 1) * 32].astype(F32)
    cols[...] = jnp.zeros_like(cols)
    for v in range(cin // 128):
        lanes = slice(v * 128, (v + 1) * 128)
        for r in range(tr + 3):
            if r == 0:
                row = north[:tc, lanes]
            elif r <= tr:
                row = region[r - 1, :, lanes]
            else:
                row = south[(r - tr) * tc : (1 + r - tr) * tc, lanes]
            ext[v, r, 8 : 8 + tc] = row.astype(F32)
            ext[v, r, 7:8] = left[r : r + 1, lanes]
            cols[0, v, r : r + 1] = ext[v, r, 7 + tc : 8 + tc]
        for b in (1, 2):
            at = ((b - 1) * tiles + v) * 32
            cols[b, v, :32] = east[at : at + 32].astype(F32)
        for b in range(3):
            base = b * sizes.band
            for r in list(range(0, tr + 3, 2)) + list(range(1, tr + 3, 2)):
                picked = ext[v, r, pl.ds(7 + b, hc, stride=2)]
                x[base : base + hc, lanes] = picked.astype(BF16)
                base += hc
            for a in range(3):
                at = sizes.tap_side(3 * a + b)
                x[at : at + 16, lanes] = cols[b, v, pl.ds(a, 16, stride=2)].astype(BF16)
    half = cot_all.shape[1] // 2
    cot_all[: sizes.main] = cot[...].reshape(sizes.main, 2 * half)
    cot_all[sizes.main : sizes.wide, :half] = south[3 * tc : 3 * tc + hc]
    cot_all[sizes.main : sizes.wide, half:] = south[3 * tc + hc :]
    for v in range(2 * half // 128):
        at = 2 * tiles * 32 + v * 16
        cot_all[sizes.wide :, v * 128 : (v + 1) * 128] = east[at : at + 16]


def forward_part(sizes, halves, x, *refs):
    hidden, slope_one, hidden_two, slope_two, back, reduce_t = refs[3:9]
    pre, group_t, group, front, pre_two, beside = refs[9:]
    cin = reduce_t.shape[1]
    mid = reduce_t.shape[0]
    shard = mid // (2 * halves)
    lane = lax.broadcasted_iota(jnp.int32, (GW, 128), 1)
    for block, first in pieces(halves, shard, *refs[:3], beside):
        rows = pl.ds(pl.multiple_of(first, 16), shard)
        for v in range(cin // 128):
            reduce_t[rows, v * 128 : (v + 1) * 128] = block[v * shard : (v + 1) * shard]
        at = cin // 128 * shard
        group_t[rows, :128] = block[at : at + shard]
        tail = block[block.shape[0] - GW :].astype(F32)
        for i, part in enumerate(unfold(tail, shard)):
            rows = pl.ds(pl.multiple_of(first + i * GW, 16), GW)
            group_t[rows, 128:] = jnp.where(lane < GW, part, 0.0).astype(BF16)
    pre[...] = dot(x[...], reduce_t[...], ((1,), (1,)))
    group[...] = group_t[...].astype(F32).T.astype(BF16)
    row_group = lax.broadcasted_iota(jnp.int32, (HALF, HALF), 0) // GW
    lane_group = lax.broadcasted_iota(jnp.int32, (HALF, HALF), 1) // GW
    mask = jnp.where(row_group == lane_group, 1.0, 0.0).astype(BF16)
    for n in range(mid // HALF):
        for tap in range(TAPS):
            rows = group[tap * GW : (tap + 1) * GW, n * HALF : (n + 1) * HALF]
            dense = jnp.concatenate([rows] * (HALF // GW), axis=0) * mask
            front[n, tap * HALF : (tap + 1) * HALF] = dense
            spot = BACK.index(tap)
            back[n, :, spot * HALF : (spot + 1) * HALF] = dense

    planes = sizes.planes()
    first = 0
    for start in sorted(planes) + [sizes.pixels]:
        for at in range(first, start, 32):
            rows = slice(at, min(at + 32, start))
            value = pre[rows, :]
            hidden[rows, :] = (value * sigmoid(value)).astype(BF16)
        first = start + sizes.main
    for i, start in enumerate(planes):
        for at in range(0, sizes.main, 32):
            rows = slice(start + at, start + at + 32)
            value = pre[rows, :]
            sigma = sigmoid(value)
            active = value * sigma
            hidden[rows, :] = active.astype(BF16)
            rows = slice(i * sizes.main + at, i * sizes.main + at + 32)
            slope_one[rows, :] = sigma + active * (1.0 - sigma)
    for n in range(mid // HALF):
        lanes = slice(n * HALF, (n + 1) * HALF)
        patches = []
        for tap in range(TAPS):
            at, side = sizes.tap(tap), sizes.tap_side(tap)
            patches.append(
                jnp.concatenate(
                    [hidden[at : at + sizes.wide, lanes], hidden[side : side + 16, lanes]], axis=0
                )
            )
        pre_two[:, lanes] = dot(jnp.concatenate(patches, axis=1), front[n])
    value = pre_two[...]
    sigma = sigmoid(value)
    active = value * sigma
    hidden_two[...] = active.astype(BF16)
    slope_two[...] = sigma + active * (1.0 - sigma)


def split_out(halves, total, shard, rest, keeps, give):
    tiles = [at for at in range(0, total.shape[1], 128) if at != rest]
    h, low, core = place()
    keep = low + core - 2 * low * core
    for j in range(halves):
        base = 2 * lax.rem(h + j, halves)
        mine = pl.ds(pl.multiple_of((base + keep) * shard, shard), shard)
        theirs = pl.ds(pl.multiple_of((base + 1 - keep) * shard, shard), shard)
        for i, at in enumerate(tiles):
            slab = slice(i * shard, (i + 1) * shard)
            keeps[j][slab] = total[mine, at : at + 128]
            give[j, slab] = total[theirs, at : at + 128].astype(BF16)
        keeps[j][len(tiles) * shard :] = fold(total[mine, rest : rest + 128])
        give[j, len(tiles) * shard :] = fold(total[theirs, rest : rest + 128]).astype(BF16)


def middle_part(sizes, halves, x, hidden_two, slope_two, cot, *refs):
    active_three, grad_two, grad_side, own, short_t, total, expand_t, shift, beside = refs[3:]
    mid = expand_t.shape[1]
    width = expand_t.shape[0]
    shard = width // (2 * halves)
    cin = short_t.shape[1]
    for block, first in pieces(halves, shard, *refs[:3], beside):
        rows = pl.ds(pl.multiple_of(first, 16), shard)
        at = (cin // 128 + 1) * shard
        for ref in (expand_t, short_t):
            for v in range(ref.shape[1] // 128):
                ref[rows, v * 128 : (v + 1) * 128] = block[at : at + shard]
                at += shard
    at, side = sizes.tap(4), sizes.tap_side(4)
    strided = jnp.concatenate([x[at : at + sizes.wide], x[side : side + 16]], axis=0)
    summed = dot(hidden_two[...], expand_t[...], ((1,), (1,))) + dot(
        strided, short_t[...], ((1,), (1,))
    )
    sigma = sigmoid(summed)
    active = summed * sigma
    active_three[...] = active[: sizes.main].astype(BF16)
    grad_sum = (cot[...].astype(F32) * (sigma + active * (1.0 - sigma))).astype(BF16)
    own[...] = grad_sum[: sizes.main]
    flipped = grad_sum[: sizes.main].astype(F32).T.astype(BF16)
    total[:, :mid] = dot(flipped, hidden_two[: sizes.main])
    total[:, mid:] = dot(flipped, strided[: sizes.main])
    back = dot(grad_sum, expand_t[...]) * slope_two[...]
    grad_two[...] = back[: sizes.wide].astype(BF16)
    for i in range(sizes.hr + 1):
        shift[i, : sizes.hc] = back[i * sizes.hc : (i + 1) * sizes.hc]
        shift[i, sizes.hc : sizes.hc + 1] = back[sizes.wide + i : sizes.wide + i + 1]
    for i in range(sizes.hr + 1):
        grad_side[i * sizes.hc : (i + 1) * sizes.hc] = shift[i, 1 : sizes.hc + 1].astype(BF16)


def backward_part(
    sizes, halves, cin, x, hidden, slope_one, back, grad_two, grad_side, *refs
):
    grad_one, give = refs[:2]
    keeps = refs[2 : 2 + halves]
    total = refs[2 + halves]
    mid = hidden.shape[1]
    main, hc = sizes.main, sizes.hc
    shard = mid // (2 * halves)
    down = slice(hc, hc + main)
    own = slice(0, main)
    for n in range(mid // HALF):
        lanes = slice(n * HALF, (n + 1) * HALF)
        two, low = grad_two[own, lanes], grad_two[down, lanes]
        side, corner = grad_side[own, lanes], grad_side[down, lanes]
        first = 0
        for i, parts in enumerate(((two,), (two, side), (two, low), (two, low, side, corner))):
            left = jnp.concatenate(parts, axis=1)
            last = first + len(parts) * HALF
            spread = dot(left, back[n, :, first:last], ((1,), (1,)))
            first = last
            rows = slice(i * main, (i + 1) * main)
            grad_one[rows, lanes] = (spread * slope_one[rows, lanes]).astype(BF16)
    flat = jnp.concatenate([x[at : at + main] for at in sizes.planes()], axis=0)
    total[:, :cin] = dot(grad_one[...].astype(F32).T.astype(BF16), flat)
    flipped = grad_two[own, :].astype(F32).T.astype(BF16)
    lane = lax.broadcasted_iota(jnp.int32, (GW, 128), 1) // GW
    for n in range(mid // HALF):
        lanes = slice(n * HALF, (n + 1) * HALF)
        sums = [jnp.zeros((GW, 128), F32)] * (HALF // GW)
        for tap in range(TAPS):
            at = sizes.tap(tap)
            piece = dot(flipped[n * HALF : (n + 1) * HALF], hidden[at : at + main, lanes])
            for q in range(HALF // GW):
                tile = q // 8
                block = piece[q * GW : (q + 1) * GW, tile * 128 : (tile + 1) * 128]
                block = pltpu.roll(block, (GW * (tap - q)) % 128, 1)
                if tap < 8:
                    sums[q] = jnp.where(lane == tap, block, sums[q])
                else:
                    rows = slice(n * HALF + q * GW, n * HALF + (q + 1) * GW)
                    total[rows, cin : cin + 128] = sums[q]
                    total[rows, cin + 128 : cin + 256] = jnp.where(lane == 0, block, 0.0)
    split_out(halves, total, shard, cin + 128, keeps, give)


def main_kernel(sizes, halves, cin, x, cot, own, passed, swapped, *refs):
    active_three, grad_sum, short_t, reduce_t, grad_one, give = refs[:6]
    keeps, refs = refs[6 : 6 + halves], refs[6 + halves :]
    hidden, slope_one, hidden_two, slope_two, back, pre, group_t, group, front = refs[:9]
    pre_two, beside, grad_two, grad_side, expand_t, shift, total = refs[9:]
    weights = (own, passed, swapped)
    forward_part(
        sizes, halves, x, *weights, hidden, slope_one, hidden_two, slope_two, back, reduce_t,
        pre, group_t, group, front, pre_two, beside,
    )
    middle_part(
        sizes, halves, x, hidden_two, slope_two, cot, *weights, active_three, grad_two, grad_side,
        grad_sum, short_t, total.at[:, cin + 256 :], expand_t, shift, beside,
    )
    backward_part(
        sizes, halves, cin, x, hidden, slope_one, back, grad_two, grad_side, grad_one, give,
        *keeps, total,
    )


def outputs_kernel(sizes, grad_one, reduce_t, grad_sum, short_t, active, block_out, region_grad, planes, spread_out):
    main, hc, cin = sizes.main, sizes.hc, reduce_t.shape[1]
    block_out[...] = active[...].reshape(block_out.shape)
    planes[...] = dot(grad_one[...], reduce_t[...])
    planes[:main] += dot(grad_sum[...], short_t[...])
    for i in range(4):
        for r in range(sizes.hr):
            at = i * main + r * hc
            for v in range(cin // 128):
                lanes = slice(v * 128, (v + 1) * 128)
                spread_out[v, 2 * r + i // 2, pl.ds(i % 2, hc, stride=2)] = planes[at : at + hc, lanes]
    for v in range(cin // 128):
        region_grad[:, :, v * 128 : (v + 1) * 128] = spread_out[v].astype(BF16)


def call(kernel, out_shape, scratch, *operands, flops=0, space=pltpu.VMEM, limit=VMEM_LIMIT):
    sizes = sum(o.size * o.dtype.itemsize for o in operands)
    sizes += sum(o.size * o.dtype.itemsize for o in jax.tree.leaves(out_shape))
    return pl.pallas_call(
        kernel,
        out_shape=out_shape,
        in_specs=[pl.BlockSpec(memory_space=space)] * len(operands),
        out_specs=jax.tree.map(lambda _: pl.BlockSpec(memory_space=pltpu.VMEM), out_shape),
        scratch_shapes=scratch,
        compiler_params=pltpu.CompilerParams(vmem_limit_bytes=limit),
        cost_estimate=pl.CostEstimate(flops=flops, bytes_accessed=sizes, transcendentals=0),
    )(*operands)


def chip_kernel(one, other, whole, part):
    whole[...] = (one[...].astype(F32) + other[...].astype(F32)).astype(BF16)
    core = lax.rem(lax.axis_index("row"), 2)
    first = pl.multiple_of(core * (whole.shape[0] - part.shape[0]), 16)
    part[...] = whole[pl.ds(first, part.shape[0]), :]


def finish_kernel(whole, mine, theirs, *refs):
    outs, across = refs[:-1], refs[-1]
    core = lax.rem(lax.axis_index("row"), 2)
    for ref, at in ((mine, core), (theirs, 1 - core)):
        first = pl.multiple_of(at * (whole.shape[0] - ref.shape[0]), 16)
        across[pl.ds(first, ref.shape[0]), :] = ref[...]
    value = whole[...].astype(F32) + across[...].astype(F32)
    shard = outs[0].shape[0]
    at = 0
    for out in outs:
        for v in range(out.shape[1] // 128):
            out[:, v * 128 : (v + 1) * 128] = value[at : at + shard]
            at += shard
    rest = outs[1].shape[1] - 128
    for i, part in enumerate(unfold(value[at:], shard)):
        outs[1][i * GW : (i + 1) * GW, 128:] = part[:, :rest]


def both(rows, cols, target):
    pairs = []
    for r in range(rows):
        for c in range(cols):
            to = target(r % 2, c // 2, c % 2)
            if to is not None:
                pairs.append((r * cols + c, r * cols + 2 * to[0] + to[1]))
    return pairs


def swap_odd(x, axis):
    pairs = []
    for i in range(1, lax.axis_size(axis) - 1, 2):
        pairs += [(i, i + 1), (i + 1, i)]
    return lax.ppermute(x, axis, pairs)


def swap_even(x, axis):
    return lax.ppermute(x, axis, [(i, i ^ 1) for i in range(lax.axis_size(axis))])


def cross(x, j):
    rows, cols = lax.axis_size("row"), lax.axis_size("col")
    halves = cols // 2

    def target(k, h, low):
        return None if j == k == 0 else ((h + j) % halves, low ^ k)

    return lax.ppermute(x, ("row", "col"), both(rows, cols, target))


def reduce(keeps, give, share):
    rows, halves = lax.axis_size("row"), lax.axis_size("col") // 2
    core = lax.axis_index("row") % 2
    other = swap_even(give, "row")
    sums = [keeps[j] + other[j].astype(F32) for j in range(halves)]
    total = None
    for j in sorted(range(halves), key=lambda j: (j > 0, -min(j, halves - j), -j)):
        came = cross(sums[j].astype(BF16), j).astype(F32)
        if j == 0:
            came = jnp.where(core == 0, sums[0], came)
        total = came if total is None else total + came
    part = jax.ShapeDtypeStruct((share, 128), BF16)
    if rows != 4:
        nothing = jnp.zeros(part.shape, part.dtype)
        return lax.psum(total, "row"), nothing, nothing
    total = total.astype(BF16)
    whole, part = call(
        chip_kernel,
        (jax.ShapeDtypeStruct(total.shape, BF16), part),
        [],
        total, swap_even(total, "row"),
    )
    across = lax.ppermute(part, "row", [(r, r ^ 2) for r in range(4)])
    return whole, across, swap_even(across, "row")


def per_device(region, reduce_weight, group_weight, expand_weight, shortcut_weight, cotangent):
    tile_rows, tile_cols, cin = region.shape
    sizes = Sizes(tile_rows, tile_cols)
    halves = lax.axis_size("col") // 2
    mid, shard = expand_weight.shape
    width = shard * lax.axis_size("col")
    taps = group_weight.shape[0]
    early, late = cin + 256, mid + cin
    length = (early + late) // 128 * shard - shard + GW
    share = (length + 31) // 32 * 16
    halo = 3 * cin // 128 * 32 + width // 128 * 16
    sent = halo - cin // 128 * 32

    def shape(dims, dtype=BF16):
        return jax.ShapeDtypeStruct(dims, dtype)

    def scratch(*dims, dtype=F32):
        return pltpu.VMEM(dims, dtype)

    inputs = (
        region, cotangent, reduce_weight.T, group_weight.T, expand_weight.T, shortcut_weight.T,
    )
    weights, outer, draft = call(
        functools.partial(send_kernel, sizes),
        (
            shape((length, 128)),
            shape((4 * tile_cols, cin)),
            shape((share + halo, 128)),
        ),
        [scratch(halo, 128)]
        + [scratch(*given.shape, dtype=BF16) for given in inputs]
        + [pltpu.SemaphoreType.DMA((len(inputs),))],
        *inputs,
        space=pltpu.HBM,
        limit=62 * 1024 * 1024,
    )
    far = [cross(weights, j) for j in range(1, halves)]
    core_rows = swap_even(outer, "row")
    far_rows = swap_odd(outer, "row")
    rows_scratch = [scratch(4 * tile_cols, cin, dtype=BF16)] * 2
    beside, edge = call(
        functools.partial(columns_kernel, sizes),
        (shape((share + sent, 128)), shape((sent, 128))),
        rows_scratch + [scratch(halo, 128)],
        core_rows, far_rows, draft,
    )
    beside, edge = swap_even(beside, "col"), swap_odd(edge, "col")
    x, cot_all = call(
        functools.partial(spread_kernel, sizes),
        (shape((sizes.pixels, cin)), shape((sizes.out, width))),
        rows_scratch
        + [
            scratch(sent, 128, dtype=BF16),
            scratch(sent, 128, dtype=BF16),
            scratch(32, cin),
            scratch(cin // 128, tile_rows + 3, 8 + tile_cols, 128),
            scratch(3, cin // 128, 40, 128),
        ],
        region, cotangent, core_rows, far_rows, beside, edge,
    )
    passed = call(
        pass_kernel,
        shape(((halves - 1) * length + share, 128)),
        [],
        beside, edge, *far,
    )
    blocks = [weights, passed, swap_even(passed, "row")]
    active_three, grad_sum, short_t, reduce_t, grad_one, give, *keeps = call(
        functools.partial(main_kernel, sizes, halves, cin),
        (
            shape((sizes.main, width)),
            shape((sizes.main, width)),
            shape((width, cin)),
            shape((mid, cin)),
            shape((4 * sizes.main, mid)),
            shape((halves, length, 128)),
        )
        + (shape((length, 128), F32),) * halves,
        [
            scratch(sizes.pixels, mid, dtype=BF16),
            scratch(4 * sizes.main, mid),
            scratch(sizes.out, mid, dtype=BF16),
            scratch(sizes.out, mid),
            scratch(mid // HALF, HALF, TAPS * HALF, dtype=BF16),
            scratch(sizes.pixels, mid),
            scratch(mid, 256, dtype=BF16),
            scratch(256, mid, dtype=BF16),
            scratch(mid // HALF, TAPS * HALF, HALF, dtype=BF16),
            scratch(sizes.out, mid),
            scratch(length, 128, dtype=BF16),
            scratch(sizes.wide, mid, dtype=BF16),
            scratch(sizes.wide, mid, dtype=BF16),
            scratch(width, mid, dtype=BF16),
            scratch(sizes.hr + 1, 24, mid),
            scratch(mid, early + late),
        ],
        x, cot_all, *blocks,
        flops=2 * sizes.pixels * cin * mid + 10 * sizes.out * TAPS * HALF * mid,
    )
    block_out, region_grad = call(
        functools.partial(outputs_kernel, sizes),
        (shape((sizes.hr, sizes.hc, width)), shape(region.shape)),
        [
            scratch(4 * sizes.main, cin),
            scratch(cin // 128, tile_rows, tile_cols, 128),
        ],
        grad_one, reduce_t, grad_sum, short_t, active_three,
        flops=2 * 4 * sizes.main * cin * mid,
    )
    sums = reduce(keeps, give, share)
    grads = call(
        finish_kernel,
        tuple(shape((shard, lanes), F32) for lanes in (cin, taps, mid, cin)),
        [scratch(length, 128, dtype=BF16)],
        *sums,
    )
    return (block_out, region_grad, *(grad.T for grad in grads))


def solution(mesh):
    tiles, split = P("row", "col", None), P(None, "col")
    return jax.shard_map(
        per_device,
        mesh=mesh,
        in_specs=(tiles, split, split, split, split, tiles),
        out_specs=(tiles, tiles, split, split, split, split),
        check_vma=False,
    )
```

```python
import functools

import jax
import jax.numpy as jnp
from jax import lax
from jax.experimental import pallas as pl
from jax.experimental.pallas import tpu as pltpu
from jax.sharding import PartitionSpec as P

GW = 16
TAPS = 9
HALF = 256
BACK = (4, 5, 3, 7, 1, 8, 2, 6, 0)
F32 = jnp.float32
BF16 = jnp.bfloat16
VMEM_LIMIT = 40 * 1024 * 1024


class Sizes:
    def __init__(self, tile_rows, tile_cols):
        self.tr, self.tc = tile_rows, tile_cols
        self.hr, self.hc = tile_rows // 2, tile_cols // 2
        self.odd = (self.hr + 2) * self.hc
        self.even = (self.hr + 1) * self.hc
        self.band = self.odd + self.even
        self.side = 3 * self.band
        self.pixels = self.side + TAPS * 16
        self.main = self.hr * self.hc
        self.wide = self.main + self.hc
        self.out = self.wide + 16

    def tap(self, tap):
        a, b = divmod(tap, 3)
        return b * self.band + (0, self.odd, self.hc)[a]

    def tap_side(self, tap):
        return self.side + tap * 16

    def planes(self):
        return (
            self.band + self.odd,
            2 * self.band + self.odd,
            self.band + self.hc,
            2 * self.band + self.hc,
        )


def dot(a, b, dims=((1,), (0,))):
    return lax.dot_general(a, b, (dims, ((), ())), preferred_element_type=F32)


def sigmoid(value):
    below = 1.0 + jnp.exp(jnp.minimum(-value, 80.0))
    guess = pl.reciprocal(below, approx=True)
    return guess * (2.0 - below * guess)


def place():
    col = lax.axis_index("col")
    return col // 2, lax.rem(col, 2), lax.rem(lax.axis_index("row"), 2)


def fold(block):
    parts = [
        pltpu.roll(block[at : at + GW], at, 1) if at else block[:GW]
        for at in range(0, block.shape[0], GW)
    ]
    return sum(parts[1:], parts[0])


def unfold(tail, rows):
    return [pltpu.roll(tail, (128 - at) % 128, 1) if at else tail for at in range(0, rows, GW)]


def pieces(halves, shard, own, passed, swapped, beside):
    h, low, core = place()
    length = own.shape[0]
    flips = (low + core - 2 * low * core, 1 - low - core + 2 * low * core)
    found = [(own, (2 * h + low) * shard)]
    for ref, flip in zip((passed, swapped), flips, strict=True):
        for j in range(1, halves):
            spot = 2 * lax.rem(h - j + halves, halves) + flip
            found.append((ref.at[(j - 1) * length : j * length], spot * shard))
    first = (halves - 1) * length
    share = passed.shape[0] - first
    for ref, part in ((passed, core), (swapped, 1 - core)):
        rows = pl.ds(pl.multiple_of(part * (length - share), 16), share)
        beside[rows, :] = ref[first : first + share]
    return found + [(beside, (2 * h + 1 - low) * shard)]


def send_kernel(sizes, *refs):
    given, (weights, outer, draft, cols) = refs[:6], refs[6:10]
    local, arrived = refs[10:16], refs[16]
    copies = [
        pltpu.make_async_copy(given[i], local[i], arrived.at[i]) for i in range(len(given))
    ]
    for copy in copies:
        copy.start()
    for copy in copies:
        copy.wait()
    region, cot, reduce_t, group_t, expand_t, short_t = local
    shard, taps = group_t.shape
    cin, mid = reduce_t.shape[1], expand_t.shape[1]
    tiles = [reduce_t[:, at : at + 128] for at in range(0, cin, 128)]
    tiles.append(group_t[:, :128])
    tiles += [expand_t[:, at : at + 128] for at in range(0, mid, 128)]
    tiles += [short_t[:, at : at + 128] for at in range(0, cin, 128)]
    for i, tile in enumerate(tiles):
        weights[i * shard : (i + 1) * shard] = tile
    pad = jnp.zeros((shard, 256 - taps), BF16)
    rest = jnp.concatenate([group_t[...], pad], axis=1)[:, 128:].astype(F32)
    weights[len(tiles) * shard :] = fold(rest).astype(BF16)
    tc, half = sizes.tc, cot.shape[2] // 2
    for i, r in enumerate((sizes.tr - 1, 0, 1)):
        outer[i * tc : (i + 1) * tc] = region[r]
    outer[3 * tc : 3 * tc + sizes.hc] = cot[0, :, :half]
    outer[3 * tc + sizes.hc :] = cot[0, :, half:]
    cols[...] = jnp.zeros_like(cols)
    for r in range(sizes.tr):
        put_columns(cols, r + 1, region[r, :16], region[r, tc - 16 :])
    for i in range(sizes.hr):
        put_cotangent(cols, i, cot[i, :16])
    share = draft.shape[0] - cols.shape[0]
    core = lax.rem(lax.axis_index("row"), 2)
    first = pl.multiple_of(core * (weights.shape[0] - share), 16)
    draft[:share] = weights[pl.ds(first, share), :]
    draft[share:] = cols[...].astype(BF16)


def put_columns(cols, row, head, tail):
    head, tail = head.astype(F32), tail.astype(F32)
    tiles = head.shape[1] // 128
    for i, pixel in enumerate((tail[15:16], head[0:1], head[1:2])):
        for v in range(tiles):
            at = (i * tiles + v) * 32 + row
            cols[at : at + 1] = pixel[:, v * 128 : (v + 1) * 128]


def put_cotangent(cols, row, head):
    pixel = head.astype(F32)[0:1]
    tiles = pixel.shape[1] // 128
    for v in range(tiles):
        at = cols.shape[0] - (tiles - v) * 16 + row
        cols[at : at + 1] = pixel[:, v * 128 : (v + 1) * 128]


def choose(first, one, other, to_one, to_other):
    @pl.when(first)
    def _():
        to_one[...] = one[...]
        to_other[...] = other[...]

    @pl.when(jnp.logical_not(first))
    def _():
        to_one[...] = other[...]
        to_other[...] = one[...]


def columns_kernel(sizes, core_rows, far_rows, draft, beside, edge, north, south, cols):
    choose(lax.rem(lax.axis_index("row"), 2) == 0, core_rows, far_rows, south, north)
    tc, tr, hc = sizes.tc, sizes.tr, sizes.hc
    share = draft.shape[0] - cols.shape[0]
    beside[:share] = draft[:share]
    cols[...] = draft[share:].astype(F32)
    for to, rows, at in ((0, north, 0), (tr + 1, south, tc), (tr + 2, south, 2 * tc)):
        put_columns(cols, to, rows[at : at + 16], rows[at + tc - 16 : at + tc])
    ends = [south[at : at + 16] for at in (3 * tc, 3 * tc + hc)]
    put_cotangent(cols, sizes.hr, jnp.concatenate(ends, axis=1))
    low = lax.rem(lax.axis_index("col"), 2)
    skip = cols.shape[0] - edge.shape[0]
    for out, first in ((beside.at[share:], skip * low), (edge, skip * (1 - low))):
        first = pl.multiple_of(first, 16)
        out[...] = cols[pl.ds(first, out.shape[0]), :].astype(BF16)


def pass_kernel(beside, edge, *refs):
    far, passed = refs[:-1], refs[-1]
    length, share = far[0].shape[0], beside.shape[0] - edge.shape[0]
    for j, block in enumerate(far):
        passed[j * length : (j + 1) * length] = block[...]
    passed[len(far) * length :] = beside[:share]


def spread_kernel(sizes, region, cot, core_rows, far_rows, beside, edge, *refs):
    x, cot_all, north, south, west, east, left, ext, cols = refs
    choose(lax.rem(lax.axis_index("row"), 2) == 0, core_rows, far_rows, south, north)
    choose(lax.rem(lax.axis_index("col"), 2) == 0, beside.at[beside.shape[0] - edge.shape[0] :], edge, east, west)
    cin, tc, tr, hc = region.shape[2], sizes.tc, sizes.tr, sizes.hc
    tiles = cin // 128
    for v in range(tiles):
        left[:, v * 128 : (v + 1) * 128] = west[v * 32 : (v + 1) * 32].astype(F32)
    cols[...] = jnp.zeros_like(cols)
    for v in range(cin // 128):
        lanes = slice(v * 128, (v + 1) * 128)
        for r in range(tr + 3):
            if r == 0:
                row = north[:tc, lanes]
            elif r <= tr:
                row = region[r - 1, :, lanes]
            else:
                row = south[(r - tr) * tc : (1 + r - tr) * tc, lanes]
            ext[v, r, 8 : 8 + tc] = row.astype(F32)
            ext[v, r, 7:8] = left[r : r + 1, lanes]
            cols[0, v, r : r + 1] = ext[v, r, 7 + tc : 8 + tc]
        for b in (1, 2):
            at = ((b - 1) * tiles + v) * 32
            cols[b, v, :32] = east[at : at + 32].astype(F32)
        for b in range(3):
            base = b * sizes.band
            for r in list(range(0, tr + 3, 2)) + list(range(1, tr + 3, 2)):
                picked = ext[v, r, pl.ds(7 + b, hc, stride=2)]
                x[base : base + hc, lanes] = picked.astype(BF16)
                base += hc
            for a in range(3):
                at = sizes.tap_side(3 * a + b)
                x[at : at + 16, lanes] = cols[b, v, pl.ds(a, 16, stride=2)].astype(BF16)
    half = cot_all.shape[1] // 2
    cot_all[: sizes.main] = cot[...].reshape(sizes.main, 2 * half)
    cot_all[sizes.main : sizes.wide, :half] = south[3 * tc : 3 * tc + hc]
    cot_all[sizes.main : sizes.wide, half:] = south[3 * tc + hc :]
    for v in range(2 * half // 128):
        at = 2 * tiles * 32 + v * 16
        cot_all[sizes.wide :, v * 128 : (v + 1) * 128] = east[at : at + 16]


def forward_part(sizes, halves, x, *refs):
    hidden, slope_one, hidden_two, slope_two, back, reduce_t = refs[3:9]
    pre, group_t, group, front, pre_two, beside = refs[9:]
    cin = reduce_t.shape[1]
    mid = reduce_t.shape[0]
    shard = mid // (2 * halves)
    lane = lax.broadcasted_iota(jnp.int32, (GW, 128), 1)
    for block, first in pieces(halves, shard, *refs[:3], beside):
        rows = pl.ds(pl.multiple_of(first, 16), shard)
        for v in range(cin // 128):
            reduce_t[rows, v * 128 : (v + 1) * 128] = block[v * shard : (v + 1) * shard]
        at = cin // 128 * shard
        group_t[rows, :128] = block[at : at + shard]
        tail = block[block.shape[0] - GW :].astype(F32)
        for i, part in enumerate(unfold(tail, shard)):
            rows = pl.ds(pl.multiple_of(first + i * GW, 16), GW)
            group_t[rows, 128:] = jnp.where(lane < GW, part, 0.0).astype(BF16)
    pre[...] = dot(x[...], reduce_t[...], ((1,), (1,)))
    group[...] = group_t[...].astype(F32).T.astype(BF16)
    row_group = lax.broadcasted_iota(jnp.int32, (HALF, HALF), 0) // GW
    lane_group = lax.broadcasted_iota(jnp.int32, (HALF, HALF), 1) // GW
    mask = jnp.where(row_group == lane_group, 1.0, 0.0).astype(BF16)
    for n in range(mid // HALF):
        for tap in range(TAPS):
            rows = group[tap * GW : (tap + 1) * GW, n * HALF : (n + 1) * HALF]
            dense = jnp.concatenate([rows] * (HALF // GW), axis=0) * mask
            front[n, tap * HALF : (tap + 1) * HALF] = dense
            spot = BACK.index(tap)
            back[n, :, spot * HALF : (spot + 1) * HALF] = dense

    planes = sizes.planes()
    first = 0
    for start in sorted(planes) + [sizes.pixels]:
        for at in range(first, start, 32):
            rows = slice(at, min(at + 32, start))
            value = pre[rows, :]
            hidden[rows, :] = (value * sigmoid(value)).astype(BF16)
        first = start + sizes.main
    for i, start in enumerate(planes):
        for at in range(0, sizes.main, 32):
            rows = slice(start + at, start + at + 32)
            value = pre[rows, :]
            sigma = sigmoid(value)
            active = value * sigma
            hidden[rows, :] = active.astype(BF16)
            rows = slice(i * sizes.main + at, i * sizes.main + at + 32)
            slope_one[rows, :] = sigma + active * (1.0 - sigma)
    for n in range(mid // HALF):
        lanes = slice(n * HALF, (n + 1) * HALF)
        patches = []
        for tap in range(TAPS):
            at, side = sizes.tap(tap), sizes.tap_side(tap)
            patches.append(
                jnp.concatenate(
                    [hidden[at : at + sizes.wide, lanes], hidden[side : side + 16, lanes]], axis=0
                )
            )
        pre_two[:, lanes] = dot(jnp.concatenate(patches, axis=1), front[n])
    value = pre_two[...]
    sigma = sigmoid(value)
    active = value * sigma
    hidden_two[...] = active.astype(BF16)
    slope_two[...] = sigma + active * (1.0 - sigma)


def split_out(halves, total, shard, rest, keeps, give):
    tiles = [at for at in range(0, total.shape[1], 128) if at != rest]
    h, low, core = place()
    keep = low + core - 2 * low * core
    for j in range(halves):
        base = 2 * lax.rem(h + j, halves)
        mine = pl.ds(pl.multiple_of((base + keep) * shard, shard), shard)
        theirs = pl.ds(pl.multiple_of((base + 1 - keep) * shard, shard), shard)
        for i, at in enumerate(tiles):
            slab = slice(i * shard, (i + 1) * shard)
            keeps[j][slab] = total[mine, at : at + 128]
            give[j, slab] = total[theirs, at : at + 128].astype(BF16)
        keeps[j][len(tiles) * shard :] = fold(total[mine, rest : rest + 128])
        give[j, len(tiles) * shard :] = fold(total[theirs, rest : rest + 128]).astype(BF16)


def middle_part(sizes, halves, x, hidden_two, slope_two, cot, *refs):
    active_three, grad_two, grad_side, own, short_t, total, expand_t, shift, beside = refs[3:]
    mid = expand_t.shape[1]
    width = expand_t.shape[0]
    shard = width // (2 * halves)
    cin = short_t.shape[1]
    for block, first in pieces(halves, shard, *refs[:3], beside):
        rows = pl.ds(pl.multiple_of(first, 16), shard)
        at = (cin // 128 + 1) * shard
        for ref in (expand_t, short_t):
            for v in range(ref.shape[1] // 128):
                ref[rows, v * 128 : (v + 1) * 128] = block[at : at + shard]
                at += shard
    at, side = sizes.tap(4), sizes.tap_side(4)
    strided = jnp.concatenate([x[at : at + sizes.wide], x[side : side + 16]], axis=0)
    summed = dot(hidden_two[...], expand_t[...], ((1,), (1,))) + dot(
        strided, short_t[...], ((1,), (1,))
    )
    sigma = sigmoid(summed)
    active = summed * sigma
    active_three[...] = active[: sizes.main].astype(BF16)
    grad_sum = (cot[...].astype(F32) * (sigma + active * (1.0 - sigma))).astype(BF16)
    own[...] = grad_sum[: sizes.main]
    flipped = grad_sum[: sizes.main].astype(F32).T.astype(BF16)
    total[:, :mid] = dot(flipped, hidden_two[: sizes.main])
    total[:, mid:] = dot(flipped, strided[: sizes.main])
    back = dot(grad_sum, expand_t[...]) * slope_two[...]
    grad_two[...] = back[: sizes.wide].astype(BF16)
    for i in range(sizes.hr + 1):
        shift[i, : sizes.hc] = back[i * sizes.hc : (i + 1) * sizes.hc]
        shift[i, sizes.hc : sizes.hc + 1] = back[sizes.wide + i : sizes.wide + i + 1]
    for i in range(sizes.hr + 1):
        grad_side[i * sizes.hc : (i + 1) * sizes.hc] = shift[i, 1 : sizes.hc + 1].astype(BF16)


def backward_part(
    sizes, halves, cin, x, hidden, slope_one, back, grad_two, grad_side, *refs
):
    grad_one, give = refs[:2]
    keeps = refs[2 : 2 + halves]
    total = refs[2 + halves]
    mid = hidden.shape[1]
    main, hc = sizes.main, sizes.hc
    shard = mid // (2 * halves)
    down = slice(hc, hc + main)
    own = slice(0, main)
    for n in range(mid // HALF):
        lanes = slice(n * HALF, (n + 1) * HALF)
        two, low = grad_two[own, lanes], grad_two[down, lanes]
        side, corner = grad_side[own, lanes], grad_side[down, lanes]
        first = 0
        for i, parts in enumerate(((two,), (two, side), (two, low), (two, low, side, corner))):
            left = jnp.concatenate(parts, axis=1)
            last = first + len(parts) * HALF
            spread = dot(left, back[n, :, first:last], ((1,), (1,)))
            first = last
            rows = slice(i * main, (i + 1) * main)
            grad_one[rows, lanes] = (spread * slope_one[rows, lanes]).astype(BF16)
    flat = jnp.concatenate([x[at : at + main] for at in sizes.planes()], axis=0)
    total[:, :cin] = dot(grad_one[...].astype(F32).T.astype(BF16), flat)
    flipped = grad_two[own, :].astype(F32).T.astype(BF16)
    lane = lax.broadcasted_iota(jnp.int32, (GW, 128), 1) // GW
    for n in range(mid // HALF):
        lanes = slice(n * HALF, (n + 1) * HALF)
        sums = [jnp.zeros((GW, 128), F32)] * (HALF // GW)
        for tap in range(TAPS):
            at = sizes.tap(tap)
            piece = dot(flipped[n * HALF : (n + 1) * HALF], hidden[at : at + main, lanes])
            for q in range(HALF // GW):
                tile = q // 8
                block = piece[q * GW : (q + 1) * GW, tile * 128 : (tile + 1) * 128]
                block = pltpu.roll(block, (GW * (tap - q)) % 128, 1)
                if tap < 8:
                    sums[q] = jnp.where(lane == tap, block, sums[q])
                else:
                    rows = slice(n * HALF + q * GW, n * HALF + (q + 1) * GW)
                    total[rows, cin : cin + 128] = sums[q]
                    total[rows, cin + 128 : cin + 256] = jnp.where(lane == 0, block, 0.0)
    split_out(halves, total, shard, cin + 128, keeps, give)


def main_kernel(sizes, halves, cin, x, cot, own, passed, swapped, *refs):
    active_three, grad_sum, short_t, reduce_t, grad_one, give = refs[:6]
    keeps, refs = refs[6 : 6 + halves], refs[6 + halves :]
    hidden, slope_one, hidden_two, slope_two, back, pre, group_t, group, front = refs[:9]
    pre_two, beside, grad_two, grad_side, expand_t, shift, total = refs[9:]
    weights = (own, passed, swapped)
    forward_part(
        sizes, halves, x, *weights, hidden, slope_one, hidden_two, slope_two, back, reduce_t,
        pre, group_t, group, front, pre_two, beside,
    )
    middle_part(
        sizes, halves, x, hidden_two, slope_two, cot, *weights, active_three, grad_two, grad_side,
        grad_sum, short_t, total.at[:, cin + 256 :], expand_t, shift, beside,
    )
    backward_part(
        sizes, halves, cin, x, hidden, slope_one, back, grad_two, grad_side, grad_one, give,
        *keeps, total,
    )


def outputs_kernel(sizes, grad_one, reduce_t, grad_sum, short_t, active, block_out, region_grad, planes, spread_out):
    main, hc, cin = sizes.main, sizes.hc, reduce_t.shape[1]
    block_out[...] = active[...].reshape(block_out.shape)
    planes[...] = dot(grad_one[...], reduce_t[...])
    planes[:main] += dot(grad_sum[...], short_t[...])
    for i in range(4):
        for r in range(sizes.hr):
            at = i * main + r * hc
            for v in range(cin // 128):
                lanes = slice(v * 128, (v + 1) * 128)
                spread_out[v, 2 * r + i // 2, pl.ds(i % 2, hc, stride=2)] = planes[at : at + hc, lanes]
    for v in range(cin // 128):
        region_grad[:, :, v * 128 : (v + 1) * 128] = spread_out[v, :, : sizes.tc].astype(BF16)


def call(kernel, out_shape, scratch, *operands, flops=0, space=pltpu.VMEM, limit=VMEM_LIMIT):
    sizes = sum(o.size * o.dtype.itemsize for o in operands)
    sizes += sum(o.size * o.dtype.itemsize for o in jax.tree.leaves(out_shape))
    return pl.pallas_call(
        kernel,
        out_shape=out_shape,
        in_specs=[pl.BlockSpec(memory_space=space)] * len(operands),
        out_specs=jax.tree.map(lambda _: pl.BlockSpec(memory_space=pltpu.VMEM), out_shape),
        scratch_shapes=scratch,
        compiler_params=pltpu.CompilerParams(vmem_limit_bytes=limit),
        cost_estimate=pl.CostEstimate(flops=flops, bytes_accessed=sizes, transcendentals=0),
    )(*operands)


def chip_kernel(one, other, whole, part):
    whole[...] = (one[...].astype(F32) + other[...].astype(F32)).astype(BF16)
    core = lax.rem(lax.axis_index("row"), 2)
    first = pl.multiple_of(core * (whole.shape[0] - part.shape[0]), 16)
    part[...] = whole[pl.ds(first, part.shape[0]), :]


def finish_kernel(whole, mine, theirs, *refs):
    outs, across = refs[:-1], refs[-1]
    core = lax.rem(lax.axis_index("row"), 2)
    for ref, at in ((mine, core), (theirs, 1 - core)):
        first = pl.multiple_of(at * (whole.shape[0] - ref.shape[0]), 16)
        across[pl.ds(first, ref.shape[0]), :] = ref[...]
    value = whole[...].astype(F32) + across[...].astype(F32)
    shard = outs[0].shape[0]
    at = 0
    for out in outs:
        for v in range(out.shape[1] // 128):
            out[:, v * 128 : (v + 1) * 128] = value[at : at + shard]
            at += shard
    rest = outs[1].shape[1] - 128
    for i, part in enumerate(unfold(value[at:], shard)):
        outs[1][i * GW : (i + 1) * GW, 128:] = part[:, :rest]


def both(rows, cols, target):
    pairs = []
    for r in range(rows):
        for c in range(cols):
            to = target(r % 2, c // 2, c % 2)
            if to is not None:
                pairs.append((r * cols + c, r * cols + 2 * to[0] + to[1]))
    return pairs


def swap_odd(x, axis):
    pairs = []
    for i in range(1, lax.axis_size(axis) - 1, 2):
        pairs += [(i, i + 1), (i + 1, i)]
    return lax.ppermute(x, axis, pairs)


def swap_even(x, axis):
    return lax.ppermute(x, axis, [(i, i ^ 1) for i in range(lax.axis_size(axis))])


def cross(x, j):
    rows, cols = lax.axis_size("row"), lax.axis_size("col")
    halves = cols // 2

    def target(k, h, low):
        return None if j == k == 0 else ((h + j) % halves, low ^ k)

    return lax.ppermute(x, ("row", "col"), both(rows, cols, target))


def reduce(keeps, give, share):
    rows, halves = lax.axis_size("row"), lax.axis_size("col") // 2
    core = lax.axis_index("row") % 2
    other = swap_even(give, "row")
    sums = [keeps[j] + other[j].astype(F32) for j in range(halves)]
    total = None
    for j in sorted(range(halves), key=lambda j: (j > 0, -min(j, halves - j), -j)):
        came = cross(sums[j].astype(BF16), j).astype(F32)
        if j == 0:
            came = jnp.where(core == 0, sums[0], came)
        total = came if total is None else total + came
    part = jax.ShapeDtypeStruct((share, 128), BF16)
    if rows != 4:
        nothing = jnp.zeros(part.shape, part.dtype)
        return lax.psum(total, "row"), nothing, nothing
    total = total.astype(BF16)
    whole, part = call(
        chip_kernel,
        (jax.ShapeDtypeStruct(total.shape, BF16), part),
        [],
        total, swap_even(total, "row"),
    )
    across = lax.ppermute(part, "row", [(r, r ^ 2) for r in range(4)])
    return whole, across, swap_even(across, "row")


def per_device(region, reduce_weight, group_weight, expand_weight, shortcut_weight, cotangent):
    tile_rows, tile_cols, cin = region.shape
    sizes = Sizes(tile_rows, tile_cols)
    halves = lax.axis_size("col") // 2
    mid, shard = expand_weight.shape
    width = shard * lax.axis_size("col")
    taps = group_weight.shape[0]
    early, late = cin + 256, mid + cin
    length = (early + late) // 128 * shard - shard + GW
    share = (length + 31) // 32 * 16
    halo = 3 * cin // 128 * 32 + width // 128 * 16
    sent = halo - cin // 128 * 32

    def shape(dims, dtype=BF16):
        return jax.ShapeDtypeStruct(dims, dtype)

    def scratch(*dims, dtype=F32):
        return pltpu.VMEM(dims, dtype)

    inputs = (
        region, cotangent, reduce_weight.T, group_weight.T, expand_weight.T, shortcut_weight.T,
    )
    weights, outer, draft = call(
        functools.partial(send_kernel, sizes),
        (
            shape((length, 128)),
            shape((4 * tile_cols, cin)),
            shape((share + halo, 128)),
        ),
        [scratch(halo, 128)]
        + [scratch(*given.shape, dtype=BF16) for given in inputs]
        + [pltpu.SemaphoreType.DMA((len(inputs),))],
        *inputs,
        space=pltpu.HBM,
        limit=62 * 1024 * 1024,
    )
    far = [cross(weights, j) for j in range(1, halves)]
    core_rows = swap_even(outer, "row")
    far_rows = swap_odd(outer, "row")
    rows_scratch = [scratch(4 * tile_cols, cin, dtype=BF16)] * 2
    beside, edge = call(
        functools.partial(columns_kernel, sizes),
        (shape((share + sent, 128)), shape((sent, 128))),
        rows_scratch + [scratch(halo, 128)],
        core_rows, far_rows, draft,
    )
    beside, edge = swap_even(beside, "col"), swap_odd(edge, "col")
    x, cot_all = call(
        functools.partial(spread_kernel, sizes),
        (shape((sizes.pixels, cin)), shape((sizes.out, width))),
        rows_scratch
        + [
            scratch(sent, 128, dtype=BF16),
            scratch(sent, 128, dtype=BF16),
            scratch(32, cin),
            scratch(cin // 128, tile_rows + 3, 16 + tile_cols, 128),
            scratch(3, cin // 128, 40, 128),
        ],
        region, cotangent, core_rows, far_rows, beside, edge,
    )
    passed = call(
        pass_kernel,
        shape(((halves - 1) * length + share, 128)),
        [],
        beside, edge, *far,
    )
    blocks = [weights, passed, swap_even(passed, "row")]
    active_three, grad_sum, short_t, reduce_t, grad_one, give, *keeps = call(
        functools.partial(main_kernel, sizes, halves, cin),
        (
            shape((sizes.main, width)),
            shape((sizes.main, width)),
            shape((width, cin)),
            shape((mid, cin)),
            shape((4 * sizes.main, mid)),
            shape((halves, length, 128)),
        )
        + (shape((length, 128), F32),) * halves,
        [
            scratch(sizes.pixels, mid, dtype=BF16),
            scratch(4 * sizes.main, mid),
            scratch(sizes.out, mid, dtype=BF16),
            scratch(sizes.out, mid),
            scratch(mid // HALF, HALF, TAPS * HALF, dtype=BF16),
            scratch(sizes.pixels, mid),
            scratch(mid, 256, dtype=BF16),
            scratch(256, mid, dtype=BF16),
            scratch(mid // HALF, TAPS * HALF, HALF, dtype=BF16),
            scratch(sizes.out, mid),
            scratch(length, 128, dtype=BF16),
            scratch(sizes.wide, mid, dtype=BF16),
            scratch(sizes.wide, mid, dtype=BF16),
            scratch(width, mid, dtype=BF16),
            scratch(sizes.hr + 1, 24, mid),
            scratch(mid, early + late),
        ],
        x, cot_all, *blocks,
        flops=2 * sizes.pixels * cin * mid + 10 * sizes.out * TAPS * HALF * mid,
    )
    block_out, region_grad = call(
        functools.partial(outputs_kernel, sizes),
        (shape((sizes.hr, sizes.hc, width)), shape(region.shape)),
        [
            scratch(4 * sizes.main, cin),
            scratch(cin // 128, tile_rows, 8 + tile_cols, 128),
        ],
        grad_one, reduce_t, grad_sum, short_t, active_three,
        flops=2 * 4 * sizes.main * cin * mid,
    )
    sums = reduce(keeps, give, share)
    grads = call(
        finish_kernel,
        tuple(shape((shard, lanes), F32) for lanes in (cin, taps, mid, cin)),
        [scratch(length, 128, dtype=BF16)],
        *sums,
    )
    return (block_out, region_grad, *(grad.T for grad in grads))


def solution(mesh):
    tiles, split = P("row", "col", None), P(None, "col")
    return jax.shard_map(
        per_device,
        mesh=mesh,
        in_specs=(tiles, split, split, split, split, tiles),
        out_specs=(tiles, tiles, split, split, split, split),
        check_vma=False,
    )
```

```python
import functools

import jax
import jax.numpy as jnp
from jax import lax
from jax.experimental import pallas as pl
from jax.experimental.pallas import tpu as pltpu
from jax.sharding import PartitionSpec as P

GW = 16
TAPS = 9
HALF = 256
BACK = (4, 5, 3, 7, 1, 8, 2, 6, 0)
F32 = jnp.float32
BF16 = jnp.bfloat16
VMEM_LIMIT = 40 * 1024 * 1024


class Sizes:
    def __init__(self, tile_rows, tile_cols):
        self.tr, self.tc = tile_rows, tile_cols
        self.hr, self.hc = tile_rows // 2, tile_cols // 2
        self.odd = (self.hr + 2) * self.hc
        self.even = (self.hr + 1) * self.hc
        self.band = self.odd + self.even
        self.side = 3 * self.band
        self.pixels = self.side + TAPS * 16
        self.main = self.hr * self.hc
        self.wide = self.main + self.hc
        self.out = self.wide + 16

    def tap(self, tap):
        a, b = divmod(tap, 3)
        return b * self.band + (0, self.odd, self.hc)[a]

    def tap_side(self, tap):
        return self.side + tap * 16

    def planes(self):
        return (
            self.band + self.odd,
            2 * self.band + self.odd,
            self.band + self.hc,
            2 * self.band + self.hc,
        )


def dot(a, b, dims=((1,), (0,))):
    return lax.dot_general(a, b, (dims, ((), ())), preferred_element_type=F32)


def sigmoid(value):
    below = 1.0 + jnp.exp(jnp.minimum(-value, 80.0))
    guess = pl.reciprocal(below, approx=True)
    return guess * (2.0 - below * guess)


def place():
    col = lax.axis_index("col")
    return col // 2, lax.rem(col, 2), lax.rem(lax.axis_index("row"), 2)


def fold(block):
    parts = [
        pltpu.roll(block[at : at + GW], at, 1) if at else block[:GW]
        for at in range(0, block.shape[0], GW)
    ]
    return sum(parts[1:], parts[0])


def unfold(tail, rows):
    return [pltpu.roll(tail, (128 - at) % 128, 1) if at else tail for at in range(0, rows, GW)]


def pieces(halves, shard, own, passed, swapped, beside):
    h, low, core = place()
    length = own.shape[0]
    flips = (low + core - 2 * low * core, 1 - low - core + 2 * low * core)
    found = [(own, (2 * h + low) * shard)]
    for ref, flip in zip((passed, swapped), flips, strict=True):
        for j in range(1, halves):
            spot = 2 * lax.rem(h - j + halves, halves) + flip
            found.append((ref.at[(j - 1) * length : j * length], spot * shard))
    first = (halves - 1) * length
    share = passed.shape[0] - first
    for ref, part in ((passed, core), (swapped, 1 - core)):
        rows = pl.ds(pl.multiple_of(part * (length - share), 16), share)
        beside[rows, :] = ref[first : first + share]
    return found + [(beside, (2 * h + 1 - low) * shard)]


def send_kernel(sizes, *refs):
    given, (sent, outer, draft, cols) = refs[:6], refs[6:10]
    local, arrived, weights, gone = refs[10:16], refs[16], refs[17], refs[18]
    copies = [
        pltpu.make_async_copy(given[i], local[i], arrived.at[i]) for i in range(len(given))
    ]
    for copy in copies[2:] + copies[:2]:
        copy.start()
    for copy in copies[2:]:
        copy.wait()
    region, cot, reduce_t, group_t, expand_t, short_t = local
    shard, taps = group_t.shape
    cin, mid = reduce_t.shape[1], expand_t.shape[1]
    tiles = [reduce_t[:, at : at + 128] for at in range(0, cin, 128)]
    tiles.append(group_t[:, :128])
    tiles += [expand_t[:, at : at + 128] for at in range(0, mid, 128)]
    tiles += [short_t[:, at : at + 128] for at in range(0, cin, 128)]
    for i, tile in enumerate(tiles):
        weights[i * shard : (i + 1) * shard] = tile
    pad = jnp.zeros((shard, 256 - taps), BF16)
    rest = jnp.concatenate([group_t[...], pad], axis=1)[:, 128:].astype(F32)
    weights[len(tiles) * shard :] = fold(rest).astype(BF16)
    leave = pltpu.make_async_copy(weights, sent, gone)
    leave.start()
    for copy in copies[:2]:
        copy.wait()
    tc, half = sizes.tc, cot.shape[2] // 2
    for i, r in enumerate((sizes.tr - 1, 0, 1)):
        outer[i * tc : (i + 1) * tc] = region[r]
    outer[3 * tc : 3 * tc + sizes.hc] = cot[0, :, :half]
    outer[3 * tc + sizes.hc :] = cot[0, :, half:]
    cols[...] = jnp.zeros_like(cols)
    for r in range(sizes.tr):
        put_columns(cols, r + 1, region[r, :16], region[r, tc - 16 :])
    for i in range(sizes.hr):
        put_cotangent(cols, i, cot[i, :16])
    share = draft.shape[0] - cols.shape[0]
    core = lax.rem(lax.axis_index("row"), 2)
    first = pl.multiple_of(core * (weights.shape[0] - share), 16)
    draft[:share] = weights[pl.ds(first, share), :]
    draft[share:] = cols[...].astype(BF16)
    leave.wait()


def put_columns(cols, row, head, tail):
    head, tail = head.astype(F32), tail.astype(F32)
    tiles = head.shape[1] // 128
    for i, pixel in enumerate((tail[15:16], head[0:1], head[1:2])):
        for v in range(tiles):
            at = (i * tiles + v) * 32 + row
            cols[at : at + 1] = pixel[:, v * 128 : (v + 1) * 128]


def put_cotangent(cols, row, head):
    pixel = head.astype(F32)[0:1]
    tiles = pixel.shape[1] // 128
    for v in range(tiles):
        at = cols.shape[0] - (tiles - v) * 16 + row
        cols[at : at + 1] = pixel[:, v * 128 : (v + 1) * 128]


def choose(first, one, other, to_one, to_other):
    @pl.when(first)
    def _():
        to_one[...] = one[...]
        to_other[...] = other[...]

    @pl.when(jnp.logical_not(first))
    def _():
        to_one[...] = other[...]
        to_other[...] = one[...]


def columns_kernel(sizes, core_rows, far_rows, draft, beside, edge, north, south, cols):
    choose(lax.rem(lax.axis_index("row"), 2) == 0, core_rows, far_rows, south, north)
    tc, tr, hc = sizes.tc, sizes.tr, sizes.hc
    share = draft.shape[0] - cols.shape[0]
    beside[:share] = draft[:share]
    cols[...] = draft[share:].astype(F32)
    for to, rows, at in ((0, north, 0), (tr + 1, south, tc), (tr + 2, south, 2 * tc)):
        put_columns(cols, to, rows[at : at + 16], rows[at + tc - 16 : at + tc])
    ends = [south[at : at + 16] for at in (3 * tc, 3 * tc + hc)]
    put_cotangent(cols, sizes.hr, jnp.concatenate(ends, axis=1))
    low = lax.rem(lax.axis_index("col"), 2)
    skip = cols.shape[0] - edge.shape[0]
    for out, first in ((beside.at[share:], skip * low), (edge, skip * (1 - low))):
        first = pl.multiple_of(first, 16)
        out[...] = cols[pl.ds(first, out.shape[0]), :].astype(BF16)


def pass_kernel(beside, edge, *refs):
    far, passed = refs[:-1], refs[-1]
    length, share = far[0].shape[0], beside.shape[0] - edge.shape[0]
    for j, block in enumerate(far):
        passed[j * length : (j + 1) * length] = block[...]
    passed[len(far) * length :] = beside[:share]


def spread_kernel(sizes, region, cot, core_rows, far_rows, beside, edge, *refs):
    x, cot_all, north, south, west, east, left, ext, cols = refs
    choose(lax.rem(lax.axis_index("row"), 2) == 0, core_rows, far_rows, south, north)
    choose(lax.rem(lax.axis_index("col"), 2) == 0, beside.at[beside.shape[0] - edge.shape[0] :], edge, east, west)
    cin, tc, tr, hc = region.shape[2], sizes.tc, sizes.tr, sizes.hc
    tiles = cin // 128
    for v in range(tiles):
        left[:, v * 128 : (v + 1) * 128] = west[v * 32 : (v + 1) * 32].astype(F32)
    cols[...] = jnp.zeros_like(cols)
    for v in range(cin // 128):
        lanes = slice(v * 128, (v + 1) * 128)
        for r in range(tr + 3):
            if r == 0:
                row = north[:tc, lanes]
            elif r <= tr:
                row = region[r - 1, :, lanes]
            else:
                row = south[(r - tr) * tc : (1 + r - tr) * tc, lanes]
            ext[v, r, 8 : 8 + tc] = row.astype(F32)
            ext[v, r, 7:8] = left[r : r + 1, lanes]
            cols[0, v, r : r + 1] = ext[v, r, 7 + tc : 8 + tc]
        for b in (1, 2):
            at = ((b - 1) * tiles + v) * 32
            cols[b, v, :32] = east[at : at + 32].astype(F32)
        for b in range(3):
            base = b * sizes.band
            for r in list(range(0, tr + 3, 2)) + list(range(1, tr + 3, 2)):
                picked = ext[v, r, pl.ds(7 + b, hc, stride=2)]
                x[base : base + hc, lanes] = picked.astype(BF16)
                base += hc
            for a in range(3):
                at = sizes.tap_side(3 * a + b)
                x[at : at + 16, lanes] = cols[b, v, pl.ds(a, 16, stride=2)].astype(BF16)
    half = cot_all.shape[1] // 2
    cot_all[: sizes.main] = cot[...].reshape(sizes.main, 2 * half)
    cot_all[sizes.main : sizes.wide, :half] = south[3 * tc : 3 * tc + hc]
    cot_all[sizes.main : sizes.wide, half:] = south[3 * tc + hc :]
    for v in range(2 * half // 128):
        at = 2 * tiles * 32 + v * 16
        cot_all[sizes.wide :, v * 128 : (v + 1) * 128] = east[at : at + 16]


def forward_part(sizes, halves, x, *refs):
    hidden, slope_one, hidden_two, slope_two, back, reduce_t = refs[3:9]
    pre, group_t, group, front, pre_two, beside = refs[9:]
    cin = reduce_t.shape[1]
    mid = reduce_t.shape[0]
    shard = mid // (2 * halves)
    lane = lax.broadcasted_iota(jnp.int32, (GW, 128), 1)
    for block, first in pieces(halves, shard, *refs[:3], beside):
        rows = pl.ds(pl.multiple_of(first, 16), shard)
        for v in range(cin // 128):
            reduce_t[rows, v * 128 : (v + 1) * 128] = block[v * shard : (v + 1) * shard]
        at = cin // 128 * shard
        group_t[rows, :128] = block[at : at + shard]
        tail = block[block.shape[0] - GW :].astype(F32)
        for i, part in enumerate(unfold(tail, shard)):
            rows = pl.ds(pl.multiple_of(first + i * GW, 16), GW)
            group_t[rows, 128:] = jnp.where(lane < GW, part, 0.0).astype(BF16)
    pre[...] = dot(x[...], reduce_t[...], ((1,), (1,)))
    group[...] = group_t[...].astype(F32).T.astype(BF16)
    row_group = lax.broadcasted_iota(jnp.int32, (HALF, HALF), 0) // GW
    lane_group = lax.broadcasted_iota(jnp.int32, (HALF, HALF), 1) // GW
    mask = jnp.where(row_group == lane_group, 1.0, 0.0).astype(BF16)
    for n in range(mid // HALF):
        for tap in range(TAPS):
            rows = group[tap * GW : (tap + 1) * GW, n * HALF : (n + 1) * HALF]
            dense = jnp.concatenate([rows] * (HALF // GW), axis=0) * mask
            front[n, tap * HALF : (tap + 1) * HALF] = dense
            spot = BACK.index(tap)
            back[n, :, spot * HALF : (spot + 1) * HALF] = dense

    planes = sizes.planes()
    first = 0
    for start in sorted(planes) + [sizes.pixels]:
        for at in range(first, start, 32):
            rows = slice(at, min(at + 32, start))
            value = pre[rows, :]
            hidden[rows, :] = (value * sigmoid(value)).astype(BF16)
        first = start + sizes.main
    for i, start in enumerate(planes):
        for at in range(0, sizes.main, 32):
            rows = slice(start + at, start + at + 32)
            value = pre[rows, :]
            sigma = sigmoid(value)
            active = value * sigma
            hidden[rows, :] = active.astype(BF16)
            rows = slice(i * sizes.main + at, i * sizes.main + at + 32)
            slope_one[rows, :] = sigma + active * (1.0 - sigma)
    for n in range(mid // HALF):
        lanes = slice(n * HALF, (n + 1) * HALF)
        patches = []
        for tap in range(TAPS):
            at, side = sizes.tap(tap), sizes.tap_side(tap)
            patches.append(
                jnp.concatenate(
                    [hidden[at : at + sizes.wide, lanes], hidden[side : side + 16, lanes]], axis=0
                )
            )
        pre_two[:, lanes] = dot(jnp.concatenate(patches, axis=1), front[n])
    value = pre_two[...]
    sigma = sigmoid(value)
    active = value * sigma
    hidden_two[...] = active.astype(BF16)
    slope_two[...] = sigma + active * (1.0 - sigma)


def split_out(halves, total, shard, rest, keeps, give):
    tiles = [at for at in range(0, total.shape[1], 128) if at != rest]
    h, low, core = place()
    keep = low + core - 2 * low * core
    for j in range(halves):
        base = 2 * lax.rem(h + j, halves)
        mine = pl.ds(pl.multiple_of((base + keep) * shard, shard), shard)
        theirs = pl.ds(pl.multiple_of((base + 1 - keep) * shard, shard), shard)
        for i, at in enumerate(tiles):
            slab = slice(i * shard, (i + 1) * shard)
            keeps[j][slab] = total[mine, at : at + 128]
            give[j, slab] = total[theirs, at : at + 128].astype(BF16)
        keeps[j][len(tiles) * shard :] = fold(total[mine, rest : rest + 128])
        give[j, len(tiles) * shard :] = fold(total[theirs, rest : rest + 128]).astype(BF16)


def middle_part(sizes, halves, x, hidden_two, slope_two, cot, *refs):
    active_three, grad_two, grad_side, own, short_t, total, expand_t, shift, beside = refs[3:]
    mid = expand_t.shape[1]
    width = expand_t.shape[0]
    shard = width // (2 * halves)
    cin = short_t.shape[1]
    for block, first in pieces(halves, shard, *refs[:3], beside):
        rows = pl.ds(pl.multiple_of(first, 16), shard)
        at = (cin // 128 + 1) * shard
        for ref in (expand_t, short_t):
            for v in range(ref.shape[1] // 128):
                ref[rows, v * 128 : (v + 1) * 128] = block[at : at + shard]
                at += shard
    at, side = sizes.tap(4), sizes.tap_side(4)
    strided = jnp.concatenate([x[at : at + sizes.wide], x[side : side + 16]], axis=0)
    summed = dot(hidden_two[...], expand_t[...], ((1,), (1,))) + dot(
        strided, short_t[...], ((1,), (1,))
    )
    sigma = sigmoid(summed)
    active = summed * sigma
    active_three[...] = active[: sizes.main].astype(BF16)
    grad_sum = (cot[...].astype(F32) * (sigma + active * (1.0 - sigma))).astype(BF16)
    own[...] = grad_sum[: sizes.main]
    flipped = grad_sum[: sizes.main].astype(F32).T.astype(BF16)
    total[:, :mid] = dot(flipped, hidden_two[: sizes.main])
    total[:, mid:] = dot(flipped, strided[: sizes.main])
    back = dot(grad_sum, expand_t[...]) * slope_two[...]
    grad_two[...] = back[: sizes.wide].astype(BF16)
    for i in range(sizes.hr + 1):
        shift[i, : sizes.hc] = back[i * sizes.hc : (i + 1) * sizes.hc]
        shift[i, sizes.hc : sizes.hc + 1] = back[sizes.wide + i : sizes.wide + i + 1]
    for i in range(sizes.hr + 1):
        grad_side[i * sizes.hc : (i + 1) * sizes.hc] = shift[i, 1 : sizes.hc + 1].astype(BF16)


def backward_part(
    sizes, halves, cin, x, hidden, slope_one, back, grad_two, grad_side, *refs
):
    grad_one, give = refs[:2]
    keeps = refs[2 : 2 + halves]
    total = refs[2 + halves]
    mid = hidden.shape[1]
    main, hc = sizes.main, sizes.hc
    shard = mid // (2 * halves)
    down = slice(hc, hc + main)
    own = slice(0, main)
    for n in range(mid // HALF):
        lanes = slice(n * HALF, (n + 1) * HALF)
        two, low = grad_two[own, lanes], grad_two[down, lanes]
        side, corner = grad_side[own, lanes], grad_side[down, lanes]
        first = 0
        for i, parts in enumerate(((two,), (two, side), (two, low), (two, low, side, corner))):
            left = jnp.concatenate(parts, axis=1)
            last = first + len(parts) * HALF
            spread = dot(left, back[n, :, first:last], ((1,), (1,)))
            first = last
            rows = slice(i * main, (i + 1) * main)
            grad_one[rows, lanes] = (spread * slope_one[rows, lanes]).astype(BF16)
    flat = jnp.concatenate([x[at : at + main] for at in sizes.planes()], axis=0)
    total[:, :cin] = dot(grad_one[...].astype(F32).T.astype(BF16), flat)
    flipped = grad_two[own, :].astype(F32).T.astype(BF16)
    lane = lax.broadcasted_iota(jnp.int32, (GW, 128), 1) // GW
    for n in range(mid // HALF):
        lanes = slice(n * HALF, (n + 1) * HALF)
        sums = [jnp.zeros((GW, 128), F32)] * (HALF // GW)
        for tap in range(TAPS):
            at = sizes.tap(tap)
            piece = dot(flipped[n * HALF : (n + 1) * HALF], hidden[at : at + main, lanes])
            for q in range(HALF // GW):
                tile = q // 8
                block = piece[q * GW : (q + 1) * GW, tile * 128 : (tile + 1) * 128]
                block = pltpu.roll(block, (GW * (tap - q)) % 128, 1)
                if tap < 8:
                    sums[q] = jnp.where(lane == tap, block, sums[q])
                else:
                    rows = slice(n * HALF + q * GW, n * HALF + (q + 1) * GW)
                    total[rows, cin : cin + 128] = sums[q]
                    total[rows, cin + 128 : cin + 256] = jnp.where(lane == 0, block, 0.0)
    split_out(halves, total, shard, cin + 128, keeps, give)


def main_kernel(sizes, halves, cin, x, cot, own, passed, swapped, *refs):
    active_three, grad_sum, short_t, reduce_t, grad_one, give = refs[:6]
    keeps, refs = refs[6 : 6 + halves], refs[6 + halves :]
    hidden, slope_one, hidden_two, slope_two, back, pre, group_t, group, front = refs[:9]
    pre_two, beside, grad_two, grad_side, expand_t, shift, total = refs[9:]
    weights = (own, passed, swapped)
    forward_part(
        sizes, halves, x, *weights, hidden, slope_one, hidden_two, slope_two, back, reduce_t,
        pre, group_t, group, front, pre_two, beside,
    )
    middle_part(
        sizes, halves, x, hidden_two, slope_two, cot, *weights, active_three, grad_two, grad_side,
        grad_sum, short_t, total.at[:, cin + 256 :], expand_t, shift, beside,
    )
    backward_part(
        sizes, halves, cin, x, hidden, slope_one, back, grad_two, grad_side, grad_one, give,
        *keeps, total,
    )


def outputs_kernel(sizes, grad_one, reduce_t, grad_sum, short_t, active, block_out, region_grad, planes, spread_out):
    main, hc, cin = sizes.main, sizes.hc, reduce_t.shape[1]
    block_out[...] = active[...].reshape(block_out.shape)
    planes[...] = dot(grad_one[...], reduce_t[...])
    planes[:main] += dot(grad_sum[...], short_t[...])
    for i in range(4):
        for r in range(sizes.hr):
            at = i * main + r * hc
            for v in range(cin // 128):
                lanes = slice(v * 128, (v + 1) * 128)
                spread_out[v, 2 * r + i // 2, pl.ds(i % 2, hc, stride=2)] = planes[at : at + hc, lanes]
    for v in range(cin // 128):
        region_grad[:, :, v * 128 : (v + 1) * 128] = spread_out[v, :, : sizes.tc].astype(BF16)


def call(kernel, out_shape, scratch, *operands, flops=0, space=pltpu.VMEM, limit=VMEM_LIMIT, first=pltpu.VMEM):
    leaves = jax.tree.leaves(out_shape)
    sizes = sum(o.size * o.dtype.itemsize for o in [*operands, *leaves])
    return pl.pallas_call(
        kernel,
        out_shape=out_shape,
        in_specs=[pl.BlockSpec(memory_space=space)] * len(operands),
        out_specs=jax.tree.map(
            lambda shape: pl.BlockSpec(memory_space=first if shape is leaves[0] else pltpu.VMEM),
            out_shape,
        ),
        scratch_shapes=scratch,
        compiler_params=pltpu.CompilerParams(vmem_limit_bytes=limit),
        cost_estimate=pl.CostEstimate(flops=flops, bytes_accessed=sizes, transcendentals=0),
    )(*operands)


def chip_kernel(one, other, whole, part):
    whole[...] = (one[...].astype(F32) + other[...].astype(F32)).astype(BF16)
    core = lax.rem(lax.axis_index("row"), 2)
    first = pl.multiple_of(core * (whole.shape[0] - part.shape[0]), 16)
    part[...] = whole[pl.ds(first, part.shape[0]), :]


def finish_kernel(whole, mine, theirs, *refs):
    outs, across = refs[:-1], refs[-1]
    core = lax.rem(lax.axis_index("row"), 2)
    for ref, at in ((mine, core), (theirs, 1 - core)):
        first = pl.multiple_of(at * (whole.shape[0] - ref.shape[0]), 16)
        across[pl.ds(first, ref.shape[0]), :] = ref[...]
    value = whole[...].astype(F32) + across[...].astype(F32)
    shard = outs[0].shape[0]
    at = 0
    for out in outs:
        for v in range(out.shape[1] // 128):
            out[:, v * 128 : (v + 1) * 128] = value[at : at + shard]
            at += shard
    rest = outs[1].shape[1] - 128
    for i, part in enumerate(unfold(value[at:], shard)):
        outs[1][i * GW : (i + 1) * GW, 128:] = part[:, :rest]


def both(rows, cols, target):
    pairs = []
    for r in range(rows):
        for c in range(cols):
            to = target(r % 2, c // 2, c % 2)
            if to is not None:
                pairs.append((r * cols + c, r * cols + 2 * to[0] + to[1]))
    return pairs


def swap_odd(x, axis):
    pairs = []
    for i in range(1, lax.axis_size(axis) - 1, 2):
        pairs += [(i, i + 1), (i + 1, i)]
    return lax.ppermute(x, axis, pairs)


def swap_even(x, axis):
    return lax.ppermute(x, axis, [(i, i ^ 1) for i in range(lax.axis_size(axis))])


def cross(x, j):
    rows, cols = lax.axis_size("row"), lax.axis_size("col")
    halves = cols // 2

    def target(k, h, low):
        return None if j == k == 0 else ((h + j) % halves, low ^ k)

    return lax.ppermute(x, ("row", "col"), both(rows, cols, target))


def reduce(keeps, give, share):
    rows, halves = lax.axis_size("row"), lax.axis_size("col") // 2
    core = lax.axis_index("row") % 2
    other = swap_even(give, "row")
    sums = [keeps[j] + other[j].astype(F32) for j in range(halves)]
    total = None
    for j in sorted(range(halves), key=lambda j: (j > 0, -min(j, halves - j), -j)):
        came = cross(sums[j].astype(BF16), j).astype(F32)
        if j == 0:
            came = jnp.where(core == 0, sums[0], came)
        total = came if total is None else total + came
    part = jax.ShapeDtypeStruct((share, 128), BF16)
    if rows != 4:
        nothing = jnp.zeros(part.shape, part.dtype)
        return lax.psum(total, "row"), nothing, nothing
    total = total.astype(BF16)
    whole, part = call(
        chip_kernel,
        (jax.ShapeDtypeStruct(total.shape, BF16), part),
        [],
        total, swap_even(total, "row"),
    )
    across = lax.ppermute(part, "row", [(r, r ^ 2) for r in range(4)])
    return whole, across, swap_even(across, "row")


def per_device(region, reduce_weight, group_weight, expand_weight, shortcut_weight, cotangent):
    tile_rows, tile_cols, cin = region.shape
    sizes = Sizes(tile_rows, tile_cols)
    halves = lax.axis_size("col") // 2
    mid, shard = expand_weight.shape
    width = shard * lax.axis_size("col")
    taps = group_weight.shape[0]
    early, late = cin + 256, mid + cin
    length = (early + late) // 128 * shard - shard + GW
    share = (length + 31) // 32 * 16
    halo = 3 * cin // 128 * 32 + width // 128 * 16
    sent = halo - cin // 128 * 32

    def shape(dims, dtype=BF16):
        return jax.ShapeDtypeStruct(dims, dtype)

    def scratch(*dims, dtype=F32):
        return pltpu.VMEM(dims, dtype)

    inputs = (
        region, cotangent, reduce_weight.T, group_weight.T, expand_weight.T, shortcut_weight.T,
    )
    weights, outer, draft = call(
        functools.partial(send_kernel, sizes),
        (
            shape((length, 128)),
            shape((4 * tile_cols, cin)),
            shape((share + halo, 128)),
        ),
        [scratch(halo, 128)]
        + [scratch(*given.shape, dtype=BF16) for given in inputs]
        + [
            pltpu.SemaphoreType.DMA((len(inputs),)),
            scratch(length, 128, dtype=BF16),
            pltpu.SemaphoreType.DMA,
        ],
        *inputs,
        space=pltpu.HBM,
        limit=62 * 1024 * 1024,
        first=pltpu.HBM,
    )
    far = [cross(weights, j) for j in range(1, halves)]
    core_rows = swap_even(outer, "row")
    far_rows = swap_odd(outer, "row")
    rows_scratch = [scratch(4 * tile_cols, cin, dtype=BF16)] * 2
    beside, edge = call(
        functools.partial(columns_kernel, sizes),
        (shape((share + sent, 128)), shape((sent, 128))),
        rows_scratch + [scratch(halo, 128)],
        core_rows, far_rows, draft,
    )
    beside, edge = swap_even(beside, "col"), swap_odd(edge, "col")
    x, cot_all = call(
        functools.partial(spread_kernel, sizes),
        (shape((sizes.pixels, cin)), shape((sizes.out, width))),
        rows_scratch
        + [
            scratch(sent, 128, dtype=BF16),
            scratch(sent, 128, dtype=BF16),
            scratch(32, cin),
            scratch(cin // 128, tile_rows + 3, 16 + tile_cols, 128),
            scratch(3, cin // 128, 40, 128),
        ],
        region, cotangent, core_rows, far_rows, beside, edge,
    )
    passed = call(
        pass_kernel,
        shape(((halves - 1) * length + share, 128)),
        [],
        beside, edge, *far,
    )
    blocks = [weights, passed, swap_even(passed, "row")]
    active_three, grad_sum, short_t, reduce_t, grad_one, give, *keeps = call(
        functools.partial(main_kernel, sizes, halves, cin),
        (
            shape((sizes.main, width)),
            shape((sizes.main, width)),
            shape((width, cin)),
            shape((mid, cin)),
            shape((4 * sizes.main, mid)),
            shape((halves, length, 128)),
        )
        + (shape((length, 128), F32),) * halves,
        [
            scratch(sizes.pixels, mid, dtype=BF16),
            scratch(4 * sizes.main, mid),
            scratch(sizes.out, mid, dtype=BF16),
            scratch(sizes.out, mid),
            scratch(mid // HALF, HALF, TAPS * HALF, dtype=BF16),
            scratch(sizes.pixels, mid),
            scratch(mid, 256, dtype=BF16),
            scratch(256, mid, dtype=BF16),
            scratch(mid // HALF, TAPS * HALF, HALF, dtype=BF16),
            scratch(sizes.out, mid),
            scratch(length, 128, dtype=BF16),
            scratch(sizes.wide, mid, dtype=BF16),
            scratch(sizes.wide, mid, dtype=BF16),
            scratch(width, mid, dtype=BF16),
            scratch(sizes.hr + 1, 24, mid),
            scratch(mid, early + late),
        ],
        x, cot_all, *blocks,
        flops=2 * sizes.pixels * cin * mid + 10 * sizes.out * TAPS * HALF * mid,
    )
    block_out, region_grad = call(
        functools.partial(outputs_kernel, sizes),
        (shape((sizes.hr, sizes.hc, width)), shape(region.shape)),
        [
            scratch(4 * sizes.main, cin),
            scratch(cin // 128, tile_rows, 8 + tile_cols, 128),
        ],
        grad_one, reduce_t, grad_sum, short_t, active_three,
        flops=2 * 4 * sizes.main * cin * mid,
    )
    sums = reduce(keeps, give, share)
    grads = call(
        finish_kernel,
        tuple(shape((shard, lanes), F32) for lanes in (cin, taps, mid, cin)),
        [scratch(length, 128, dtype=BF16)],
        *sums,
    )
    return (block_out, region_grad, *(grad.T for grad in grads))


def solution(mesh):
    tiles, split = P("row", "col", None), P(None, "col")
    return jax.shard_map(
        per_device,
        mesh=mesh,
        in_specs=(tiles, split, split, split, split, tiles),
        out_specs=(tiles, tiles, split, split, split, split),
        check_vma=False,
    )
```
